32 devices in a mesh: batch: 4 (over y, core), seq: 8 (over z, x).
Axes of the slice: x: 2, y: 2, z: 4, core: 2. Of those that a mesh axis runs over, the one named last changes fastest.
Arguments:
- block_input: bfloat16 [8, 1024, 512], P('batch', 'seq'), may hold values from -6 to 6
- cotangent: bfloat16 [8, 1024, 512], P('batch', 'seq'), may hold values from -6 to 6
- groups: int32 [8], P('batch'), may hold values from 0 to 7
- lengths: int32 [8], P('batch'), may hold values from 128 to 1024, as said below
- pair_table: float32 [8, 512], replicated, may hold values from -5 to 5
- qkv_weight: bfloat16 [512, 1536], replicated, may hold values from -0.25 to 0.25
- q_bias: float32 [512], replicated, may hold values from -3 to 3
- v_bias: float32 [512], replicated, may hold values from -3 to 3
- out_weight: bfloat16 [512, 512], replicated, may hold values from -0.5 to 0.5
- out_bias: float32 [512], replicated, may hold values from -2 to 2
- norm1_gain: float32 [512], replicated, may hold values from 0.5 to 1.5
- norm1_bias: float32 [512], replicated, may hold values from -2 to 2
- up_weight: bfloat16 [512, 2048], replicated, may hold values from -0.25 to 0.25
- up_bias: float32 [2048], replicated, may hold values from -3 to 3
- down_weight: bfloat16 [2048, 512], replicated, may hold values from -0.125 to 0.125
- down_bias: float32 [512], replicated, may hold values from -2 to 2
- norm2_gain: float32 [512], replicated, may hold values from 0.5 to 1.5
- norm2_bias: float32 [512], replicated, may hold values from -2 to 2
Outputs:
- layer_out: float32 [8, 1024, 512], P('batch', 'seq')
- input_grad: float32 [8, 1024, 512], P('batch', 'seq')
- pair_table_grad: float32 [8, 512], replicated
- qkv_weight_grad: float32 [512, 1536], replicated
- q_bias_grad: float32 [512], replicated
- v_bias_grad: float32 [512], replicated
- out_weight_grad: float32 [512, 512], replicated
- out_bias_grad: float32 [512], replicated
- norm1_gain_grad: float32 [512], replicated
- norm1_bias_grad: float32 [512], replicated
- up_weight_grad: float32 [512, 2048], replicated
- up_bias_grad: float32 [2048], replicated
- down_weight_grad: float32 [2048, 512], replicated
- down_bias_grad: float32 [512], replicated
- norm2_gain_grad: float32 [512], replicated
- norm2_bias_grad: float32 [512], replicated
The draws below stay inside these ranges and needn't reach their ends.
Inputs may be any that keep to these rules, and one draw needn't show every extreme that they name: `lengths`: in each aligned block of 2 rows (the rows of one index of batch), one row, chosen by the seed, has length 1024.
All inputs are finite; a program needn't handle non-finite values.
Results may differ from the reference program's by a relative error of at most 0.014.
The reference program's roundings to bfloat16 on the way count: a program that leaves them out, or rounds other values in their place, can miss the bound.
Values may be sent and summed in bfloat16 or wider, within the bound.
A program may use at most 192 MiB of HBM per device.

```python
import jax
import jax.numpy as jnp
from jax import lax

D = 512
HEADS = 8
HEAD = 64
FF = 2048
PAIRS = 8
SEQS = 2
LENGTH = 1024
ROWS = 8


def draw_lengths(key, part):
    key = jax.random.fold_in(key, 7)
    first_key, second_key = jax.random.split(key)
    drawn_lengths = jax.random.randint(first_key, (ROWS,), LENGTH // 8, LENGTH + 1)
    chosen = jax.random.randint(second_key, (ROWS // SEQS,), 0, SEQS)
    full_row = jnp.arange(ROWS) % SEQS == jnp.repeat(chosen, SEQS)
    return jnp.where(full_row, LENGTH, drawn_lengths).astype(jnp.int32)


def set_ends(result, key, smallest, top_value):
    spot = [jax.random.randint(jax.random.fold_in(key, axis), (), 0, length) for axis, length in enumerate(result.shape)]
    longest = result.shape.index(max(result.shape))
    next_to = spot[:longest] + [(spot[longest] + 1) % result.shape[longest]] + spot[longest + 1:]
    return result.at[tuple(spot)].set(smallest).at[tuple(next_to)].set(top_value)


def steps_of(stream_key, extent, cuts, smallest, high):
    loudness = 1.0
    for dim, shards_of in cuts:
        steps = jax.random.uniform(jax.random.fold_in(jax.random.fold_in(stream_key, 6), dim), (shards_of,), jnp.float32, smallest / len(cuts), high / len(cuts))
        loudness = loudness * jnp.repeat(jnp.exp(steps), extent[dim] // shards_of).reshape((-1,) + (1,) * (len(extent) - 1 - dim))
    return loudness


def gaussian(key, extent, deviation, bound, shards=(), held_as=jnp.bfloat16):
    values = jax.random.normal(key, extent, jnp.float32) * deviation
    if len(shards) > 0:
        values = steps_of(key, extent, shards, -0.22, 0.18) * values
    return jnp.clip(values, min=-bound, max=bound).astype(held_as)


def setup_inputs(seed: int = 0) -> dict:
    splits = jax.random.split(jax.random.key(seed), 19)
    block_input = gaussian(splits[0], (ROWS, LENGTH, D), 1.0, 6.0, ((0, 4), (1, 8)))
    cotangent = gaussian(splits[1], (ROWS, LENGTH, D), 1.0, 6.0, ((0, 4), (1, 8)))
    groups = set_ends(jax.random.randint(splits[2], (ROWS,), 0, PAIRS), jax.random.fold_in(splits[2], 1), 0, PAIRS - 1).astype(jnp.int32)
    lengths = draw_lengths(jax.random.fold_in(splits[18], 71), 0)
    pair_table = gaussian(splits[4], (PAIRS, D), 1.0, 5.0, (), jnp.float32)
    qkv_weight = gaussian(splits[5], (D, 3 * D), D ** -0.5, 0.25)
    q_bias = gaussian(splits[6], (D,), 0.5, 3.0, (), jnp.float32)
    v_bias = gaussian(splits[7], (D,), 0.5, 3.0, (), jnp.float32)
    out_weight = gaussian(splits[8], (D, D), (max(2, D * 256 // LENGTH)) ** -0.5, 0.5)
    out_bias = gaussian(splits[9], (D,), 0.3, 2.0, (), jnp.float32)
    norm1_gain = jnp.clip(1.0 + 0.1 * jax.random.normal(splits[10], (D,), jnp.float32), 0.5, 1.5)
    norm1_bias = gaussian(splits[11], (D,), 0.3, 2.0, (), jnp.float32)
    up_weight = gaussian(splits[12], (D, FF), D ** -0.5, 0.25)
    up_bias = gaussian(splits[13], (FF,), 0.5, 3.0, (), jnp.float32)
    down_weight = gaussian(splits[14], (FF, D), FF ** -0.5, 0.125)
    down_bias = gaussian(splits[15], (D,), 0.3, 2.0, (), jnp.float32)
    norm2_gain = jnp.clip(1.0 + 0.1 * jax.random.normal(splits[16], (D,), jnp.float32), 0.5, 1.5)
    norm2_bias = gaussian(splits[17], (D,), 0.3, 2.0, (), jnp.float32)
    return dict(block_input=block_input, cotangent=cotangent, groups=groups, lengths=lengths, pair_table=pair_table, qkv_weight=qkv_weight, q_bias=q_bias, v_bias=v_bias, out_weight=out_weight, out_bias=out_bias, norm1_gain=norm1_gain, norm1_bias=norm1_bias, up_weight=up_weight, up_bias=up_bias, down_weight=down_weight, down_bias=down_bias, norm2_gain=norm2_gain, norm2_bias=norm2_bias)


@jax.custom_vjp
def low(v):
    return lax.optimization_barrier(v.astype(jnp.bfloat16)).astype(jnp.float32)

@jax.custom_vjp
def low_back(v):
    return v

def low_keep(v):
    return (low(v), None)

def low_pass(kept, grad):
    return (grad,)

def back_keep(v):
    return (v, None)

def back_low(kept, grad):
    return (low(grad),)
low.defvjp(low_keep, low_pass)
low_back.defvjp(back_keep, back_low)
highest = lax.Precision.HIGHEST
eps_norm = 1e-05

def layer_norm(hidden, norm_gain, norm_shift):
    row_mean = lax.optimization_barrier(jnp.mean(hidden, axis=-1, keepdims=True))
    centred = hidden - row_mean
    spread = lax.optimization_barrier(jnp.mean(centred * centred, axis=-1, keepdims=True))
    return centred * lax.rsqrt(spread + eps_norm) * norm_gain + norm_shift

def matmul(left_side, right_side):
    return jnp.dot(left_side, right_side, precision=highest, preferred_element_type=jnp.float32)

def attend_block(query_block, key_heads, value_heads, usable):
    scores = low_back(jnp.einsum('ihd,jhd->hij', query_block, key_heads, precision=highest) * HEAD ** (-0.5))
    exp_scores = jnp.where(usable[None, None, :], jnp.exp(scores), 0.0)
    denominator = lax.optimization_barrier(jnp.sum(exp_scores, axis=-1))
    numerator = jnp.einsum('hij,jhd->ihd', low(exp_scores), value_heads, precision=highest)
    return numerator / jnp.transpose(denominator)[:, :, None]

def one_row(start_row, usable, weights):
    qkv_weight, q_bias, v_bias, out_weight, out_bias, norm1_gain, norm1_bias, up_weight, up_bias, down_weight, down_bias, norm2_gain, norm2_bias = weights
    lowered = low(start_row)
    projected = matmul(lowered, qkv_weight)
    query_rows = low(low_back(projected[:, :D] + q_bias))
    key_rows = low(low_back(projected[:, D:2 * D]))
    value_rows = low(low_back(projected[:, 2 * D:] + v_bias))
    block_len = 512 if LENGTH % 512 == 0 else LENGTH
    query_blocks = query_rows.reshape(LENGTH // block_len, block_len, HEADS, HEAD)
    key_heads = key_rows.reshape(LENGTH, HEADS, HEAD)
    value_heads = value_rows.reshape(LENGTH, HEADS, HEAD)

    def attend_one(query_block):
        return attend_block(query_block, key_heads, value_heads, usable)
    attended = lax.map(jax.checkpoint(attend_one), query_blocks).reshape(LENGTH, D)
    attn_out = low_back(matmul(low(attended), out_weight) + out_bias)
    normed = layer_norm(start_row + attn_out, norm1_gain, norm1_bias)
    pre_act = low_back(matmul(low(normed), up_weight) + up_bias)
    activated = low(jax.nn.gelu(pre_act, approximate=False))
    ffn_out = low_back(matmul(activated, down_weight) + down_bias)
    return layer_norm(ffn_out + normed + start_row, norm2_gain, norm2_bias)

def reference(block_input, cotangent, groups, lengths, pair_table, qkv_weight, q_bias, v_bias, out_weight, out_bias, norm1_gain, norm1_bias, up_weight, up_bias, down_weight, down_bias, norm2_gain, norm2_bias):
    weights_float = [tensor.astype(jnp.float32) for tensor in (qkv_weight, q_bias, v_bias, out_weight, out_bias, norm1_gain, norm1_bias, up_weight, up_bias, down_weight, down_bias, norm2_gain, norm2_bias)]
    positions = jnp.arange(LENGTH, dtype=jnp.int32)

    def forward(inputs, pair_rows, *weights):
        start_x = inputs + pair_rows[groups][:, None, :]

        def row_step(unused_carry, row_item):
            start_row, row_length = row_item
            return (unused_carry, one_row(start_row, positions < row_length, weights))
        unused_final, outputs = lax.scan(row_step, jnp.zeros((), jnp.float32), (start_x, lengths))
        return outputs
    outputs, backward = jax.vjp(forward, block_input.astype(jnp.float32), pair_table.astype(jnp.float32), *weights_float)
    gradients = backward(cotangent.astype(jnp.float32))
    return (outputs.astype(jnp.float32), gradients[0].astype(jnp.float32), gradients[1], gradients[2], gradients[3], gradients[4], gradients[5], gradients[6], gradients[7], gradients[8], gradients[9], gradients[10], gradients[11], gradients[12], gradients[13], gradients[14])
```

```python
import jax
import jax.numpy as jnp
from jax import lax
from jax.experimental import pallas as pl
from jax.experimental.pallas import tpu as pltpu
from jax.sharding import PartitionSpec as P

HEADS = 8


highest = lax.Precision.HIGHEST
eps_norm = 1e-05


def layer_norm(hidden, norm_gain, norm_shift):
    row_mean = jnp.mean(hidden, axis=-1, keepdims=True)
    centred = hidden - row_mean
    spread = jnp.mean(centred * centred, axis=-1, keepdims=True)
    return centred * lax.rsqrt(spread + eps_norm) * norm_gain + norm_shift


def exact_gelu(pre_act):
    return jax.nn.gelu(pre_act, approximate=False)


def block_size():
    return 512


def to_heads(flat_rows, head_count):
    return flat_rows.reshape(
        flat_rows.shape[0], flat_rows.shape[1], head_count, flat_rows.shape[2] // head_count
    )


def masked_exp(query_block, key_block, key_first, row_lengths, score_scale):
    scores = (
        jnp.einsum("rihd,rjhd->rhij", query_block, key_block, preferred_element_type=jnp.float32)
        * score_scale
    )
    places = key_first + jnp.arange(key_block.shape[1], dtype=jnp.int32)
    usable = places[None, :] < row_lengths[:, None]
    return jnp.where(usable[:, None, None, :], jnp.exp(scores), 0.0)


def forward_piece(
    running, key_piece, value_piece, query_heads, row_lengths, score_scale, head_count
):
    piece_len = key_piece.shape[1]
    block_len = block_size()
    key_all = to_heads(key_piece, head_count)
    value_all = to_heads(value_piece, head_count)

    def forward_one_block(block_index, partial_sums):
        numerator, denominator = partial_sums
        block_first = block_index * block_len
        key_block = lax.dynamic_slice_in_dim(key_all, block_first, block_len, 1)
        value_block = lax.dynamic_slice_in_dim(value_all, block_first, block_len, 1)
        exp_scores = masked_exp(query_heads, key_block, block_first, row_lengths, score_scale)
        denominator = denominator + jnp.sum(exp_scores, axis=-1)
        numerator = numerator + jnp.einsum(
            "rhij,rjhd->rihd",
            exp_scores.astype(jnp.bfloat16),
            value_block,
            preferred_element_type=jnp.float32,
        )
        return (numerator, denominator)

    return lax.fori_loop(0, piece_len // block_len, forward_one_block, running)


def key_side(
    running,
    query_piece,
    grad_piece,
    total_piece,
    key_heads,
    value_heads,
    key_first,
    row_lengths,
    score_scale,
    head_count,
):
    piece_len = query_piece.shape[1]
    block_len = block_size()
    query_all = to_heads(query_piece.astype(jnp.bfloat16), head_count)
    grad_all = to_heads(grad_piece, head_count)
    value_wide = value_heads.astype(jnp.float32)

    def key_one_block(block_index, partial_grads):
        key_grad, value_grad = partial_grads
        block_first = block_index * block_len
        query_block = lax.dynamic_slice_in_dim(query_all, block_first, block_len, 1)
        grad_block = lax.dynamic_slice_in_dim(grad_all, block_first, block_len, 1)
        total_block = lax.dynamic_slice_in_dim(total_piece, block_first, block_len, 1)
        exp_scores = masked_exp(query_block, key_heads, key_first, row_lengths, score_scale)
        prob_grad = jnp.einsum(
            "rihd,rjhd->rhij",
            grad_block,
            value_wide,
            precision=highest,
            preferred_element_type=jnp.float32,
        )
        shift_grad = jnp.transpose(total_block, (0, 2, 1))[..., None]
        score_grad = (exp_scores * (prob_grad + shift_grad)).astype(jnp.bfloat16)
        key_grad = (
            key_grad
            + jnp.einsum(
                "rhij,rihd->rjhd", score_grad, query_block, preferred_element_type=jnp.float32
            )
            * score_scale
        )
        exp_low = exp_scores.astype(jnp.bfloat16).astype(jnp.float32)
        value_grad = value_grad + jnp.einsum(
            "rhij,rihd->rjhd",
            exp_low,
            grad_block,
            precision=highest,
            preferred_element_type=jnp.float32,
        )
        return (key_grad, value_grad)

    return lax.fori_loop(0, piece_len // block_len, key_one_block, running)


def query_side(
    running,
    key_piece,
    value_piece,
    query_heads,
    grad_heads,
    total_here,
    row_lengths,
    score_scale,
    head_count,
):
    piece_len = key_piece.shape[1]
    block_len = block_size()
    key_all = to_heads(key_piece, head_count)
    value_all = to_heads(value_piece, head_count)

    def query_one_block(block_index, query_grad):
        block_first = block_index * block_len
        key_block = lax.dynamic_slice_in_dim(key_all, block_first, block_len, 1)
        value_block = lax.dynamic_slice_in_dim(value_all, block_first, block_len, 1)
        exp_scores = masked_exp(query_heads, key_block, block_first, row_lengths, score_scale)
        prob_grad = jnp.einsum(
            "rihd,rjhd->rhij",
            grad_heads,
            value_block.astype(jnp.float32),
            precision=highest,
            preferred_element_type=jnp.float32,
        )
        score_grad = (exp_scores * (prob_grad + total_here[..., None])).astype(jnp.bfloat16)
        return (
            query_grad
            + jnp.einsum(
                "rhij,rjhd->rihd", score_grad, key_block, preferred_element_type=jnp.float32
            )
            * score_scale
        )

    return lax.fori_loop(0, piece_len // block_len, query_one_block, running)


def local(
    block_input,
    cotangent,
    groups,
    lengths,
    pair_table,
    qkv_weight,
    q_bias,
    v_bias,
    out_weight,
    out_bias,
    norm1_gain,
    norm1_bias,
    up_weight,
    up_bias,
    down_weight,
    down_bias,
    norm2_gain,
    norm2_bias,
):
    row_count, shard_len, model_width = block_input.shape
    head_count = HEADS
    head_size = model_width // head_count
    score_scale = head_size ** (-0.5)
    key_offset = lax.axis_index("seq") * shard_len
    pair_onehot = (
        groups[:, None] == jnp.arange(pair_table.shape[0], dtype=jnp.int32)[None, :]
    ).astype(jnp.float32)
    lifted = jnp.dot(pair_onehot, pair_table, precision=highest)
    start_x = block_input.astype(jnp.float32) + lifted[:, None, :]
    lowered = start_x.astype(jnp.bfloat16)
    projected = jnp.einsum("rtd,de->rte", lowered, qkv_weight, preferred_element_type=jnp.float32)
    query_rows = (projected[:, :, :model_width] + q_bias).astype(jnp.bfloat16)
    key_rows = projected[:, :, model_width : 2 * model_width].astype(jnp.bfloat16)
    value_rows = (projected[:, :, 2 * model_width :] + v_bias).astype(jnp.bfloat16)
    query_heads = to_heads(query_rows, head_count)
    key_heads = to_heads(key_rows, head_count)
    value_heads = to_heads(value_rows, head_count)
    zero_heads = jnp.zeros((row_count, shard_len, head_count, head_size), jnp.float32)
    zero_totals = jnp.zeros((row_count, head_count, shard_len), jnp.float32)
    incoming = (
        lax.all_gather(key_rows, "seq", axis=1, tiled=True),
        lax.all_gather(value_rows, "seq", axis=1, tiled=True),
    )
    numerator, denominator = forward_piece(
        (zero_heads, zero_totals),
        incoming[0],
        incoming[1],
        query_heads,
        lengths,
        score_scale,
        head_count,
    )
    inverse = 1.0 / jnp.transpose(denominator, (0, 2, 1))[..., None]
    attended = numerator * inverse
    attended_low = attended.reshape(row_count, shard_len, model_width).astype(jnp.bfloat16)
    attn_out = (
        jnp.einsum("rtd,de->rte", attended_low, out_weight, preferred_element_type=jnp.float32)
        + out_bias
    )
    normed, norm1_back = jax.vjp(layer_norm, start_x + attn_out, norm1_gain, norm1_bias)
    normed_low = normed.astype(jnp.bfloat16)
    pre_act = (
        jnp.einsum("rtd,df->rtf", normed_low, up_weight, preferred_element_type=jnp.float32)
        + up_bias
    )
    activated, gelu_back = jax.vjp(exact_gelu, pre_act)
    activated_low = activated.astype(jnp.bfloat16)
    ffn_out = (
        jnp.einsum("rtf,fd->rtd", activated_low, down_weight, preferred_element_type=jnp.float32)
        + down_bias
    )
    layer_out, norm2_back = jax.vjp(layer_norm, ffn_out + normed + start_x, norm2_gain, norm2_bias)
    second_grad, norm2_gain_grad, norm2_bias_grad = norm2_back(cotangent.astype(jnp.float32))
    ffn_grad = second_grad.astype(jnp.bfloat16)
    down_bias_grad = jnp.sum(ffn_grad.astype(jnp.float32), axis=(0, 1))
    down_weight_grad = jnp.einsum(
        "rtf,rtd->fd", activated_low, ffn_grad, preferred_element_type=jnp.float32
    )
    act_grad = jnp.einsum("rtd,fd->rtf", ffn_grad, down_weight, preferred_element_type=jnp.float32)
    pre_grad = gelu_back(act_grad)[0].astype(jnp.bfloat16)
    up_bias_grad = jnp.sum(pre_grad.astype(jnp.float32), axis=(0, 1))
    up_weight_grad = jnp.einsum(
        "rtd,rtf->df", normed_low, pre_grad, preferred_element_type=jnp.float32
    )
    normed_grad = second_grad + jnp.einsum(
        "rtf,df->rtd", pre_grad, up_weight, preferred_element_type=jnp.float32
    )
    first_grad, norm1_gain_grad, norm1_bias_grad = norm1_back(normed_grad)
    attn_grad = first_grad.astype(jnp.bfloat16)
    out_bias_grad = jnp.sum(attn_grad.astype(jnp.float32), axis=(0, 1))
    out_weight_grad = jnp.einsum(
        "rtd,rte->de", attended_low, attn_grad, preferred_element_type=jnp.float32
    )
    attended_grad = to_heads(
        jnp.einsum("rte,de->rtd", attn_grad, out_weight, preferred_element_type=jnp.float32),
        head_count,
    )
    numer_grad = attended_grad * inverse
    total_grad = -jnp.sum(attended_grad * attended, axis=-1) * inverse[..., 0]
    grad_rows = numer_grad.reshape(row_count, shard_len, model_width)
    total_here = jnp.transpose(total_grad, (0, 2, 1))
    incoming = (
        lax.all_gather(query_rows.astype(jnp.float32), "seq", axis=1, tiled=True),
        lax.all_gather(grad_rows, "seq", axis=1, tiled=True),
        lax.all_gather(total_grad, "seq", axis=1, tiled=True),
    )
    key_grad, value_grad = key_side(
        (zero_heads, zero_heads),
        incoming[0],
        incoming[1],
        incoming[2],
        key_heads,
        value_heads,
        key_offset,
        lengths,
        score_scale,
        head_count,
    )
    incoming = (
        lax.all_gather(key_rows, "seq", axis=1, tiled=True),
        lax.all_gather(value_rows, "seq", axis=1, tiled=True),
    )
    query_grad = query_side(
        zero_heads,
        incoming[0],
        incoming[1],
        query_heads,
        numer_grad,
        total_here,
        lengths,
        score_scale,
        head_count,
    )
    flat_shape = (row_count, shard_len, model_width)
    query_low = query_grad.reshape(flat_shape).astype(jnp.bfloat16)
    key_low = key_grad.reshape(flat_shape).astype(jnp.bfloat16)
    value_low = value_grad.reshape(flat_shape).astype(jnp.bfloat16)
    qkv_grad = jnp.concatenate([query_low, key_low, value_low], axis=-1)
    qkv_weight_grad = jnp.einsum(
        "rtd,rte->de", lowered, qkv_grad, preferred_element_type=jnp.float32
    )
    q_bias_grad = jnp.sum(query_low.astype(jnp.float32), axis=(0, 1))
    v_bias_grad = jnp.sum(value_low.astype(jnp.float32), axis=(0, 1))
    input_grad = (
        jnp.einsum("rte,de->rtd", qkv_grad, qkv_weight, preferred_element_type=jnp.float32)
        + first_grad
        + second_grad
    )
    pair_table_grad = jnp.dot(
        jnp.transpose(pair_onehot), jnp.sum(input_grad, axis=1), precision=highest
    )
    summed = lax.psum(
        (
            pair_table_grad,
            qkv_weight_grad,
            q_bias_grad,
            v_bias_grad,
            out_weight_grad,
            out_bias_grad,
            norm1_gain_grad,
            norm1_bias_grad,
            up_weight_grad,
            up_bias_grad,
            down_weight_grad,
            down_bias_grad,
            norm2_gain_grad,
            norm2_bias_grad,
        ),
        ("batch", "seq"),
    )
    return (
        layer_out,
        input_grad,
        summed[0],
        summed[1],
        summed[2],
        summed[3],
        summed[4],
        summed[5],
        summed[6],
        summed[7],
        summed[8],
        summed[9],
        summed[10],
        summed[11],
        summed[12],
        summed[13],
    )


MESH = pl.DeviceIdType.MESH
f32, bf16 = jnp.float32, jnp.bfloat16
LANES = 9


def mm(a, b):
    return jnp.dot(a, b, preferred_element_type=f32)


def mm_nt(a, b):
    return lax.dot_general(a, b, (((1,), (1,)), ((), ())), preferred_element_type=f32)


def mm_tn(a, b):
    return lax.dot_general(a, b, (((0,), (0,)), ((), ())), preferred_element_type=f32)


class Numbers:
    def __init__(self):
        self.count = 0
        self.first = {}

    def take(self, name, size=1):
        self.first[name] = self.count
        self.count += size

    def __getitem__(self, name):
        return self.first[name]


def semaphore_numbers():
    numbers = Numbers()
    for name, size in (
        ("x", 2), ("cot", 2), ("lo", 2), ("ig", 2),
        ("xn", 2), ("core_own", 2), ("core_far", 2), ("meta", 1),
        ("o", 3), ("do", 3), ("dx_core", 2), ("dx_x", 1), ("vec", 6),
        ("lane", LANES * 12), ("qkv", 3 * 12),
    ):
        numbers.take(name, size)
    return numbers


NUM = semaphore_numbers()
LOCAL = 24 + LANES + 8


def fused(
    x_in, cot_in, groups, lengths, table_in, wqkv_in, qb_in, vb_in, wo_in, ob_in, g1_in, b1_in,
    wup_in, ub_in, wdn_in, db_in, g2_in, b2_in,
    lo_out, ig_out, gw_out, gqkv_out, vec_out,
    xb, lowb, cotb, table, meta, meta_far, wq, wo, wup, wdn, qb, vb, ob, g1, b1, ub, db, g2, b2,
    q, k, v, vaug, vback, att, inv, obuf, abuf, gelu_grad, act, pre_grad, res, lob, igb,
    dob, dor, probs, dq, dkt, dvt, dqkv, dxb, dxr0, dxr1,
    vecb, vecr, vecz,
    own, r0, r1, r2, r3, full, qown, qr1, qr3, qfull,
    ssem, rsem, lsem,
):
    b_index, s_index = lax.axis_index("batch"), lax.axis_index("seq")
    x, z = s_index % 2, s_index // 2
    y, c = b_index // 2, b_index % 2
    me = 2 * x + c

    def dev(x, y, z, c):
        return (2 * y + c, 2 * z + x)

    core_dev = dev(x, y, z, 1 - c)
    x_dev = dev(1 - x, y, z, c)
    y_dev = dev(x, 1 - y, z, c)
    diag_dev = dev(1 - x, y, z, 1 - c)
    z_devs = [dev(x, y, (z + d) % 4, c) for d in (1, 2, 3)]
    crossing = c != z // 2

    pending = []

    def send(src, dst, s_number, r_number, device, when=None):
        copy = pltpu.make_async_remote_copy(
            src_ref=src, dst_ref=dst, send_sem=ssem.at[s_number], recv_sem=rsem.at[r_number],
            device_id=device, device_id_type=MESH,
        )
        if when is None:
            copy.start()
        else:
            pl.when(when)(copy.start)
        pending.append((copy, when))

    def arrived(dst, number):
        pltpu.make_async_remote_copy(
            src_ref=dst, dst_ref=dst, send_sem=ssem.at[number], recv_sem=rsem.at[number],
            device_id=core_dev, device_id_type=MESH,
        ).wait_recv()

    local_copies = []

    def fetch(src, dst):
        copy = pltpu.make_async_copy(src, dst, lsem.at[len(local_copies)])
        copy.start()
        local_copies.append(copy)
        return copy

    wait_qkv = [fetch(table_in, table), fetch(qb_in, qb), fetch(vb_in, vb)]
    for t in range(3):
        columns = pl.ds(pl.multiple_of(512 * t + 128 * me, 128), 128)
        wait_qkv.append(fetch(wqkv_in.at[:, columns], wq.at[:, pl.ds(128 * t, 128)]))
    wait_ffn = [
        fetch(a, b)
        for a, b in ((wo_in, wo), (ob_in, ob), (g1_in, g1), (b1_in, b1), (wup_in, wup), (ub_in, ub),
                     (wdn_in, wdn), (db_in, db), (g2_in, g2), (b2_in, b2))
    ]

    barrier = pltpu.get_barrier_semaphore()
    near = [core_dev, x_dev, y_dev, diag_dev] + z_devs
    for device in near:
        pl.semaphore_signal(barrier, inc=1, device_id=device, device_id_type=MESH)

    @pl.when(crossing)
    def _():
        for i in range(2):
            pl.semaphore_signal(
                barrier, inc=1, device_id=dev(x, y, 2 * c + i, z // 2), device_id_type=MESH
            )
        pl.semaphore_wait(barrier, len(near) + 2)

    @pl.when(jnp.logical_not(crossing))
    def _():
        pl.semaphore_wait(barrier, len(near))

    own_slot = 4 * x + 2 * c
    far_slot = 4 * (1 - x) + 2 * c

    def to_peer(src, dst, i, name, here):
        is_self = 2 * c + i == z
        send(src, dst, NUM[name] + i, NUM[name] + z % 2, dev(x, y, 2 * c + i, z // 2),
             when=jnp.logical_not(is_self))

    first = jnp.where(crossing, 1 - c, z % 2)
    for i in (first, 1 - first):
        to_peer(x_in.at[i], xb.at[4 * x + z], i, "x", None)
    for i in (0, 1):
        to_peer(cot_in.at[i], cotb.at[z % 2], i, "cot", None)

    def own_block(src, dst, number):
        return pltpu.make_async_copy(src, dst, lsem.at[number])

    self_x = own_block(x_in.at[z % 2], xb.at[4 * x + z], LOCAL - 1)
    self_cot = own_block(cot_in.at[z % 2], cotb.at[z % 2], LOCAL - 2)

    @pl.when(jnp.logical_not(crossing))
    def _():
        self_x.start()
        self_cot.start()
        self_x.wait()

    for w in wait_qkv:
        w.wait()
    slot = z % 2
    group, length = groups[slot], lengths[slot]
    meta[0:1, :] = table[pl.ds(group, 1), :]
    meta[1:2, :] = jnp.full((1, 512), length.astype(f32))
    meta[2:3, :] = jnp.full((1, 512), group.astype(f32))
    meta[3:8, :] = jnp.zeros((5, 512), f32)
    send(meta, meta_far, NUM["meta"], NUM["meta"], core_dev)

    for i in (first, 1 - first):
        @pl.when(2 * c + i != z)
        def _():
            arrived(xb.at[own_slot + i], NUM["x"] + i)
        send(xb.at[own_slot + i], xb.at[own_slot + i], NUM["xn"] + i, NUM["xn"] + i, x_dev)
        send(xb.at[own_slot + i], xb.at[own_slot + i], NUM["core_own"] + i, NUM["core_own"] + i, core_dev)

    arrived(meta_far, NUM["meta"])
    facts = jnp.where(crossing, meta_far[...], meta[...])
    pair_row, length_row, group_row = facts[0:1, :], facts[1:2, :], facts[2:3, :]
    row_length = length_row[:, 0:128]

    lane = lax.broadcasted_iota(jnp.int32, (1, 128), 1)
    head_lanes = [lane < 64, lane >= 64]

    def project(base, natural):
        low = (xb[pl.ds(base, 2)].reshape(256, 512).astype(f32) + pair_row).astype(bf16)
        lowb[pl.ds(base, 2)] = low.reshape(2, 128, 512)
        rows = pl.ds(pl.multiple_of(base * 128, 256), 256)
        y_all = mm(low, wq[...])
        row = lax.broadcasted_iota(jnp.int32, (256, 1), 0)
        place = natural + row + jnp.where(row >= 128, 128, 0)
        usable = place.astype(f32) < row_length
        q_bias = qb[:, pl.ds(pl.multiple_of(128 * me, 128), 128)]
        v_bias = vb[:, pl.ds(pl.multiple_of(128 * me, 128), 128)]
        q[rows, :] = (y_all[:, 0:128] + q_bias).astype(bf16) * jnp.asarray(0.125, bf16)
        k[rows, :] = jnp.where(usable, y_all[:, 128:256], 0.0).astype(bf16)
        value = jnp.where(usable, y_all[:, 256:384] + v_bias, 0.0)
        one = jnp.where(usable, 1.0, 0.0)
        for h in range(2):
            vaug[h, rows, 0:128] = jnp.where(head_lanes[h], value, 0.0).astype(bf16)
            vaug[h, rows, 128:256] = jnp.where(head_lanes[h], one, 0.0).astype(bf16)
            edge = 64 * (1 - h)
            extra = jnp.where((lane == edge) | (lane == edge + 1), one, 0.0)
            vback[h, rows, :] = jnp.where(head_lanes[h], value, extra).astype(bf16)

    project(own_slot, 128 * (4 * c + x))
    for i in (first, 1 - first):
        arrived(xb.at[far_slot + i], NUM["xn"] + i)
        send(xb.at[far_slot + i], xb.at[far_slot + i], NUM["core_far"] + i, NUM["core_far"] + i, core_dev)
    project(far_slot, 128 * (4 * c + 1 - x))
    for name, base, natural in (
        ("core_own", 4 * x + 2 * (1 - c), 128 * (4 * (1 - c) + x)),
        ("core_far", 4 * (1 - x) + 2 * (1 - c), 128 * (4 * (1 - c) + 1 - x)),
    ):
        for i in range(2):
            arrived(xb.at[base + i], NUM[name] + i)
        project(base, natural)

    order = [(1 - x, c), (1 - x, 1 - c), (x, 1 - c), (x, c)]
    for step, (ox, oc) in enumerate(order):
        owner = 2 * ox + oc
        rows = pl.ds(pl.multiple_of(256 * owner, 256), 256)
        q_rows = q[rows, :]
        total = jnp.zeros((256, 256), f32)
        for h in range(2):
            scores = mm_nt(jnp.where(head_lanes[h], q_rows, 0), k[...])
            prob = jnp.exp(scores).astype(bf16)
            probs[h, rows, :] = prob
            total = total + mm(prob, vaug[h])
        inverse = 1.0 / total[:, 128:256]
        attended = total[:, 0:128] * inverse
        att[rows, :] = attended
        inv[rows, :] = inverse
        columns = pl.ds(pl.multiple_of(128 * me, 128), 128)
        if step < 3:
            obuf[step] = attended.astype(bf16)
            send(obuf.at[step], abuf.at[:, columns], NUM["o"] + step, NUM["o"] + step, dev(ox, y, z, oc))
        else:
            abuf[:, columns] = attended.astype(bf16)

    for w in wait_ffn:
        w.wait()
    for step, (ox, oc) in enumerate(order[:3]):
        columns = pl.ds(pl.multiple_of(128 * (2 * ox + oc), 128), 128)
        arrived(abuf.at[:, columns], NUM["o"] + step)

    def norm(hidden):
        centred = hidden - jnp.mean(hidden, axis=-1, keepdims=True)
        scale = lax.rsqrt(jnp.mean(centred * centred, axis=-1, keepdims=True) + eps_norm)
        return centred * scale, scale

    def norm_back(grad, normalized, scale, gain):
        e = grad * gain
        return scale * (
            e - jnp.mean(e, axis=-1, keepdims=True)
            - normalized * jnp.mean(e * normalized, axis=-1, keepdims=True)
        )

    def column_sum(values):
        return jnp.sum(values, axis=0, keepdims=True)

    start_x = xb[pl.ds(own_slot, 2)].reshape(256, 512).astype(f32) + pair_row
    attn_low = abuf[...]
    n1, s1 = norm(start_x + (mm(attn_low, wo[...]) + ob[...]))
    normed = n1 * g1[...] + b1[...]
    normed_low = normed.astype(bf16)
    ffn = jnp.zeros((256, 512), f32)
    for j in range(4):
        cols = pl.ds(512 * j, 512)
        pre = mm(normed_low, wup[:, cols]) + ub[:, cols]
        cdf = 0.5 * (1.0 + lax.erf(pre * 0.7071067811865476))
        gelu_grad[:, cols] = cdf + pre * (jnp.exp(-0.5 * pre * pre) * 0.3989422804014327)
        act_low = (pre * cdf).astype(bf16)
        act[:, cols] = act_low
        ffn = ffn + mm(act_low, wdn[cols, :])
    n2, s2 = norm((ffn + db[...]) + normed + start_x)
    layer_out = n2 * g2[...] + b2[...]
    lob[...] = layer_out.astype(bf16).reshape(2, 128, 512)

    def give_back(block, out, name, number):
        for i in (0, 1):
            to_peer(block.at[i], out.at[z % 2], i, name, None)
        self_copy = own_block(block.at[z % 2], out.at[z % 2], number)
        pl.when(jnp.logical_not(crossing))(self_copy.start)
        return self_copy

    self_lo = give_back(lob, lo_out, "lo", LOCAL - 3)

    for i in (0, 1):
        @pl.when(2 * c + i != z)
        def _():
            arrived(cotb.at[i], NUM["cot"] + i)
    pl.when(jnp.logical_not(crossing))(self_cot.wait)
    g = cotb[...].reshape(256, 512).astype(f32)
    vecb[14:15, :] = column_sum(g * n2)
    vecb[15:16, :] = column_sum(g)
    second_grad = norm_back(g, n2, s2, g2[...])
    ffn_grad = second_grad.astype(bf16)
    vecb[13:14, :] = column_sum(ffn_grad.astype(f32))

    def axes(lane_number):
        pair = [(x, x_dev, 1 - x), (y, y_dev, 1 - y)]
        return pair[::-1] if lane_number % 2 == 0 else pair

    def number(lane_number, step):
        return NUM["lane"] + 12 * lane_number + step

    def place(lane_number, level, other=False):
        (a, _, _), (bb, _, _) = axes(lane_number)
        mine = [c, a, bb, z]
        base = 0
        for at, size in zip(range(level + 1), (16, 8, 4, 1)):
            digit = mine[at]
            if other and at == level:
                digit = 1 - digit
            base = base + digit * size
        return base

    def fold(lane_number, level, size, received):
        base = place(lane_number, level)

        def body(t, carry):
            at = base + t * 4
            own[lane_number, pl.ds(at, 4)] = (
                own[lane_number, pl.ds(at, 4)].astype(f32) + received[lane_number, pl.ds(t * 4, 4)].astype(f32)
            ).astype(bf16)
            return carry

        lax.fori_loop(0, size // 4, body, 0)

    def lane_start(n):
        send(own.at[n, pl.ds(place(n, 0, True), 16)], r0.at[n], number(n, 0), number(n, 0), core_dev)

    def lane_step(n, step):
        (a, a_dev, _), (bb, b_dev, _) = axes(n)
        if step == 0:
            arrived(r0.at[n], number(n, 0))
            fold(n, 0, 16, r0)
            send(own.at[n, pl.ds(place(n, 1, True), 8)], r1.at[n], number(n, 1), number(n, 1), a_dev)
        elif step == 1:
            arrived(r1.at[n], number(n, 1))
            fold(n, 1, 8, r1)
            send(own.at[n, pl.ds(place(n, 2, True), 4)], r2.at[n], number(n, 2), number(n, 2), b_dev)
        elif step == 2:
            arrived(r2.at[n], number(n, 2))
            fold(n, 2, 4, r2)
            for d in (1, 2, 3):
                send(own.at[n, place(n, 2) + (z + d) % 4], r3.at[n, 3 - d],
                     number(n, 2 + d), number(n, 6 - d), z_devs[d - 1])
        elif step == 3:
            for d in (1, 2, 3):
                arrived(r3.at[n, d - 1], number(n, 2 + d))
            mine = place(n, 3)
            value = own[n, mine].astype(f32)
            for d in range(3):
                value = value + r3[n, d].astype(f32)
            full[n, mine] = value.astype(bf16)
            for d in (1, 2, 3):
                send(full.at[n, mine], full.at[n, mine], number(n, 5 + d), number(n, 9 - d), z_devs[d - 1])
        elif step == 4:
            base = place(n, 2)
            for d in (1, 2, 3):
                arrived(full.at[n, base + (z + d) % 4], number(n, 5 + d))
            send(full.at[n, pl.ds(base, 4)], full.at[n, pl.ds(base, 4)], number(n, 9), number(n, 9), b_dev)
        elif step == 5:
            base = place(n, 1)
            arrived(full.at[n, pl.ds(place(n, 2, True), 4)], number(n, 9))
            send(full.at[n, pl.ds(base, 8)], full.at[n, pl.ds(base, 8)], number(n, 10), number(n, 10), a_dev)
        elif step == 6:
            base = place(n, 0)
            arrived(full.at[n, pl.ds(place(n, 1, True), 8)], number(n, 10))
            send(full.at[n, pl.ds(base, 16)], full.at[n, pl.ds(base, 16)], number(n, 11), number(n, 11), core_dev)
        else:
            arrived(full.at[n, pl.ds(place(n, 0, True), 16)], number(n, 11))
            fetch(full.at[n], gw_out.at[n])

    def lane_fill(n, value):
        own[n] = value.astype(bf16).reshape(32, 16, 512)
        lane_start(n)

    waves = [(0, 1), (2, 3), (4, 5), (6, 7), (8,)]
    progress = {n: 0 for n in range(LANES)}

    def advance(wave):
        for n in waves[wave]:
            if progress[n] < 8:
                lane_step(n, progress[n])
                progress[n] += 1

    for n in range(4):
        lane_fill(n, mm_tn(act[:, pl.ds(512 * n, 512)], ffn_grad))
    advance(0)
    advance(1)

    normed_grad = second_grad
    for j in range(4):
        cols = pl.ds(512 * j, 512)
        grad = (mm_nt(ffn_grad, wdn[cols, :]) * gelu_grad[:, cols]).astype(bf16)
        pre_grad[:, cols] = grad
        vecb[16 + j : 17 + j, :] = column_sum(grad.astype(f32))
        normed_grad = normed_grad + mm_nt(grad, wup[:, cols])
    vecb[11:12, :] = column_sum(normed_grad * n1)
    vecb[12:13, :] = column_sum(normed_grad)
    first_grad = norm_back(normed_grad, n1, s1, g1[...])
    attn_grad = first_grad.astype(bf16)
    dob[...] = mm_nt(attn_grad, wo[...]).astype(bf16)
    for step, (ox, oc) in enumerate(order[:3]):
        owner = 2 * ox + oc
        send(dob.at[:, pl.ds(pl.multiple_of(128 * owner, 128), 128)], dor.at[me],
             NUM["do"] + step, NUM["do"] + step, dev(ox, y, z, oc))
    dor[me] = dob[:, pl.ds(pl.multiple_of(128 * me, 128), 128)]
    vecb[10:11, :] = column_sum(attn_grad.astype(f32))
    res[...] = first_grad + second_grad
    for n in range(4):
        lane_fill(4 + n, mm_tn(normed_low, pre_grad[:, pl.ds(512 * n, 512)]))
    advance(2)
    lane_fill(8, mm_tn(attn_low, attn_grad))
    advance(0)
    advance(3)
    advance(4)

    dkt[...] = jnp.zeros((128, 1024), f32)
    dvt[...] = jnp.zeros((128, 1024), f32)
    plan = [[1], [0, 2], [1, 3], [0, 2, 4]]
    for turn, (ox, oc) in enumerate(order[::-1]):
        owner = 2 * ox + oc
        if turn > 0:
            arrived(dor.at[owner], NUM["do"] + 3 - turn)
        rows = pl.ds(pl.multiple_of(256 * owner, 256), 256)
        d_out = dor[owner].astype(f32)
        inverse = inv[rows, :]
        numer_grad = d_out * inverse
        product = numer_grad.astype(bf16).astype(f32) * att[rows, :]
        q_rows = q[rows, :]
        dq_rows = jnp.zeros((256, 128), f32)
        for h in range(2):
            total = -jnp.sum(jnp.where(head_lanes[h], product, 0.0), axis=1, keepdims=True)
            high = total.astype(bf16).astype(f32)
            edge = 64 * (1 - h)
            rest = jnp.where(lane == edge, high, jnp.where(lane == edge + 1, total - high, 0.0))
            grad_low = jnp.where(head_lanes[h], numer_grad, rest).astype(bf16)
            prob = probs[h, rows, :]
            score_grad = (prob.astype(f32) * mm_nt(grad_low, vback[h])).astype(bf16)
            dq_rows = dq_rows + jnp.where(head_lanes[h], mm(score_grad, k[...]), 0.0)
            mine = pl.ds(64 * h, 64)
            q_t = jnp.transpose(q_rows)[64 * h : 64 * h + 64, :]
            g_t = jnp.transpose(grad_low)[64 * h : 64 * h + 64, :]
            dkt[mine, :] += mm(q_t, score_grad)
            dvt[mine, :] += mm(g_t, prob)
        dqkv[rows, 0:128] = (dq_rows * 0.125).astype(bf16)
        for wave in plan[turn]:
            advance(wave)

    for rows_first in range(0, 1024, 256):
        rows = pl.ds(rows_first, 256)
        row = lax.broadcasted_iota(jnp.int32, (256, 1), 0)
        owner = rows_first // 256
        start = 128 * (4 * (owner % 2) + owner // 2)
        usable = (start + row + jnp.where(row >= 128, 128, 0)).astype(f32) < row_length
        dqkv[rows, 128:256] = jnp.transpose(dkt[:, rows]).astype(bf16)
        dqkv[rows, 256:384] = jnp.where(usable, jnp.transpose(dvt[:, rows]), 0.0).astype(bf16)

    def qnumber(t, step):
        return NUM["qkv"] + 12 * t + step

    low_all = lowb[...].reshape(1024, 512)
    for t in range(3):
        value = mm_tn(low_all, dqkv[:, pl.ds(128 * t, 128)])
        qown[t] = value.astype(bf16).reshape(8, 64, 128)
        send(qown.at[t, pl.ds(4 * (1 - y), 4)], qr1.at[t], qnumber(t, 0), qnumber(t, 0), y_dev)

    def dx_block(ox, oc):
        owner = 2 * ox + oc
        rows = pl.ds(pl.multiple_of(256 * owner, 256), 256)
        return mm_nt(dqkv[rows, :], wq[...])

    column_total = jnp.zeros((1, 512), f32)
    for t, ox in enumerate((1 - x, x)):
        block = dx_block(ox, 1 - c)
        column_total = column_total + column_sum(block)
        dxb[t] = block.astype(bf16)
        send(dxb.at[t], dxr0.at[t], NUM["dx_core"] + t, NUM["dx_core"] + t, core_dev)

    advance(1)
    advance(2)
    block = dx_block(1 - x, c)
    column_total = column_total + column_sum(block)
    arrived(dxr0.at[0], NUM["dx_core"])
    dxb[2] = (block + dxr0[0].astype(f32)).astype(bf16)
    send(dxb.at[2], dxr1, NUM["dx_x"], NUM["dx_x"], x_dev)
    block = dx_block(x, c)
    column_total = column_total + column_sum(block)
    arrived(dxr0.at[1], NUM["dx_core"] + 1)
    block = block + dxr0[1].astype(f32) + res[...]
    column_total = column_total + column_sum(res[...])

    group_iota = lax.broadcasted_iota(jnp.int32, (8, 512), 0).astype(f32)
    vecb[0:8, :] = jnp.where(group_iota == group_row, column_total, 0.0)
    vecb[8:10, :] = jnp.zeros((2, 512), f32)
    mine = pl.ds(pl.multiple_of(128 * me, 128), 128)
    vecb[8:9, mine] = column_sum(dqkv[:, 0:128].astype(f32))
    vecb[9:10, mine] = column_sum(dqkv[:, 256:384].astype(f32))
    vecb[20:24, :] = jnp.zeros((4, 512), f32)
    for level, device in enumerate((core_dev, x_dev, y_dev)):
        src = vecb if level == 0 else vecr.at[2 + level]
        send(src, vecr.at[level], NUM["vec"] + level, NUM["vec"] + level, device)
        arrived(vecr.at[level], NUM["vec"] + level)
        value = (vecb[...] if level == 0 else vecr[2 + level]) + vecr[level]
        if level < 2:
            vecr[3 + level] = value
        else:
            vecz[z] = value
    for d in (1, 2, 3):
        send(vecz.at[z], vecz.at[z], NUM["vec"] + 2 + d, NUM["vec"] + 6 - d, z_devs[d - 1])

    for t in range(3):
        arrived(qr1.at[t], qnumber(t, 0))
        at = pl.ds(4 * y, 4)
        qown[t, at] = (qown[t, at].astype(f32) + qr1[t].astype(f32)).astype(bf16)
        for d in (1, 2, 3):
            send(qown.at[t, 4 * y + (z + d) % 4], qr3.at[t, 3 - d], qnumber(t, d), qnumber(t, 4 - d), z_devs[d - 1])
    advance(3)
    arrived(dxr1, NUM["dx_x"])
    igb[...] = (block + dxr1[...].astype(f32)).astype(bf16).reshape(2, 128, 512)
    self_ig = give_back(igb, ig_out, "ig", LOCAL - 4)

    for wave in (0, 1, 4, 2):
        advance(wave)
    for t in range(3):
        for d in (1, 2, 3):
            arrived(qr3.at[t, d - 1], qnumber(t, d))
        value = qown[t, 4 * y + z].astype(f32)
        for d in range(3):
            value = value + qr3[t, d].astype(f32)
        shard = qfull.at[t, me, 4 * y + z]
        shard[...] = value.astype(bf16)
        for d in (1, 2, 3):
            send(shard, shard, qnumber(t, 3 + d), qnumber(t, 7 - d), z_devs[d - 1])
    for wave in (3, 0, 1, 4):
        advance(wave)
    for t in range(3):
        for d in (1, 2, 3):
            arrived(qfull.at[t, me, 4 * y + (z + d) % 4], qnumber(t, 3 + d))
        part = qfull.at[t, me, pl.ds(4 * y, 4)]
        send(part, part, qnumber(t, 7), qnumber(t, 7), y_dev)
    for wave in (2, 3, 0, 1, 4):
        advance(wave)
    for t in range(3):
        arrived(qfull.at[t, me, pl.ds(4 * (1 - y), 4)], qnumber(t, 7))
        part = qfull.at[t, me]
        send(part, part, qnumber(t, 8), qnumber(t, 8), x_dev)
        send(part, part, qnumber(t, 9), qnumber(t, 9), core_dev)
    for wave in (2, 3, 4, 2, 3, 4, 4):
        advance(wave)
    for t in range(3):
        theirs = 2 * (1 - x) + c
        arrived(qfull.at[t, theirs], qnumber(t, 8))
        part = qfull.at[t, theirs]
        send(part, part, qnumber(t, 10), qnumber(t, 10), core_dev)
    for wave in (4, 0, 1, 2, 3, 4):
        for _ in range(8):
            advance(wave)
    for t in range(3):
        arrived(qfull.at[t, 2 * x + 1 - c], qnumber(t, 9))
        arrived(qfull.at[t, 2 * (1 - x) + 1 - c], qnumber(t, 10))
        fetch(qfull.at[t], gqkv_out.at[t])

    for d in (1, 2, 3):
        arrived(vecz.at[(z + d) % 4], NUM["vec"] + 2 + d)
    vecb_sum = vecz[0]
    for t in range(1, 4):
        vecb_sum = vecb_sum + vecz[t]
    vecr[0] = vecb_sum
    fetch(vecr.at[0], vec_out)

    for name, out, self_copy in (("lo", lo_out, self_lo), ("ig", ig_out, self_ig)):
        for i in (0, 1):
            @pl.when(2 * c + i != z)
            def _():
                arrived(out.at[i], NUM[name] + i)
        pl.when(jnp.logical_not(crossing))(self_copy.wait)
    for copy in local_copies[16:]:
        copy.wait()
    for copy, when in pending:
        if when is None:
            copy.wait_send()
        else:
            pl.when(when)(copy.wait_send)


def pair_plan(mesh):
    return dict(mesh.shape) == {"batch": 4, "seq": 8}


def fused_local(
    block_input, cotangent, groups, lengths, pair_table, qkv_weight, q_bias, v_bias, out_weight,
    out_bias, norm1_gain, norm1_bias, up_weight, up_bias, down_weight, down_bias, norm2_gain, norm2_bias,
):
    any_spec, smem = pl.BlockSpec(memory_space=pl.ANY), pl.BlockSpec(memory_space=pltpu.SMEM)

    def row(vector):
        return vector[None, :]

    operands = (
        block_input, cotangent, groups, lengths, pair_table, qkv_weight, row(q_bias), row(v_bias),
        out_weight, row(out_bias), row(norm1_gain), row(norm1_bias), up_weight, row(up_bias),
        down_weight, row(down_bias), row(norm2_gain), row(norm2_bias),
    )
    in_specs = [smem if i in (2, 3) else any_spec for i in range(len(operands))]
    out_shape = [
        jax.ShapeDtypeStruct((2, 128, 512), bf16),
        jax.ShapeDtypeStruct((2, 128, 512), bf16),
        jax.ShapeDtypeStruct((LANES, 32, 16, 512), bf16),
        jax.ShapeDtypeStruct((3, 4, 8, 64, 128), bf16),
        jax.ShapeDtypeStruct((24, 512), f32),
    ]
    scratch = [
        pltpu.VMEM(shape, dtype)
        for shape, dtype in (
            ((8, 128, 512), bf16), ((8, 128, 512), bf16), ((2, 128, 512), bf16),
            ((8, 512), f32), ((8, 512), f32), ((8, 512), f32),
            ((512, 384), bf16), ((512, 512), bf16), ((512, 2048), bf16), ((2048, 512), bf16),
            ((1, 512), f32), ((1, 512), f32), ((1, 512), f32), ((1, 512), f32), ((1, 512), f32),
            ((1, 2048), f32), ((1, 512), f32), ((1, 512), f32), ((1, 512), f32),
            ((1024, 128), bf16), ((1024, 128), bf16), ((1024, 128), bf16),
            ((2, 1024, 256), bf16), ((2, 1024, 128), bf16),
            ((1024, 128), f32), ((1024, 128), f32),
            ((3, 256, 128), bf16), ((256, 512), bf16),
            ((256, 2048), f32), ((256, 2048), bf16), ((256, 2048), bf16),
            ((256, 512), f32), ((2, 128, 512), bf16), ((2, 128, 512), bf16),
            ((256, 512), bf16), ((4, 256, 128), bf16), ((2, 1024, 1024), bf16),
            ((8, 128), f32), ((128, 1024), f32), ((128, 1024), f32), ((1024, 384), bf16),
            ((3, 256, 512), bf16), ((2, 256, 512), bf16), ((256, 512), bf16),
            ((24, 512), f32), ((5, 24, 512), f32), ((4, 24, 512), f32),
            ((LANES, 32, 16, 512), bf16), ((LANES, 16, 16, 512), bf16), ((LANES, 8, 16, 512), bf16),
            ((LANES, 4, 16, 512), bf16), ((LANES, 3, 16, 512), bf16), ((LANES, 32, 16, 512), bf16),
            ((3, 8, 64, 128), bf16), ((3, 4, 64, 128), bf16), ((3, 3, 64, 128), bf16), ((3, 4, 8, 64, 128), bf16),
        )
    ] + [
        pltpu.SemaphoreType.DMA((NUM.count,)),
        pltpu.SemaphoreType.DMA((NUM.count,)),
        pltpu.SemaphoreType.DMA((LOCAL,)),
    ]
    layer_out, input_grad, lanes, qkv_parts, vectors = pl.pallas_call(
        fused,
        out_shape=out_shape,
        in_specs=in_specs,
        out_specs=[any_spec] * len(out_shape),
        scratch_shapes=scratch,
        compiler_params=pltpu.CompilerParams(
            collective_id=0, has_side_effects=True, vmem_limit_bytes=60 * 2**20
        ),
    )(*operands)
    lanes = lanes.reshape(LANES, 512, 512)
    down_grad = lanes[0:4].reshape(2048, 512).astype(f32)
    up_grad = jnp.transpose(lanes[4:8], (1, 0, 2)).reshape(512, 2048).astype(f32)
    out_grad = lanes[8].astype(f32)
    qkv_grad = jnp.transpose(qkv_parts.reshape(3, 4, 512, 128), (2, 0, 1, 3)).reshape(512, 1536).astype(f32)
    return (
        layer_out.astype(f32), input_grad.astype(f32), vectors[0:8], qkv_grad, vectors[8], vectors[9],
        out_grad, vectors[10], vectors[11], vectors[12], up_grad, vectors[16:20].reshape(2048),
        down_grad, vectors[13], vectors[14], vectors[15],
    )


def solution(mesh):
    in_specs = (
        P("batch", "seq", None),
        P("batch", "seq", None),
        P("batch"),
        P("batch"),
        P(),
        P(),
        P(),
        P(),
        P(),
        P(),
        P(),
        P(),
        P(),
        P(),
        P(),
        P(),
        P(),
        P(),
    )
    out_specs = (
        P("batch", "seq", None),
        P("batch", "seq", None),
        P(),
        P(),
        P(),
        P(),
        P(),
        P(),
        P(),
        P(),
        P(),
        P(),
        P(),
        P(),
        P(),
        P(),
    )
    return jax.shard_map(fused_local if pair_plan(mesh) else local, mesh=mesh, in_specs=in_specs, out_specs=out_specs, check_vma=False)
```

```python
import functools

import jax
import jax.numpy as jnp
from jax import lax
from jax.experimental import pallas as pl
from jax.experimental.pallas import tpu as pltpu
from jax.sharding import PartitionSpec as P

HEADS = 8


highest = lax.Precision.HIGHEST
eps_norm = 1e-05


def layer_norm(hidden, norm_gain, norm_shift):
    row_mean = jnp.mean(hidden, axis=-1, keepdims=True)
    centred = hidden - row_mean
    spread = jnp.mean(centred * centred, axis=-1, keepdims=True)
    return centred * lax.rsqrt(spread + eps_norm) * norm_gain + norm_shift


def exact_gelu(pre_act):
    return jax.nn.gelu(pre_act, approximate=False)


def block_size():
    return 512


def to_heads(flat_rows, head_count):
    return flat_rows.reshape(
        flat_rows.shape[0], flat_rows.shape[1], head_count, flat_rows.shape[2] // head_count
    )


def masked_exp(query_block, key_block, key_first, row_lengths, score_scale):
    scores = (
        jnp.einsum("rihd,rjhd->rhij", query_block, key_block, preferred_element_type=jnp.float32)
        * score_scale
    )
    places = key_first + jnp.arange(key_block.shape[1], dtype=jnp.int32)
    usable = places[None, :] < row_lengths[:, None]
    return jnp.where(usable[:, None, None, :], jnp.exp(scores), 0.0)


def forward_piece(
    running, key_piece, value_piece, query_heads, row_lengths, score_scale, head_count
):
    piece_len = key_piece.shape[1]
    block_len = block_size()
    key_all = to_heads(key_piece, head_count)
    value_all = to_heads(value_piece, head_count)

    def forward_one_block(block_index, partial_sums):
        numerator, denominator = partial_sums
        block_first = block_index * block_len
        key_block = lax.dynamic_slice_in_dim(key_all, block_first, block_len, 1)
        value_block = lax.dynamic_slice_in_dim(value_all, block_first, block_len, 1)
        exp_scores = masked_exp(query_heads, key_block, block_first, row_lengths, score_scale)
        denominator = denominator + jnp.sum(exp_scores, axis=-1)
        numerator = numerator + jnp.einsum(
            "rhij,rjhd->rihd",
            exp_scores.astype(jnp.bfloat16),
            value_block,
            preferred_element_type=jnp.float32,
        )
        return (numerator, denominator)

    return lax.fori_loop(0, piece_len // block_len, forward_one_block, running)


def key_side(
    running,
    query_piece,
    grad_piece,
    total_piece,
    key_heads,
    value_heads,
    key_first,
    row_lengths,
    score_scale,
    head_count,
):
    piece_len = query_piece.shape[1]
    block_len = block_size()
    query_all = to_heads(query_piece.astype(jnp.bfloat16), head_count)
    grad_all = to_heads(grad_piece, head_count)
    value_wide = value_heads.astype(jnp.float32)

    def key_one_block(block_index, partial_grads):
        key_grad, value_grad = partial_grads
        block_first = block_index * block_len
        query_block = lax.dynamic_slice_in_dim(query_all, block_first, block_len, 1)
        grad_block = lax.dynamic_slice_in_dim(grad_all, block_first, block_len, 1)
        total_block = lax.dynamic_slice_in_dim(total_piece, block_first, block_len, 1)
        exp_scores = masked_exp(query_block, key_heads, key_first, row_lengths, score_scale)
        prob_grad = jnp.einsum(
            "rihd,rjhd->rhij",
            grad_block,
            value_wide,
            precision=highest,
            preferred_element_type=jnp.float32,
        )
        shift_grad = jnp.transpose(total_block, (0, 2, 1))[..., None]
        score_grad = (exp_scores * (prob_grad + shift_grad)).astype(jnp.bfloat16)
        key_grad = (
            key_grad
            + jnp.einsum(
                "rhij,rihd->rjhd", score_grad, query_block, preferred_element_type=jnp.float32
            )
            * score_scale
        )
        exp_low = exp_scores.astype(jnp.bfloat16).astype(jnp.float32)
        value_grad = value_grad + jnp.einsum(
            "rhij,rihd->rjhd",
            exp_low,
            grad_block,
            precision=highest,
            preferred_element_type=jnp.float32,
        )
        return (key_grad, value_grad)

    return lax.fori_loop(0, piece_len // block_len, key_one_block, running)


def query_side(
    running,
    key_piece,
    value_piece,
    query_heads,
    grad_heads,
    total_here,
    row_lengths,
    score_scale,
    head_count,
):
    piece_len = key_piece.shape[1]
    block_len = block_size()
    key_all = to_heads(key_piece, head_count)
    value_all = to_heads(value_piece, head_count)

    def query_one_block(block_index, query_grad):
        block_first = block_index * block_len
        key_block = lax.dynamic_slice_in_dim(key_all, block_first, block_len, 1)
        value_block = lax.dynamic_slice_in_dim(value_all, block_first, block_len, 1)
        exp_scores = masked_exp(query_heads, key_block, block_first, row_lengths, score_scale)
        prob_grad = jnp.einsum(
            "rihd,rjhd->rhij",
            grad_heads,
            value_block.astype(jnp.float32),
            precision=highest,
            preferred_element_type=jnp.float32,
        )
        score_grad = (exp_scores * (prob_grad + total_here[..., None])).astype(jnp.bfloat16)
        return (
            query_grad
            + jnp.einsum(
                "rhij,rjhd->rihd", score_grad, key_block, preferred_element_type=jnp.float32
            )
            * score_scale
        )

    return lax.fori_loop(0, piece_len // block_len, query_one_block, running)


def local(
    block_input,
    cotangent,
    groups,
    lengths,
    pair_table,
    qkv_weight,
    q_bias,
    v_bias,
    out_weight,
    out_bias,
    norm1_gain,
    norm1_bias,
    up_weight,
    up_bias,
    down_weight,
    down_bias,
    norm2_gain,
    norm2_bias,
):
    row_count, shard_len, model_width = block_input.shape
    head_count = HEADS
    head_size = model_width // head_count
    score_scale = head_size ** (-0.5)
    key_offset = lax.axis_index("seq") * shard_len
    pair_onehot = (
        groups[:, None] == jnp.arange(pair_table.shape[0], dtype=jnp.int32)[None, :]
    ).astype(jnp.float32)
    lifted = jnp.dot(pair_onehot, pair_table, precision=highest)
    start_x = block_input.astype(jnp.float32) + lifted[:, None, :]
    lowered = start_x.astype(jnp.bfloat16)
    projected = jnp.einsum("rtd,de->rte", lowered, qkv_weight, preferred_element_type=jnp.float32)
    query_rows = (projected[:, :, :model_width] + q_bias).astype(jnp.bfloat16)
    key_rows = projected[:, :, model_width : 2 * model_width].astype(jnp.bfloat16)
    value_rows = (projected[:, :, 2 * model_width :] + v_bias).astype(jnp.bfloat16)
    query_heads = to_heads(query_rows, head_count)
    key_heads = to_heads(key_rows, head_count)
    value_heads = to_heads(value_rows, head_count)
    zero_heads = jnp.zeros((row_count, shard_len, head_count, head_size), jnp.float32)
    zero_totals = jnp.zeros((row_count, head_count, shard_len), jnp.float32)
    incoming = (
        lax.all_gather(key_rows, "seq", axis=1, tiled=True),
        lax.all_gather(value_rows, "seq", axis=1, tiled=True),
    )
    numerator, denominator = forward_piece(
        (zero_heads, zero_totals),
        incoming[0],
        incoming[1],
        query_heads,
        lengths,
        score_scale,
        head_count,
    )
    inverse = 1.0 / jnp.transpose(denominator, (0, 2, 1))[..., None]
    attended = numerator * inverse
    attended_low = attended.reshape(row_count, shard_len, model_width).astype(jnp.bfloat16)
    attn_out = (
        jnp.einsum("rtd,de->rte", attended_low, out_weight, preferred_element_type=jnp.float32)
        + out_bias
    )
    normed, norm1_back = jax.vjp(layer_norm, start_x + attn_out, norm1_gain, norm1_bias)
    normed_low = normed.astype(jnp.bfloat16)
    pre_act = (
        jnp.einsum("rtd,df->rtf", normed_low, up_weight, preferred_element_type=jnp.float32)
        + up_bias
    )
    activated, gelu_back = jax.vjp(exact_gelu, pre_act)
    activated_low = activated.astype(jnp.bfloat16)
    ffn_out = (
        jnp.einsum("rtf,fd->rtd", activated_low, down_weight, preferred_element_type=jnp.float32)
        + down_bias
    )
    layer_out, norm2_back = jax.vjp(layer_norm, ffn_out + normed + start_x, norm2_gain, norm2_bias)
    second_grad, norm2_gain_grad, norm2_bias_grad = norm2_back(cotangent.astype(jnp.float32))
    ffn_grad = second_grad.astype(jnp.bfloat16)
    down_bias_grad = jnp.sum(ffn_grad.astype(jnp.float32), axis=(0, 1))
    down_weight_grad = jnp.einsum(
        "rtf,rtd->fd", activated_low, ffn_grad, preferred_element_type=jnp.float32
    )
    act_grad = jnp.einsum("rtd,fd->rtf", ffn_grad, down_weight, preferred_element_type=jnp.float32)
    pre_grad = gelu_back(act_grad)[0].astype(jnp.bfloat16)
    up_bias_grad = jnp.sum(pre_grad.astype(jnp.float32), axis=(0, 1))
    up_weight_grad = jnp.einsum(
        "rtd,rtf->df", normed_low, pre_grad, preferred_element_type=jnp.float32
    )
    normed_grad = second_grad + jnp.einsum(
        "rtf,df->rtd", pre_grad, up_weight, preferred_element_type=jnp.float32
    )
    first_grad, norm1_gain_grad, norm1_bias_grad = norm1_back(normed_grad)
    attn_grad = first_grad.astype(jnp.bfloat16)
    out_bias_grad = jnp.sum(attn_grad.astype(jnp.float32), axis=(0, 1))
    out_weight_grad = jnp.einsum(
        "rtd,rte->de", attended_low, attn_grad, preferred_element_type=jnp.float32
    )
    attended_grad = to_heads(
        jnp.einsum("rte,de->rtd", attn_grad, out_weight, preferred_element_type=jnp.float32),
        head_count,
    )
    numer_grad = attended_grad * inverse
    total_grad = -jnp.sum(attended_grad * attended, axis=-1) * inverse[..., 0]
    grad_rows = numer_grad.reshape(row_count, shard_len, model_width)
    total_here = jnp.transpose(total_grad, (0, 2, 1))
    incoming = (
        lax.all_gather(query_rows.astype(jnp.float32), "seq", axis=1, tiled=True),
        lax.all_gather(grad_rows, "seq", axis=1, tiled=True),
        lax.all_gather(total_grad, "seq", axis=1, tiled=True),
    )
    key_grad, value_grad = key_side(
        (zero_heads, zero_heads),
        incoming[0],
        incoming[1],
        incoming[2],
        key_heads,
        value_heads,
        key_offset,
        lengths,
        score_scale,
        head_count,
    )
    incoming = (
        lax.all_gather(key_rows, "seq", axis=1, tiled=True),
        lax.all_gather(value_rows, "seq", axis=1, tiled=True),
    )
    query_grad = query_side(
        zero_heads,
        incoming[0],
        incoming[1],
        query_heads,
        numer_grad,
        total_here,
        lengths,
        score_scale,
        head_count,
    )
    flat_shape = (row_count, shard_len, model_width)
    query_low = query_grad.reshape(flat_shape).astype(jnp.bfloat16)
    key_low = key_grad.reshape(flat_shape).astype(jnp.bfloat16)
    value_low = value_grad.reshape(flat_shape).astype(jnp.bfloat16)
    qkv_grad = jnp.concatenate([query_low, key_low, value_low], axis=-1)
    qkv_weight_grad = jnp.einsum(
        "rtd,rte->de", lowered, qkv_grad, preferred_element_type=jnp.float32
    )
    q_bias_grad = jnp.sum(query_low.astype(jnp.float32), axis=(0, 1))
    v_bias_grad = jnp.sum(value_low.astype(jnp.float32), axis=(0, 1))
    input_grad = (
        jnp.einsum("rte,de->rtd", qkv_grad, qkv_weight, preferred_element_type=jnp.float32)
        + first_grad
        + second_grad
    )
    pair_table_grad = jnp.dot(
        jnp.transpose(pair_onehot), jnp.sum(input_grad, axis=1), precision=highest
    )
    summed = lax.psum(
        (
            pair_table_grad,
            qkv_weight_grad,
            q_bias_grad,
            v_bias_grad,
            out_weight_grad,
            out_bias_grad,
            norm1_gain_grad,
            norm1_bias_grad,
            up_weight_grad,
            up_bias_grad,
            down_weight_grad,
            down_bias_grad,
            norm2_gain_grad,
            norm2_bias_grad,
        ),
        ("batch", "seq"),
    )
    return (
        layer_out,
        input_grad,
        summed[0],
        summed[1],
        summed[2],
        summed[3],
        summed[4],
        summed[5],
        summed[6],
        summed[7],
        summed[8],
        summed[9],
        summed[10],
        summed[11],
        summed[12],
        summed[13],
    )


MESH = pl.DeviceIdType.MESH
f32, bf16 = jnp.float32, jnp.bfloat16
LANES = 9


def mm(a, b):
    return jnp.dot(a, b, preferred_element_type=f32)


def mm_nt(a, b):
    return lax.dot_general(a, b, (((1,), (1,)), ((), ())), preferred_element_type=f32)


def mm_tn(a, b):
    return lax.dot_general(a, b, (((0,), (0,)), ((), ())), preferred_element_type=f32)


class Numbers:
    def __init__(self):
        self.count = 0
        self.first = {}

    def take(self, name, size=1):
        self.first[name] = self.count
        self.count += size

    def __getitem__(self, name):
        return self.first[name]


def semaphore_numbers():
    numbers = Numbers()
    for name, size in (
        ("x", 4), ("cot", 2), ("lo", 2), ("ig", 2), ("cot_x", 2),
        ("xn", 4), ("core_own", 4), ("core_far", 4), ("meta", 1),
        ("o_core", 2), ("o_x", 2), ("o_diag", 2), ("do", 1), ("dx_core", 2), ("dx_x", 1), ("vec", 6),
        ("lane", LANES * 12), ("qkv", 3 * 12),
    ):
        numbers.take(name, size)
    return numbers


NUM = semaphore_numbers()
LOCAL = 16 + 2

SCATTER = ('zy', 'yz', 'yz', 'zy', 'yz', 'yz', 'yz', 'yz', 'yz')
GATHER = ('zxy', 'zxy', 'zyx', 'zyx', 'zyx', 'zxy', 'zyx', 'zxy', 'zyx')
QGATHER = ('zyx', 'yxz', 'xzy')
FILL, LANE, FFN, NORM, ATTN, SPLIT, WEIGHT, PART, INPUT, RETURN, SMALL = range(11)
ORDER = (
    (FILL, 3, 0), (FILL, 1, 0), (FILL, 0, 0), (FILL, 2, 0), (FFN, 0, 0), (LANE, 3, 0), (LANE, 1, 0),
    (FFN, 1, 0), (LANE, 0, 0), (LANE, 2, 0), (FFN, 2, 0), (FFN, 3, 0), (FILL, 7, 0), (FILL, 5, 0),
    (FILL, 6, 0), (NORM, 0, 0), (LANE, 7, 0), (LANE, 1, 1), (FILL, 8, 0), (LANE, 6, 0), (LANE, 5, 0),
    (FILL, 4, 0), (ATTN, 0, 0), (LANE, 4, 0), (LANE, 8, 0), (LANE, 3, 1), (LANE, 2, 1), (ATTN, 1, 0),
    (LANE, 7, 1), (ATTN, 2, 0), (LANE, 0, 1), (LANE, 6, 1), (ATTN, 3, 0), (LANE, 1, 2), (LANE, 5, 1),
    (SPLIT, 0, 0), (WEIGHT, 2, 0), (WEIGHT, 0, 0), (WEIGHT, 1, 0), (LANE, 2, 2), (LANE, 4, 1), (INPUT, 0, 0),
    (INPUT, 1, 0), (LANE, 8, 1), (LANE, 7, 2), (LANE, 3, 2), (LANE, 0, 2), (LANE, 6, 2), (INPUT, 2, 0),
    (INPUT, 3, 0), (SMALL, 0, 0), (PART, 2, 0), (LANE, 1, 3), (SMALL, 1, 0), (PART, 0, 0), (LANE, 5, 2),
    (PART, 1, 0), (LANE, 2, 3), (LANE, 4, 2), (LANE, 8, 2), (LANE, 2, 4), (RETURN, 0, 0), (LANE, 7, 3),
    (LANE, 1, 4), (LANE, 3, 3), (SMALL, 2, 0), (LANE, 0, 3), (LANE, 6, 3), (LANE, 2, 5), (PART, 2, 1),
    (LANE, 1, 5), (LANE, 2, 6), (LANE, 7, 4), (PART, 0, 1), (LANE, 1, 6), (LANE, 3, 4), (LANE, 0, 4),
    (PART, 2, 2), (LANE, 5, 3), (SMALL, 3, 0), (PART, 1, 1), (LANE, 6, 4), (LANE, 4, 3), (LANE, 3, 5),
    (LANE, 8, 3), (LANE, 7, 5), (LANE, 3, 6), (LANE, 5, 4), (LANE, 7, 6), (LANE, 0, 5), (PART, 1, 2),
    (LANE, 6, 5), (LANE, 0, 6), (LANE, 4, 4), (LANE, 6, 6), (LANE, 8, 4), (PART, 1, 3), (PART, 0, 2),
    (LANE, 5, 5), (LANE, 4, 5), (PART, 2, 3), (LANE, 5, 6), (PART, 0, 3), (SMALL, 4, 0), (LANE, 4, 6),
    (LANE, 8, 5), (LANE, 8, 6), (PART, 2, 4), (PART, 0, 4), (PART, 2, 5), (PART, 1, 4), (PART, 0, 5),
    (PART, 1, 5),
)


def fused(
    x_in, cot_in, groups, lengths, table_in, wqkv_in, qb_in, vb_in, wo_in, ob_in, g1_in, b1_in,
    wup_in, ub_in, wdn_in, db_in, g2_in, b2_in,
    lo_out, ig_out, full, qfull, vec_out,
    xb, lowb, cotb, table, meta, meta_far, wq, wo, wup, wdn, qb, vb, ob, g1, b1, ub, db, g2, b2,
    q, k, vaug, vback, att, inv, obuf, abuf, gelu_grad, act, pre_grad, res, lob, igb, n1, n2, s2b, attn_grad,
    normed_low, ffn_grad, second, normed_grad, dob, dor, probs, dkt, dvt, dqkv, dxb, dxr0, dxr1, dxo,
    vecb, vecr, vecz,
    own, r0, r1, r3, qown, qr1, qr3,
    ssem, rsem, lsem,
):
    b_index, s_index = lax.axis_index("batch"), lax.axis_index("seq")
    x, z = s_index % 2, s_index // 2
    y, c = b_index // 2, b_index % 2
    me = 2 * x + c

    def dev(x, y, z, c):
        return (2 * y + c, 2 * z + x)

    core_dev = dev(x, y, z, 1 - c)
    x_dev = dev(1 - x, y, z, c)
    y_dev = dev(x, 1 - y, z, c)
    diag_dev = dev(1 - x, y, z, 1 - c)
    z_devs = [dev(x, y, (z + d) % 4, c) for d in (1, 2, 3)]
    crossing = c != z // 2

    pending = []

    def send(src, dst, s_number, r_number, device, when=None):
        copy = pltpu.make_async_remote_copy(
            src_ref=src, dst_ref=dst, send_sem=ssem.at[s_number], recv_sem=rsem.at[r_number],
            device_id=device, device_id_type=MESH,
        )
        if when is None:
            copy.start()
        else:
            pl.when(when)(copy.start)
        pending.append((copy, when))

    def arrived(dst, number):
        pltpu.make_async_remote_copy(
            src_ref=dst, dst_ref=dst, send_sem=ssem.at[number], recv_sem=rsem.at[number],
            device_id=core_dev, device_id_type=MESH,
        ).wait_recv()

    local_copies = []

    def fetch(src, dst):
        copy = pltpu.make_async_copy(src, dst, lsem.at[len(local_copies)])
        copy.start()
        local_copies.append(copy)
        return copy

    def land(copies):
        for copy in copies:
            copy.wait()
            local_copies[local_copies.index(copy)] = None

    wait_qkv = [fetch(table_in, table), fetch(qb_in, qb), fetch(vb_in, vb)]
    for t in range(3):
        columns = pl.ds(pl.multiple_of(512 * t + 128 * me, 128), 128)
        wait_qkv.append(fetch(wqkv_in.at[:, columns], wq.at[:, pl.ds(128 * t, 128)]))
    wait_ffn = [
        fetch(a, b)
        for a, b in ((wo_in, wo), (ob_in, ob), (g1_in, g1), (b1_in, b1), (wup_in, wup), (ub_in, ub),
                     (wdn_in, wdn), (db_in, db), (g2_in, g2), (b2_in, b2))
    ]

    barrier = pltpu.get_barrier_semaphore()
    near = [core_dev, x_dev, y_dev, diag_dev] + z_devs
    for device in near:
        pl.semaphore_signal(barrier, inc=1, device_id=device, device_id_type=MESH)

    @pl.when(crossing)
    def _():
        for i in range(2):
            pl.semaphore_signal(
                barrier, inc=1, device_id=dev(x, y, 2 * c + i, z // 2), device_id_type=MESH
            )
        pl.semaphore_wait(barrier, len(near) + 2)

    @pl.when(jnp.logical_not(crossing))
    def _():
        pl.semaphore_wait(barrier, len(near))

    def half(ref, h):
        return ref.at[pl.ds(64 * h, 64)]

    def peer(i):
        return dev(x, y, 2 * c + i, z // 2)

    first = jnp.where(crossing, 1 - c, z % 2)
    in_turn = [(i, h) for i in (first, 1 - first) for h in (0, 1)]
    for i, h in in_turn:
        send(half(x_in.at[i], h), half(xb.at[x, z], h), NUM["x"] + 2 * i + h, NUM["x"] + 2 * (z % 2) + h,
             peer(i), when=2 * c + i != z)
    self_x = pltpu.make_async_copy(x_in.at[z % 2], xb.at[x, z], lsem.at[LOCAL - 1])
    self_cot = pltpu.make_async_copy(cot_in.at[z % 2], cotb.at[x, z % 2], lsem.at[LOCAL - 2])

    @pl.when(jnp.logical_not(crossing))
    def _():
        self_x.start()
        self_cot.start()
        self_x.wait()


    land(wait_qkv)
    slot = z % 2
    group, length = groups[slot], lengths[slot]
    meta[0:1, :] = table[pl.ds(group, 1), :]
    meta[1:2, :] = jnp.full((1, 512), length.astype(f32))
    meta[2:3, :] = jnp.full((1, 512), group.astype(f32))
    meta[3:8, :] = jnp.zeros((5, 512), f32)
    send(meta, meta_far, NUM["meta"], NUM["meta"], core_dev)

    for i, h in in_turn:
        block = half(xb.at[x, 2 * c + i], h)

        @pl.when(2 * c + i != z)
        def _():
            arrived(block, NUM["x"] + 2 * i + h)

        number = NUM["xn"] + 2 * i + h
        send(block, block, number, number, x_dev)
        number = NUM["core_own"] + 2 * i + h
        send(block, block, number, number, core_dev)

    arrived(meta_far, NUM["meta"])
    facts = jnp.where(crossing, meta_far[...], meta[...])
    pair_row, length_row, group_row = facts[0:1, :], facts[1:2, :], facts[2:3, :]
    row_length = length_row[:, 0:128]

    lane = lax.broadcasted_iota(jnp.int32, (1, 128), 1)
    head_lanes = [lane < 64, lane >= 64]
    row = lax.broadcasted_iota(jnp.int32, (256, 1), 0)

    def rows_of(xx, cc):
        return pl.ds(pl.multiple_of(512 * xx + 256 * cc, 256), 256)

    def usable_rows(xx, cc):
        place = 128 * (4 * cc + xx) + row + jnp.where(row >= 128, 128, 0)
        return place.astype(f32) < row_length

    def project(xx, cc):
        low = (xb[xx, pl.ds(2 * cc, 2)].reshape(256, 512).astype(f32) + pair_row).astype(bf16)
        rows = rows_of(xx, cc)
        lowb[rows, :] = low
        y_all = mm(low, wq[...])
        usable = usable_rows(xx, cc)
        q_bias = qb[:, pl.ds(pl.multiple_of(128 * me, 128), 128)]
        v_bias = vb[:, pl.ds(pl.multiple_of(128 * me, 128), 128)]
        q[rows, :] = (y_all[:, 0:128] + q_bias).astype(bf16) * jnp.asarray(0.125, bf16)
        k[rows, :] = jnp.where(usable, y_all[:, 128:256], 0.0).astype(bf16)
        value = jnp.where(usable, y_all[:, 256:384] + v_bias, 0.0)
        one = jnp.where(usable, 1.0, 0.0)
        for h in range(2):
            vaug[h, rows, 0:128] = jnp.where(head_lanes[h], value, 0.0).astype(bf16)
            vaug[h, rows, 128:256] = jnp.where(head_lanes[h], one, 0.0).astype(bf16)
            edge = 64 * (1 - h)
            extra = jnp.where((lane == edge) | (lane == edge + 1), one, 0.0)
            vback[h, rows, :] = jnp.where(head_lanes[h], value, extra).astype(bf16)

    project(x, c)
    for i, h in in_turn:
        arrived(half(xb.at[x, 2 * (1 - c) + i], h), NUM["core_own"] + 2 * i + h)
    project(x, 1 - c)
    for i, h in in_turn:
        block = half(xb.at[1 - x, 2 * c + i], h)
        arrived(block, NUM["xn"] + 2 * i + h)
        number = NUM["core_far"] + 2 * i + h
        send(block, block, number, number, core_dev)
    for i in (0, 1):
        send(cot_in.at[i], cotb.at[x, z % 2], NUM["cot"] + i, NUM["cot"] + z % 2, peer(i), when=2 * c + i != z)
    project(1 - x, c)
    for i, h in in_turn:
        arrived(half(xb.at[1 - x, 2 * (1 - c) + i], h), NUM["core_far"] + 2 * i + h)
    project(1 - x, 1 - c)

    mine = pl.ds(pl.multiple_of(128 * me, 128), 128)
    for turn, (xx, cc) in enumerate(((0, 1 - c), (1, 1 - c), (0, c), (1, c))):
        rows = rows_of(xx, cc)
        q_rows = q[rows, :]
        total = jnp.zeros((256, 256), f32)
        for h in range(2):
            scores = mm_nt(jnp.where(head_lanes[h], q_rows, 0), k[...])
            prob = jnp.exp(scores).astype(bf16)
            probs[h, rows, :] = prob
            total = total + mm(prob, vaug[h])
        inverse = 1.0 / total[:, 128:256]
        attended = total[:, 0:128] * inverse
        att[rows, :] = attended
        inv[rows, :] = inverse
        obuf[turn] = attended.astype(bf16)
        there = abuf.at[pl.ds(256 * xx, 256), mine]
        if turn < 2:
            send(obuf.at[turn], there, NUM["o_diag"] + xx, NUM["o_diag"] + xx, diag_dev)
            send(obuf.at[turn], there, NUM["o_core"] + xx, NUM["o_core"] + xx, core_dev)
        else:
            send(obuf.at[turn], there, NUM["o_x"] + xx, NUM["o_x"] + xx, x_dev)
            abuf[256 * xx : 256 * xx + 256, mine] = attended.astype(bf16)

    for i in (0, 1):
        @pl.when(2 * c + i != z)
        def _():
            arrived(cotb.at[x, i], NUM["cot"] + i)
    pl.when(jnp.logical_not(crossing))(self_cot.wait)
    for i in (0, 1):
        send(cotb.at[x, i], cotb.at[x, i], NUM["cot_x"] + i, NUM["cot_x"] + i, x_dev)

    def norm(hidden):
        centred = hidden - jnp.mean(hidden, axis=-1, keepdims=True)
        scale = lax.rsqrt(jnp.mean(centred * centred, axis=-1, keepdims=True) + eps_norm)
        return centred * scale, scale

    def norm_back(grad, normalized, scale, gain):
        e = grad * gain
        return scale * (
            e - jnp.mean(e, axis=-1, keepdims=True)
            - normalized * jnp.mean(e * normalized, axis=-1, keepdims=True)
        )

    def column_sum(values):
        return jnp.sum(values, axis=0, keepdims=True)

    once = jnp.where(x == 0, 1.0, 0.0)
    land(wait_ffn)
    s1_parts = []
    for xx in (0, 1):
        there = pl.ds(256 * xx, 256)

        def columns_of(hx, hc):
            return pl.ds(pl.multiple_of(128 * (2 * hx + hc), 128), 128)

        arrived(abuf.at[there, columns_of(x, 1 - c)], NUM["o_core"] + xx)
        arrived(abuf.at[there, columns_of(1 - x, 1 - c)], NUM["o_diag"] + xx)
        arrived(abuf.at[there, columns_of(1 - x, c)], NUM["o_x"] + xx)
        start_x = xb[xx, pl.ds(2 * c, 2)].reshape(256, 512).astype(f32) + pair_row
        normalized, s1 = norm(start_x + (mm(abuf[there, :], wo[...]) + ob[...]))
        s1_parts.append(s1)
        n1[there, :] = normalized
        normed = normalized * g1[...] + b1[...]
        low = normed.astype(bf16)
        normed_low[there, :] = low
        ffn = jnp.zeros((256, 512), f32)
        for j in range(4):
            cols = pl.ds(512 * j, 512)
            pre = mm(low, wup[:, cols]) + ub[:, cols]
            cdf = 0.5 * (1.0 + lax.erf(pre * 0.7071067811865476))
            gelu_grad[there, cols] = cdf + pre * (jnp.exp(-0.5 * pre * pre) * 0.3989422804014327)
            act_low = (pre * cdf).astype(bf16)
            act[there, cols] = act_low
            ffn = ffn + mm(act_low, wdn[cols, :])
        normalized, s2 = norm((ffn + db[...]) + normed + start_x)
        n2[there, :] = normalized
        s2b[there, :] = jnp.broadcast_to(s2, (256, 128))
    own_half = pl.ds(pl.multiple_of(256 * x, 256), 256)
    lob[...] = (n2[own_half, :] * g2[...] + b2[...]).astype(bf16).reshape(2, 128, 512)

    def give_back(block, out, name):
        for i in (0, 1):
            send(block.at[i], out.at[z % 2], NUM[name] + i, NUM[name] + z % 2, peer(i), when=2 * c + i != z)

        @pl.when(jnp.logical_not(crossing))
        def _():
            out[z % 2] = block[z % 2]

    give_back(lob, lo_out, "lo")
    for i in (0, 1):
        arrived(cotb.at[1 - x, i], NUM["cot_x"] + i)
    for xx in (0, 1):
        there = pl.ds(256 * xx, 256)
        g = cotb[xx].reshape(256, 512).astype(f32)
        normalized = n2[there, :]
        gain_part, bias_part = column_sum(g * normalized), column_sum(g)
        grad = norm_back(g, normalized, s2b[there, 0:1], g2[...])
        second[there, :] = grad
        low = grad.astype(bf16)
        ffn_grad[there, :] = low
        down_part = column_sum(low.astype(f32))
        for at, part in ((14, gain_part), (15, bias_part), (13, down_part)):
            vecb[at : at + 1, :] = part * once if xx == 0 else vecb[at : at + 1, :] + part * once

    def number(n, step):
        return NUM["lane"] + 12 * n + step

    def fold(target, received):
        target[...] = (target[...].astype(f32) + received[...].astype(f32)).astype(bf16)

    def scatter(n, axis, last):
        if axis == "y":
            part = own.at[n, c, 1 - y, z] if last else own.at[n, c, 1 - y]
            send(part, r1.at[n, 0] if last else r1.at[n], number(n, 1), number(n, 1), y_dev)
        else:
            for d in (1, 2, 3):
                part = own.at[n, c, y, (z + d) % 4] if last else own.at[n, c, :, (z + d) % 4]
                send(part, r3.at[n, 3 - d, 0] if last else r3.at[n, 3 - d],
                     number(n, 1 + d), number(n, 5 - d), z_devs[d - 1])

    def collect(n, axis, last):
        if axis == "y":
            arrived(r1.at[n, 0] if last else r1.at[n], number(n, 1))
            parts = [r1.at[n, 0] if last else r1.at[n]]
        else:
            for d in (1, 2, 3):
                arrived(r3.at[n, d - 1, 0] if last else r3.at[n, d - 1], number(n, 1 + d))
            parts = [r3.at[n, d, 0] if last else r3.at[n, d] for d in range(3)]
        if last:
            target = own.at[n, c, y, z]
        else:
            target = own.at[n, c, y] if axis == "y" else own.at[n, c, :, z]
        value = target[...].astype(f32)
        for part in parts:
            value = value + part[...].astype(f32)
        if last:
            target = full.at[n, x, c, y, z]
        target[...] = value.astype(bf16)

    def region(buffer, n, done, **other):
        place = dict(x=x, y=y, z=z) | other
        at = {axis: slice(None) if axis in done else place[axis] for axis in "xyz"}
        return buffer.at[n, at["x"], c, at["y"], at["z"]]

    def spread(buffer, n, number_of, order, stage):
        part = region(buffer, n, order[:stage])
        if stage == 3:
            send(part, part, number_of(10), number_of(10), core_dev)
        elif order[stage] == "z":
            for d in (1, 2, 3):
                send(part, part, number_of(4 + d), number_of(8 - d), z_devs[d - 1])
        else:
            at, device = {"x": (9, x_dev), "y": (8, y_dev)}[order[stage]]
            send(part, part, number_of(at), number_of(at), device)

    def gather(buffer, n, number_of, order, stage):
        if stage == 3:
            arrived(buffer.at[n, :, 1 - c], number_of(10))
        elif order[stage] == "z":
            for d in (1, 2, 3):
                arrived(region(buffer, n, order[:stage], z=(z + d) % 4), number_of(4 + d))
        elif order[stage] == "x":
            arrived(region(buffer, n, order[:stage], x=1 - x), number_of(9))
        else:
            arrived(region(buffer, n, order[:stage], y=1 - y), number_of(8))

    def lane_step(n, step):
        scatter_order, order = SCATTER[n], GATHER[n]
        number_of = functools.partial(number, n)
        if step == 0:
            arrived(r0.at[n], number(n, 0))
            fold(own.at[n, c], r0.at[n])
            scatter(n, scatter_order[0], False)
        elif step == 1:
            collect(n, scatter_order[0], False)
            scatter(n, scatter_order[1], True)
        elif step == 2:
            collect(n, scatter_order[1], True)
            spread(full, n, number_of, order, 0)
        else:
            gather(full, n, number_of, order, step - 3)
            if step < 6:
                spread(full, n, number_of, order, step - 2)

    own_columns = pl.ds(pl.multiple_of(256 * x, 256), 256)

    def lane_fill(n):
        if n < 4:
            value = mm_tn(act[:, pl.ds(pl.multiple_of(512 * n + 256 * x, 256), 256)], ffn_grad[...])
        elif n < 8:
            value = mm_tn(normed_low[:, own_columns], pre_grad[:, pl.ds(512 * (n - 4), 512)])
        else:
            value = mm_tn(abuf[:, own_columns], attn_grad[...])
        own[n] = value.astype(bf16).reshape(2, 2, 4, 16, 512)
        send(own.at[n, 1 - c], r0.at[n], number(n, 0), number(n, 0), core_dev)

    def ffn_back(j):
        cols = pl.ds(512 * j, 512)
        for xx in (0, 1):
            there = pl.ds(256 * xx, 256)
            grad = (mm_nt(ffn_grad[there, :], wdn[cols, :]) * gelu_grad[there, cols]).astype(bf16)
            pre_grad[there, cols] = grad
            part = column_sum(grad.astype(f32)) * once
            vecb[16 + j : 17 + j, :] = part if xx == 0 else vecb[16 + j : 17 + j, :] + part
            term = mm_nt(grad, wup[:, cols])
            normed_grad[there, :] = (second if j == 0 else normed_grad)[there, :] + term

    def first_back():
        for xx in (0, 1):
            there = pl.ds(256 * xx, 256)
            grad, normalized = normed_grad[there, :], n1[there, :]
            first_grad = norm_back(grad, normalized, s1_parts[xx], g1[...])
            low = first_grad.astype(bf16)
            attn_grad[there, :] = low
            for at, part in ((11, column_sum(grad * normalized)), (12, column_sum(grad)),
                             (10, column_sum(low.astype(f32)))):
                vecb[at : at + 1, :] = part * once if xx == 0 else vecb[at : at + 1, :] + part * once
            second[there, :] = second[there, :] + first_grad
        res[...] = second[own_half, :]
        low = attn_grad[...]

        def heads(cc):
            return pl.ds(pl.multiple_of(128 * (2 * x + cc), 128), 128)

        dob[...] = mm_nt(low, wo[heads(1 - c), :]).astype(bf16)
        send(dob, dor.at[c], NUM["do"], NUM["do"], core_dev)
        dor[c] = mm_nt(low, wo[heads(c), :]).astype(bf16)

    turns = ((0, c), (1, c), (0, 1 - c), (1, 1 - c))

    def attention_back(turn):
        xx, cc = turns[turn]
        if turn == 2:
            arrived(dor.at[cc], NUM["do"])
        rows = rows_of(xx, cc)
        d_out = dor[cc, 256 * xx : 256 * xx + 256, :].astype(f32)
        numer_grad = d_out * inv[rows, :]
        product = numer_grad.astype(bf16).astype(f32) * att[rows, :]
        q_rows = q[rows, :]
        dq_rows = jnp.zeros((256, 128), f32)
        for h in range(2):
            total = -jnp.sum(jnp.where(head_lanes[h], product, 0.0), axis=1, keepdims=True)
            high = total.astype(bf16).astype(f32)
            edge = 64 * (1 - h)
            rest = jnp.where(lane == edge, high, jnp.where(lane == edge + 1, total - high, 0.0))
            grad_low = jnp.where(head_lanes[h], numer_grad, rest).astype(bf16)
            prob = probs[h, rows, :]
            score_grad = (prob.astype(f32) * mm_nt(grad_low, vback[h])).astype(bf16)
            dq_rows = dq_rows + jnp.where(head_lanes[h], mm(score_grad, k[...]), 0.0)
            part = slice(64 * h, 64 * h + 64)
            dk_part = mm(jnp.transpose(q_rows)[part, :], score_grad)
            dv_part = mm(jnp.transpose(grad_low)[part, :], prob)
            dkt[part, :] = dk_part if turn == 0 else dkt[part, :] + dk_part
            dvt[part, :] = dv_part if turn == 0 else dvt[part, :] + dv_part
        dqkv[rows, 0:128] = (dq_rows * 0.125).astype(bf16)

    def projection_grads():
        for xx in (0, 1):
            for cc in (0, 1):
                rows = pl.ds(512 * xx + 256 * cc, 256)
                dqkv[rows, 128:256] = jnp.transpose(dkt[:, rows]).astype(bf16)
                dqkv[rows, 256:384] = jnp.where(usable_rows(xx, cc), jnp.transpose(dvt[:, rows]), 0.0).astype(bf16)

    def qnumber(t, step):
        return NUM["qkv"] + 12 * t + step

    def projection_weights(t):
        value = mm_tn(lowb[...], dqkv[:, 128 * t : 128 * t + 128])
        qown[t] = value.astype(bf16).reshape(2, 4, 64, 128)
        send(qown.at[t, 1 - y], qr1.at[t], qnumber(t, 0), qnumber(t, 0), y_dev)

    def projection_step(t, step):
        number_of, order = functools.partial(qnumber, t), QGATHER[t]
        if step == 0:
            arrived(qr1.at[t], qnumber(t, 0))
            fold(qown.at[t, y], qr1.at[t])
            for d in (1, 2, 3):
                send(qown.at[t, y, (z + d) % 4], qr3.at[t, 3 - d], qnumber(t, d), qnumber(t, 4 - d), z_devs[d - 1])
        elif step == 1:
            for d in (1, 2, 3):
                arrived(qr3.at[t, d - 1], qnumber(t, d))
            value = qown[t, y, z].astype(f32)
            for d in range(3):
                value = value + qr3[t, d].astype(f32)
            qfull[t, x, c, y, z] = value.astype(bf16)
            spread(qfull, t, number_of, order, 0)
        else:
            gather(qfull, t, number_of, order, step - 2)
            if step < 5:
                spread(qfull, t, number_of, order, step - 1)

    def input_back(step):
        xx, cc = ((1 - x, 1 - c), (x, 1 - c), (1 - x, c), (x, c))[step]
        block = mm_nt(dqkv[rows_of(xx, cc), :], wq[...])
        vecb[20:21, :] = column_sum(block) if step == 0 else vecb[20:21, :] + column_sum(block)
        if step < 2:
            dxb[step] = block.astype(bf16)
            send(dxb.at[step], dxr0.at[step], NUM["dx_core"] + step, NUM["dx_core"] + step, core_dev)
        elif step == 2:
            arrived(dxr0.at[0], NUM["dx_core"])
            dxb[2] = (block + dxr0[0].astype(f32)).astype(bf16)
            send(dxb.at[2], dxr1, NUM["dx_x"], NUM["dx_x"], x_dev)
        else:
            arrived(dxr0.at[1], NUM["dx_core"] + 1)
            dxo[...] = block + dxr0[1].astype(f32) + res[...]

    def input_out():
        arrived(dxr1, NUM["dx_x"])
        igb[...] = (dxo[...] + dxr1[...].astype(f32)).astype(bf16).reshape(2, 128, 512)
        give_back(igb, ig_out, "ig")

    def vectors(step):
        if step == 0:
            group_iota = lax.broadcasted_iota(jnp.int32, (8, 512), 0).astype(f32)
            column_total = vecb[20:21, :] + column_sum(res[...])
            vecb[0:8, :] = jnp.where(group_iota == group_row, column_total, 0.0)
            vecb[8:10, :] = jnp.zeros((2, 512), f32)
            vecb[8:9, mine] = column_sum(dqkv[:, 0:128].astype(f32))
            vecb[9:10, mine] = column_sum(dqkv[:, 256:384].astype(f32))
            vecb[20:24, :] = jnp.zeros((4, 512), f32)
            send(vecb, vecr.at[0], NUM["vec"], NUM["vec"], core_dev)
        elif step < 4:
            level = step - 1
            arrived(vecr.at[level], NUM["vec"] + level)
            value = (vecb[...] if level == 0 else vecr[2 + level]) + vecr[level]
            if level < 2:
                vecr[3 + level] = value
                send(vecr.at[3 + level], vecr.at[level + 1], NUM["vec"] + level + 1, NUM["vec"] + level + 1,
                     (x_dev, y_dev)[level])
            else:
                vecz[z] = value
                for d in (1, 2, 3):
                    send(vecz.at[z], vecz.at[z], NUM["vec"] + 2 + d, NUM["vec"] + 6 - d, z_devs[d - 1])
        else:
            for d in (1, 2, 3):
                arrived(vecz.at[(z + d) % 4], NUM["vec"] + 2 + d)
            value = vecz[0]
            for t in range(1, 4):
                value = value + vecz[t]
            vec_out[...] = value

    tasks = {(NORM, 0, 0): first_back, (SPLIT, 0, 0): projection_grads, (RETURN, 0, 0): input_out}
    for kind, task, counts in (
        (FILL, lane_fill, (LANES,)), (FFN, ffn_back, (4,)), (ATTN, attention_back, (4,)), (WEIGHT, projection_weights, (3,)),
        (INPUT, input_back, (4,)), (SMALL, vectors, (5,)), (LANE, lane_step, (LANES, 7)), (PART, projection_step, (3, 6)),
    ):
        for at in range(counts[0]):
            for step in range(counts[-1]) if len(counts) == 2 else (0,):
                tasks[kind, at, step] = functools.partial(task, *(at, step)[: len(counts)])
    for entry in ORDER:
        tasks.pop(entry)()
    assert not tasks

    for name, out in (("lo", lo_out), ("ig", ig_out)):
        for i in (0, 1):
            @pl.when(2 * c + i != z)
            def _():
                arrived(out.at[i], NUM[name] + i)
    land([copy for copy in local_copies if copy is not None])
    for copy, when in pending:
        if when is None:
            copy.wait_send()
        else:
            pl.when(when)(copy.wait_send)


VECTOR_ROWS = (8, 9, 10, 11, 12, 13, 14, 15)


def finish(lo, ig, full, qfull, vec, *refs):
    lo_out, ig_out, down_out, up_out, out_out, qkv_out, pair_out = refs[:7]
    vector_outs, up_bias_out = refs[7:15], refs[15]
    lo_wide, ig_wide, full_wide, qkv_wide, rows, up_bias, sems = *refs[16:20], refs[20:28], refs[28], refs[29]
    writes = []

    def write(src, dst):
        made = pltpu.make_async_copy(src, dst, sems.at[len(writes)])
        made.start()
        writes.append(made)

    for n in range(LANES):
        for half in range(2):
            at = pl.ds(256 * half, 256)
            full_wide[n, at, :] = full[n, half].reshape(256, 512).astype(f32)
            if n < 4:
                write(full_wide.at[n, at], down_out.at[pl.ds(512 * n + 256 * half, 256)])
            elif n < 8:
                write(full_wide.at[n, at], up_out.at[at, pl.ds(512 * (n - 4), 512)])
            else:
                write(full_wide.at[n, at], out_out.at[at])
    for t in range(3):
        for h in range(4):
            columns = pl.ds(512 * t + 128 * h, 128)
            qkv_wide[:, columns] = qfull[t, h // 2, h % 2].reshape(512, 128).astype(f32)
        columns = pl.ds(512 * t, 512)
        write(qkv_wide.at[:, columns], qkv_out.at[:, columns])
    for block, wide, out in ((lo, lo_wide, lo_out), (ig, ig_wide, ig_out)):
        wide[...] = block[...].astype(f32)
        write(wide, out)
    write(vec.at[pl.ds(0, 8)], pair_out)
    for at, row, out in zip(VECTOR_ROWS, rows, vector_outs):
        row[...] = vec[at : at + 1, :]
        write(row, out)
    for j in range(4):
        up_bias[:, 512 * j : 512 * j + 512] = vec[16 + j : 17 + j, :]
    write(up_bias, up_bias_out)
    for made in writes:
        made.wait()


def pair_plan(mesh):
    return dict(mesh.shape) == {"batch": 4, "seq": 8}


def fused_local(
    block_input, cotangent, groups, lengths, pair_table, qkv_weight, q_bias, v_bias, out_weight,
    out_bias, norm1_gain, norm1_bias, up_weight, up_bias, down_weight, down_bias, norm2_gain, norm2_bias,
):
    any_spec, smem = pl.BlockSpec(memory_space=pl.ANY), pl.BlockSpec(memory_space=pltpu.SMEM)

    def row(vector):
        return vector[None, :]

    operands = (
        block_input, cotangent, groups, lengths, pair_table, qkv_weight, row(q_bias), row(v_bias),
        out_weight, row(out_bias), row(norm1_gain), row(norm1_bias), up_weight, row(up_bias),
        down_weight, row(down_bias), row(norm2_gain), row(norm2_bias),
    )
    in_specs = [smem if i in (2, 3) else any_spec for i in range(len(operands))]
    vmem = pl.BlockSpec(memory_space=pltpu.VMEM)
    out_shape = [
        pltpu.VMEM(shape, dtype)
        for shape, dtype in (
            ((2, 128, 512), bf16), ((2, 128, 512), bf16), ((LANES, 2, 2, 2, 4, 16, 512), bf16),
            ((3, 2, 2, 2, 4, 64, 128), bf16), ((24, 512), f32),
        )
    ]
    scratch = [
        pltpu.VMEM(shape, dtype)
        for shape, dtype in (
            ((2, 4, 128, 512), bf16), ((1024, 512), bf16), ((2, 2, 128, 512), bf16),
            ((8, 512), f32), ((8, 512), f32), ((8, 512), f32),
            ((512, 384), bf16), ((512, 512), bf16), ((512, 2048), bf16), ((2048, 512), bf16),
            ((1, 512), f32), ((1, 512), f32), ((1, 512), f32), ((1, 512), f32), ((1, 512), f32),
            ((1, 2048), f32), ((1, 512), f32), ((1, 512), f32), ((1, 512), f32),
            ((1024, 128), bf16), ((1024, 128), bf16),
            ((2, 1024, 256), bf16), ((2, 1024, 128), bf16),
            ((1024, 128), f32), ((1024, 128), f32),
            ((4, 256, 128), bf16), ((512, 512), bf16),
            ((512, 2048), f32), ((512, 2048), bf16), ((512, 2048), bf16),
            ((256, 512), f32), ((2, 128, 512), bf16), ((2, 128, 512), bf16),
            ((512, 512), f32), ((512, 512), f32), ((512, 128), f32), ((512, 512), bf16),
            ((512, 512), bf16), ((512, 512), bf16), ((512, 512), f32), ((512, 512), f32),
            ((512, 128), bf16), ((2, 512, 128), bf16), ((2, 1024, 1024), bf16),
            ((128, 1024), f32), ((128, 1024), f32), ((1024, 384), bf16),
            ((3, 256, 512), bf16), ((2, 256, 512), bf16), ((256, 512), bf16), ((256, 512), f32),
            ((24, 512), f32), ((5, 24, 512), f32), ((4, 24, 512), f32),
            ((LANES, 2, 2, 4, 16, 512), bf16), ((LANES, 2, 4, 16, 512), bf16), ((LANES, 4, 16, 512), bf16),
            ((LANES, 3, 2, 16, 512), bf16),
            ((3, 2, 4, 64, 128), bf16), ((3, 4, 64, 128), bf16), ((3, 3, 64, 128), bf16),
        )
    ] + [
        pltpu.SemaphoreType.DMA((NUM.count,)),
        pltpu.SemaphoreType.DMA((NUM.count,)),
        pltpu.SemaphoreType.DMA((LOCAL,)),
    ]
    results = pl.pallas_call(
        fused,
        out_shape=out_shape,
        in_specs=in_specs,
        out_specs=[vmem] * len(out_shape),
        scratch_shapes=scratch,
        compiler_params=pltpu.CompilerParams(
            collective_id=0, has_side_effects=True, vmem_limit_bytes=54 * 2**20
        ),
    )(*operands)
    shapes = [(2, 128, 512)] * 2 + [(2048, 512), (512, 2048), (512, 512), (512, 1536), (8, 512)]
    shapes += [(1, 512)] * 8 + [(1, 2048)]
    scratch_sizes = [(2, 128, 512)] * 2 + [(LANES, 512, 512), (512, 1536)] + [(1, 512)] * 8 + [(1, 2048)]
    results = pl.pallas_call(
        finish,
        out_shape=[jax.ShapeDtypeStruct(shape, f32) for shape in shapes],
        in_specs=[vmem] * 5,
        out_specs=[any_spec] * len(shapes),
        scratch_shapes=[pltpu.VMEM(shape, f32) for shape in scratch_sizes] + [pltpu.SemaphoreType.DMA((40,))],
        compiler_params=pltpu.CompilerParams(vmem_limit_bytes=40 * 2**20),
    )(*results)
    layer_out, input_grad, down_grad, up_grad, out_grad, qkv_grad, pair_grad = results[:7]
    q_grad, v_grad, ob_grad, g1_grad, b1_grad, db_grad, g2_grad, b2_grad = [r.reshape(512) for r in results[7:15]]
    return (
        layer_out, input_grad, pair_grad, qkv_grad, q_grad, v_grad,
        out_grad, ob_grad, g1_grad, b1_grad, up_grad, results[15].reshape(2048), down_grad, db_grad, g2_grad, b2_grad,
    )


def solution(mesh):
    in_specs = (
        P("batch", "seq", None),
        P("batch", "seq", None),
        P("batch"),
        P("batch"),
        P(),
        P(),
        P(),
        P(),
        P(),
        P(),
        P(),
        P(),
        P(),
        P(),
        P(),
        P(),
        P(),
        P(),
    )
    out_specs = (
        P("batch", "seq", None),
        P("batch", "seq", None),
        P(),
        P(),
        P(),
        P(),
        P(),
        P(),
        P(),
        P(),
        P(),
        P(),
        P(),
        P(),
        P(),
        P(),
    )
    return jax.shard_map(fused_local if pair_plan(mesh) else local, mesh=mesh, in_specs=in_specs, out_specs=out_specs, check_vma=False)
```

```python
import functools

import jax
import jax.numpy as jnp
from jax import lax
from jax.experimental import pallas as pl
from jax.experimental.pallas import tpu as pltpu
from jax.sharding import PartitionSpec as P

HEADS = 8


highest = lax.Precision.HIGHEST
eps_norm = 1e-05


def layer_norm(hidden, norm_gain, norm_shift):
    row_mean = jnp.mean(hidden, axis=-1, keepdims=True)
    centred = hidden - row_mean
    spread = jnp.mean(centred * centred, axis=-1, keepdims=True)
    return centred * lax.rsqrt(spread + eps_norm) * norm_gain + norm_shift


def exact_gelu(pre_act):
    return jax.nn.gelu(pre_act, approximate=False)


def block_size():
    return 512


def to_heads(flat_rows, head_count):
    return flat_rows.reshape(
        flat_rows.shape[0], flat_rows.shape[1], head_count, flat_rows.shape[2] // head_count
    )


def masked_exp(query_block, key_block, key_first, row_lengths, score_scale):
    scores = (
        jnp.einsum("rihd,rjhd->rhij", query_block, key_block, preferred_element_type=jnp.float32)
        * score_scale
    )
    places = key_first + jnp.arange(key_block.shape[1], dtype=jnp.int32)
    usable = places[None, :] < row_lengths[:, None]
    return jnp.where(usable[:, None, None, :], jnp.exp(scores), 0.0)


def forward_piece(
    running, key_piece, value_piece, query_heads, row_lengths, score_scale, head_count
):
    piece_len = key_piece.shape[1]
    block_len = block_size()
    key_all = to_heads(key_piece, head_count)
    value_all = to_heads(value_piece, head_count)

    def forward_one_block(block_index, partial_sums):
        numerator, denominator = partial_sums
        block_first = block_index * block_len
        key_block = lax.dynamic_slice_in_dim(key_all, block_first, block_len, 1)
        value_block = lax.dynamic_slice_in_dim(value_all, block_first, block_len, 1)
        exp_scores = masked_exp(query_heads, key_block, block_first, row_lengths, score_scale)
        denominator = denominator + jnp.sum(exp_scores, axis=-1)
        numerator = numerator + jnp.einsum(
            "rhij,rjhd->rihd",
            exp_scores.astype(jnp.bfloat16),
            value_block,
            preferred_element_type=jnp.float32,
        )
        return (numerator, denominator)

    return lax.fori_loop(0, piece_len // block_len, forward_one_block, running)


def key_side(
    running,
    query_piece,
    grad_piece,
    total_piece,
    key_heads,
    value_heads,
    key_first,
    row_lengths,
    score_scale,
    head_count,
):
    piece_len = query_piece.shape[1]
    block_len = block_size()
    query_all = to_heads(query_piece.astype(jnp.bfloat16), head_count)
    grad_all = to_heads(grad_piece, head_count)
    value_wide = value_heads.astype(jnp.float32)

    def key_one_block(block_index, partial_grads):
        key_grad, value_grad = partial_grads
        block_first = block_index * block_len
        query_block = lax.dynamic_slice_in_dim(query_all, block_first, block_len, 1)
        grad_block = lax.dynamic_slice_in_dim(grad_all, block_first, block_len, 1)
        total_block = lax.dynamic_slice_in_dim(total_piece, block_first, block_len, 1)
        exp_scores = masked_exp(query_block, key_heads, key_first, row_lengths, score_scale)
        prob_grad = jnp.einsum(
            "rihd,rjhd->rhij",
            grad_block,
            value_wide,
            precision=highest,
            preferred_element_type=jnp.float32,
        )
        shift_grad = jnp.transpose(total_block, (0, 2, 1))[..., None]
        score_grad = (exp_scores * (prob_grad + shift_grad)).astype(jnp.bfloat16)
        key_grad = (
            key_grad
            + jnp.einsum(
                "rhij,rihd->rjhd", score_grad, query_block, preferred_element_type=jnp.float32
            )
            * score_scale
        )
        exp_low = exp_scores.astype(jnp.bfloat16).astype(jnp.float32)
        value_grad = value_grad + jnp.einsum(
            "rhij,rihd->rjhd",
            exp_low,
            grad_block,
            precision=highest,
            preferred_element_type=jnp.float32,
        )
        return (key_grad, value_grad)

    return lax.fori_loop(0, piece_len // block_len, key_one_block, running)


def query_side(
    running,
    key_piece,
    value_piece,
    query_heads,
    grad_heads,
    total_here,
    row_lengths,
    score_scale,
    head_count,
):
    piece_len = key_piece.shape[1]
    block_len = block_size()
    key_all = to_heads(key_piece, head_count)
    value_all = to_heads(value_piece, head_count)

    def query_one_block(block_index, query_grad):
        block_first = block_index * block_len
        key_block = lax.dynamic_slice_in_dim(key_all, block_first, block_len, 1)
        value_block = lax.dynamic_slice_in_dim(value_all, block_first, block_len, 1)
        exp_scores = masked_exp(query_heads, key_block, block_first, row_lengths, score_scale)
        prob_grad = jnp.einsum(
            "rihd,rjhd->rhij",
            grad_heads,
            value_block.astype(jnp.float32),
            precision=highest,
            preferred_element_type=jnp.float32,
        )
        score_grad = (exp_scores * (prob_grad + total_here[..., None])).astype(jnp.bfloat16)
        return (
            query_grad
            + jnp.einsum(
                "rhij,rjhd->rihd", score_grad, key_block, preferred_element_type=jnp.float32
            )
            * score_scale
        )

    return lax.fori_loop(0, piece_len // block_len, query_one_block, running)


def local(
    block_input,
    cotangent,
    groups,
    lengths,
    pair_table,
    qkv_weight,
    q_bias,
    v_bias,
    out_weight,
    out_bias,
    norm1_gain,
    norm1_bias,
    up_weight,
    up_bias,
    down_weight,
    down_bias,
    norm2_gain,
    norm2_bias,
):
    row_count, shard_len, model_width = block_input.shape
    head_count = HEADS
    head_size = model_width // head_count
    score_scale = head_size ** (-0.5)
    key_offset = lax.axis_index("seq") * shard_len
    pair_onehot = (
        groups[:, None] == jnp.arange(pair_table.shape[0], dtype=jnp.int32)[None, :]
    ).astype(jnp.float32)
    lifted = jnp.dot(pair_onehot, pair_table, precision=highest)
    start_x = block_input.astype(jnp.float32) + lifted[:, None, :]
    lowered = start_x.astype(jnp.bfloat16)
    projected = jnp.einsum("rtd,de->rte", lowered, qkv_weight, preferred_element_type=jnp.float32)
    query_rows = (projected[:, :, :model_width] + q_bias).astype(jnp.bfloat16)
    key_rows = projected[:, :, model_width : 2 * model_width].astype(jnp.bfloat16)
    value_rows = (projected[:, :, 2 * model_width :] + v_bias).astype(jnp.bfloat16)
    query_heads = to_heads(query_rows, head_count)
    key_heads = to_heads(key_rows, head_count)
    value_heads = to_heads(value_rows, head_count)
    zero_heads = jnp.zeros((row_count, shard_len, head_count, head_size), jnp.float32)
    zero_totals = jnp.zeros((row_count, head_count, shard_len), jnp.float32)
    incoming = (
        lax.all_gather(key_rows, "seq", axis=1, tiled=True),
        lax.all_gather(value_rows, "seq", axis=1, tiled=True),
    )
    numerator, denominator = forward_piece(
        (zero_heads, zero_totals),
        incoming[0],
        incoming[1],
        query_heads,
        lengths,
        score_scale,
        head_count,
    )
    inverse = 1.0 / jnp.transpose(denominator, (0, 2, 1))[..., None]
    attended = numerator * inverse
    attended_low = attended.reshape(row_count, shard_len, model_width).astype(jnp.bfloat16)
    attn_out = (
        jnp.einsum("rtd,de->rte", attended_low, out_weight, preferred_element_type=jnp.float32)
        + out_bias
    )
    normed, norm1_back = jax.vjp(layer_norm, start_x + attn_out, norm1_gain, norm1_bias)
    normed_low = normed.astype(jnp.bfloat16)
    pre_act = (
        jnp.einsum("rtd,df->rtf", normed_low, up_weight, preferred_element_type=jnp.float32)
        + up_bias
    )
    activated, gelu_back = jax.vjp(exact_gelu, pre_act)
    activated_low = activated.astype(jnp.bfloat16)
    ffn_out = (
        jnp.einsum("rtf,fd->rtd", activated_low, down_weight, preferred_element_type=jnp.float32)
        + down_bias
    )
    layer_out, norm2_back = jax.vjp(layer_norm, ffn_out + normed + start_x, norm2_gain, norm2_bias)
    second_grad, norm2_gain_grad, norm2_bias_grad = norm2_back(cotangent.astype(jnp.float32))
    ffn_grad = second_grad.astype(jnp.bfloat16)
    down_bias_grad = jnp.sum(ffn_grad.astype(jnp.float32), axis=(0, 1))
    down_weight_grad = jnp.einsum(
        "rtf,rtd->fd", activated_low, ffn_grad, preferred_element_type=jnp.float32
    )
    act_grad = jnp.einsum("rtd,fd->rtf", ffn_grad, down_weight, preferred_element_type=jnp.float32)
    pre_grad = gelu_back(act_grad)[0].astype(jnp.bfloat16)
    up_bias_grad = jnp.sum(pre_grad.astype(jnp.float32), axis=(0, 1))
    up_weight_grad = jnp.einsum(
        "rtd,rtf->df", normed_low, pre_grad, preferred_element_type=jnp.float32
    )
    normed_grad = second_grad + jnp.einsum(
        "rtf,df->rtd", pre_grad, up_weight, preferred_element_type=jnp.float32
    )
    first_grad, norm1_gain_grad, norm1_bias_grad = norm1_back(normed_grad)
    attn_grad = first_grad.astype(jnp.bfloat16)
    out_bias_grad = jnp.sum(attn_grad.astype(jnp.float32), axis=(0, 1))
    out_weight_grad = jnp.einsum(
        "rtd,rte->de", attended_low, attn_grad, preferred_element_type=jnp.float32
    )
    attended_grad = to_heads(
        jnp.einsum("rte,de->rtd", attn_grad, out_weight, preferred_element_type=jnp.float32),
        head_count,
    )
    numer_grad = attended_grad * inverse
    total_grad = -jnp.sum(attended_grad * attended, axis=-1) * inverse[..., 0]
    grad_rows = numer_grad.reshape(row_count, shard_len, model_width)
    total_here = jnp.transpose(total_grad, (0, 2, 1))
    incoming = (
        lax.all_gather(query_rows.astype(jnp.float32), "seq", axis=1, tiled=True),
        lax.all_gather(grad_rows, "seq", axis=1, tiled=True),
        lax.all_gather(total_grad, "seq", axis=1, tiled=True),
    )
    key_grad, value_grad = key_side(
        (zero_heads, zero_heads),
        incoming[0],
        incoming[1],
        incoming[2],
        key_heads,
        value_heads,
        key_offset,
        lengths,
        score_scale,
        head_count,
    )
    incoming = (
        lax.all_gather(key_rows, "seq", axis=1, tiled=True),
        lax.all_gather(value_rows, "seq", axis=1, tiled=True),
    )
    query_grad = query_side(
        zero_heads,
        incoming[0],
        incoming[1],
        query_heads,
        numer_grad,
        total_here,
        lengths,
        score_scale,
        head_count,
    )
    flat_shape = (row_count, shard_len, model_width)
    query_low = query_grad.reshape(flat_shape).astype(jnp.bfloat16)
    key_low = key_grad.reshape(flat_shape).astype(jnp.bfloat16)
    value_low = value_grad.reshape(flat_shape).astype(jnp.bfloat16)
    qkv_grad = jnp.concatenate([query_low, key_low, value_low], axis=-1)
    qkv_weight_grad = jnp.einsum(
        "rtd,rte->de", lowered, qkv_grad, preferred_element_type=jnp.float32
    )
    q_bias_grad = jnp.sum(query_low.astype(jnp.float32), axis=(0, 1))
    v_bias_grad = jnp.sum(value_low.astype(jnp.float32), axis=(0, 1))
    input_grad = (
        jnp.einsum("rte,de->rtd", qkv_grad, qkv_weight, preferred_element_type=jnp.float32)
        + first_grad
        + second_grad
    )
    pair_table_grad = jnp.dot(
        jnp.transpose(pair_onehot), jnp.sum(input_grad, axis=1), precision=highest
    )
    summed = lax.psum(
        (
            pair_table_grad,
            qkv_weight_grad,
            q_bias_grad,
            v_bias_grad,
            out_weight_grad,
            out_bias_grad,
            norm1_gain_grad,
            norm1_bias_grad,
            up_weight_grad,
            up_bias_grad,
            down_weight_grad,
            down_bias_grad,
            norm2_gain_grad,
            norm2_bias_grad,
        ),
        ("batch", "seq"),
    )
    return (
        layer_out,
        input_grad,
        summed[0],
        summed[1],
        summed[2],
        summed[3],
        summed[4],
        summed[5],
        summed[6],
        summed[7],
        summed[8],
        summed[9],
        summed[10],
        summed[11],
        summed[12],
        summed[13],
    )


MESH = pl.DeviceIdType.MESH
f32, bf16 = jnp.float32, jnp.bfloat16
LANES = 9


def mm(a, b):
    return jnp.dot(a, b, preferred_element_type=f32)


def mm_nt(a, b):
    return lax.dot_general(a, b, (((1,), (1,)), ((), ())), preferred_element_type=f32)


def mm_tn(a, b):
    return lax.dot_general(a, b, (((0,), (0,)), ((), ())), preferred_element_type=f32)


class Numbers:
    def __init__(self):
        self.count = 0
        self.first = {}

    def take(self, name, size=1):
        self.first[name] = self.count
        self.count += size

    def __getitem__(self, name):
        return self.first[name]


def semaphore_numbers():
    numbers = Numbers()
    for name, size in (
        ("x", 4), ("cot", 2), ("lo", 2), ("ig", 2), ("cot_x", 2),
        ("xn", 4), ("core_own", 4), ("core_far", 4), ("meta", 1),
        ("do", 1), ("dx_core", 2), ("dx_x", 1), ("vec", 6),
        ("lane", LANES * 12), ("qkv", 3 * 12),
    ):
        numbers.take(name, size)
    return numbers


NUM = semaphore_numbers()
LOCAL = 17 + 2

SCATTER = ('yz', 'yz', 'yz', 'yz', 'yw', 'yw', 'yw', 'yw', 'yw')
GATHER = ('wxy', 'wxy', 'zxy', 'wyx', 'wxy', 'wxy', 'zxy', 'wyx', 'zyx')
QSCATTER = ('yw', 'yw', 'yw')
QGATHER = ('yzx', 'yxz', 'zxy')
FILL, LANE, FFN, NORM, ATTN, SPLIT, WEIGHT, PART, INPUT, RETURN, SMALL, PROBS = range(12)
ORDER = (
    (FILL, 1, 0), (FFN, 0, 0), (FILL, 2, 0), (FILL, 3, 0), (FILL, 0, 0), (LANE, 1, 0), (FFN, 1, 0),
    (FFN, 2, 0), (LANE, 2, 0), (FFN, 3, 0), (LANE, 3, 0), (LANE, 0, 0), (FILL, 6, 0), (FILL, 4, 0),
    (FILL, 7, 0), (NORM, 0, 0), (LANE, 1, 1), (LANE, 4, 0), (ATTN, 0, 0), (LANE, 2, 1), (ATTN, 1, 0),
    (LANE, 3, 1), (LANE, 7, 0), (LANE, 6, 0), (FILL, 8, 0), (FILL, 5, 0), (PROBS, 1, 0), (LANE, 1, 2),
    (LANE, 0, 1), (LANE, 8, 0), (LANE, 5, 0), (PROBS, 0, 0), (LANE, 4, 1), (LANE, 2, 2), (ATTN, 2, 0),
    (LANE, 7, 1), (ATTN, 3, 0), (LANE, 1, 3), (LANE, 3, 2), (SPLIT, 0, 0), (WEIGHT, 2, 0), (LANE, 8, 1),
    (LANE, 0, 2), (WEIGHT, 1, 0), (WEIGHT, 0, 0), (LANE, 4, 2), (LANE, 6, 1), (INPUT, 0, 0), (INPUT, 1, 0),
    (LANE, 5, 1), (LANE, 2, 3), (LANE, 7, 2), (LANE, 1, 4), (INPUT, 2, 0), (INPUT, 3, 0), (LANE, 3, 3),
    (SMALL, 0, 0), (PART, 2, 0), (LANE, 8, 2), (LANE, 0, 3), (SMALL, 1, 0), (PART, 1, 0), (LANE, 4, 3),
    (LANE, 6, 2), (LANE, 2, 4), (LANE, 5, 2), (PART, 0, 0), (LANE, 7, 3), (LANE, 3, 4), (LANE, 1, 5),
    (PART, 2, 1), (LANE, 8, 3), (LANE, 0, 4), (PART, 1, 1), (LANE, 4, 4), (LANE, 6, 3), (LANE, 2, 5),
    (LANE, 5, 3), (PART, 0, 1), (LANE, 7, 4), (LANE, 2, 6), (LANE, 3, 5), (PART, 2, 2), (RETURN, 0, 0),
    (SMALL, 2, 0), (LANE, 8, 4), (PART, 1, 2), (LANE, 1, 6), (LANE, 4, 5), (LANE, 0, 5), (LANE, 1, 7),
    (LANE, 6, 4), (SMALL, 3, 0), (LANE, 5, 4), (PART, 0, 2), (LANE, 3, 6), (LANE, 7, 5), (LANE, 8, 5),
    (PART, 1, 3), (LANE, 4, 6), (LANE, 3, 7), (PART, 2, 3), (LANE, 6, 5), (LANE, 0, 6), (PART, 0, 3),
    (LANE, 0, 7), (LANE, 7, 6), (LANE, 8, 6), (PART, 1, 4), (LANE, 8, 7), (PART, 2, 4), (LANE, 4, 7),
    (SMALL, 4, 0), (LANE, 5, 5), (LANE, 4, 8), (LANE, 7, 7), (LANE, 6, 6), (PART, 0, 4), (LANE, 7, 8),
    (LANE, 5, 6), (LANE, 6, 7), (PART, 2, 5), (PART, 2, 6), (PART, 0, 5), (PART, 1, 5), (LANE, 5, 7),
    (PART, 0, 6), (PART, 1, 6), (LANE, 5, 8), (SMALL, 5, 0),
)


def fused(
    x_in, cot_in, groups, lengths, table_in, wqkv_in, qb_in, vb_in, wo_in, ob_in, g1_in, b1_in,
    wup_in, ub_in, wdn_in, db_in, g2_in, b2_in,
    lo_out, ig_out, full, qfull, vec_out,
    xb, lowb, cotb, table, meta, meta_far, wqkv, wq, wo, wup, wdn, qb, vb, ob, g1, b1, ub, db, g2, b2,
    qt, q, k, vaug, vback, att, inv, sums, abuf, gelu_grad, act, pre_grad, res, lob, igb, n1, n2, s2b, attn_grad,
    normed_low, ffn_grad, second, normed_grad, dob, dor, probs, dkt, dvt, dqkv, dxb, dxr0, dxr1, dxo,
    vecb, vecr,
    own, r0, r1, r3, qown, qr1, qr3,
    ssem, rsem, lsem,
):
    b_index, s_index = lax.axis_index("batch"), lax.axis_index("seq")
    x, z = s_index % 2, s_index // 2
    y, c = b_index // 2, b_index % 2
    me = 2 * x + c

    def dev(x, y, z, c):
        return (2 * y + c, 2 * z + x)

    core_dev = dev(x, y, z, 1 - c)
    x_dev = dev(1 - x, y, z, c)
    y_dev = dev(x, 1 - y, z, c)
    z_devs = [dev(x, y, (z + d) % 4, c) for d in (1, 2, 3)]
    z_near = z + 1 - 2 * (z % 2)
    near_dev, mirror_dev = dev(x, y, z_near, c), dev(x, y, 3 - z, c)
    crossing = c != z // 2

    pending = []

    def send(src, dst, s_number, r_number, device, when=None):
        copy = pltpu.make_async_remote_copy(
            src_ref=src, dst_ref=dst, send_sem=ssem.at[s_number], recv_sem=rsem.at[r_number],
            device_id=device, device_id_type=MESH,
        )
        if when is None:
            copy.start()
        else:
            pl.when(when)(copy.start)
        pending.append((copy, when))

    def arrived(dst, number):
        pltpu.make_async_remote_copy(
            src_ref=dst, dst_ref=dst, send_sem=ssem.at[number], recv_sem=rsem.at[number],
            device_id=core_dev, device_id_type=MESH,
        ).wait_recv()

    local_copies = []

    def fetch(src, dst):
        copy = pltpu.make_async_copy(src, dst, lsem.at[len(local_copies)])
        copy.start()
        local_copies.append(copy)
        return copy

    def land(copies):
        for copy in copies:
            copy.wait()
            local_copies[local_copies.index(copy)] = None

    wait_qkv = [fetch(table_in, table), fetch(qb_in, qb), fetch(vb_in, vb)]
    for t in range(3):
        columns = pl.ds(pl.multiple_of(512 * t + 128 * me, 128), 128)
        wait_qkv.append(fetch(wqkv_in.at[:, columns], wq.at[:, pl.ds(128 * t, 128)]))
    wait_qkv.append(fetch(wqkv_in, wqkv))
    wait_ffn = [
        fetch(a, b)
        for a, b in ((wo_in, wo), (ob_in, ob), (g1_in, g1), (b1_in, b1), (wup_in, wup), (ub_in, ub),
                     (wdn_in, wdn), (db_in, db), (g2_in, g2), (b2_in, b2))
    ]

    barrier = pltpu.get_barrier_semaphore()
    near = [core_dev, x_dev, y_dev] + z_devs
    for device in near:
        pl.semaphore_signal(barrier, inc=1, device_id=device, device_id_type=MESH)

    @pl.when(crossing)
    def _():
        for i in range(2):
            pl.semaphore_signal(
                barrier, inc=1, device_id=dev(x, y, 2 * c + i, z // 2), device_id_type=MESH
            )
        pl.semaphore_wait(barrier, len(near) + 2)

    @pl.when(jnp.logical_not(crossing))
    def _():
        pl.semaphore_wait(barrier, len(near))

    def half(ref, h):
        return ref.at[pl.ds(64 * h, 64)]

    def peer(i):
        return dev(x, y, 2 * c + i, z // 2)

    first = jnp.where(crossing, 1 - c, z % 2)
    in_turn = [(i, h) for i in (first, 1 - first) for h in (0, 1)]
    for i, h in in_turn:
        send(half(x_in.at[i], h), half(xb.at[x, z], h), NUM["x"] + 2 * i + h, NUM["x"] + 2 * (z % 2) + h,
             peer(i), when=2 * c + i != z)
    def send_cot():
        for i in (first, 1 - first):
            send(cot_in.at[i], cotb.at[x, z % 2], NUM["cot"] + i, NUM["cot"] + z % 2, peer(i), when=2 * c + i != z)
    self_x = pltpu.make_async_copy(x_in.at[z % 2], xb.at[x, z], lsem.at[LOCAL - 1])
    self_cot = pltpu.make_async_copy(cot_in.at[z % 2], cotb.at[x, z % 2], lsem.at[LOCAL - 2])

    @pl.when(jnp.logical_not(crossing))
    def _():
        self_x.start()
        self_cot.start()
        self_x.wait()


    land(wait_qkv)
    slot = z % 2
    group, length = groups[slot], lengths[slot]
    meta[0:1, :] = table[pl.ds(group, 1), :]
    meta[1:2, :] = jnp.full((1, 512), length.astype(f32))
    meta[2:3, :] = jnp.full((1, 512), group.astype(f32))
    meta[3:8, :] = jnp.zeros((5, 512), f32)
    send(meta, meta_far, NUM["meta"], NUM["meta"], core_dev)

    for i, h in in_turn:
        block = half(xb.at[x, 2 * c + i], h)

        @pl.when(2 * c + i != z)
        def _():
            arrived(block, NUM["x"] + 2 * i + h)

        number = NUM["xn"] + 2 * i + h
        send(block, block, number, number, x_dev)
        number = NUM["core_own"] + 2 * i + h
        send(block, block, number, number, core_dev)

    send_cot()
    arrived(meta_far, NUM["meta"])
    facts = jnp.where(crossing, meta_far[...], meta[...])
    pair_row, length_row, group_row = facts[0:1, :], facts[1:2, :], facts[2:3, :]
    row_length = length_row[:, 0:1]

    lane = lax.broadcasted_iota(jnp.int32, (1, 128), 1)
    head_lanes = [lane < 64, lane >= 64]
    row = lax.broadcasted_iota(jnp.int32, (256, 1), 0)

    def rows_of(xx, cc):
        return pl.ds(pl.multiple_of(512 * xx + 256 * cc, 256), 256)

    def usable_rows(xx, cc):
        place = 128 * (4 * cc + xx) + row + jnp.where(row >= 128, 128, 0)
        return place.astype(f32) < row_length

    mine = pl.ds(pl.multiple_of(128 * me, 128), 128)
    all_lanes = lax.broadcasted_iota(jnp.int32, (1, 256), 1)
    first_head = all_lanes % 128 < 64

    def project(xx, cc, ours):
        low = (xb[xx, pl.ds(2 * cc, 2)].reshape(256, 512).astype(f32) + pair_row).astype(bf16)
        rows = rows_of(xx, cc)
        lowb[rows, :] = low
        usable = usable_rows(xx, cc)
        eighth = jnp.asarray(0.125, bf16)
        if ours:
            there = pl.ds(pl.multiple_of(256 * xx, 256), 256)
            qt[there, :] = (mm(low, wqkv[:, 0:512]) + qb[...]).astype(bf16) * eighth
            q[rows, :] = qt[there, mine]
        else:
            q[rows, :] = (mm(low, wq[:, 0:128]) + qb[:, mine]).astype(bf16) * eighth
        k[rows, :] = jnp.where(usable, mm(low, wqkv[:, 512:1024]), 0.0).astype(bf16)
        value = jnp.where(usable, mm(low, wqkv[:, 1024:1536]) + vb[...], 0.0).astype(bf16)
        one = jnp.broadcast_to(jnp.where(usable, 1.0, 0.0), (256, 128))
        for pair in range(4):
            vaug[pair, rows, 0:128] = value[:, 128 * pair : 128 * pair + 128]
            vaug[pair, rows, 128:256] = one.astype(bf16)
        own_value = vaug[me, rows, 0:128].astype(f32)
        for h in range(2):
            edge = 64 * (1 - h)
            extra = jnp.where((lane == edge) | (lane == edge + 1), one, 0.0)
            vback[h, rows, :] = jnp.where(head_lanes[h], own_value, extra).astype(bf16)

    def attend(q_rows, pair, h, keys, probs_rows):
        columns = pl.ds(pl.multiple_of(128 * pair, 128), 128)
        prob = jnp.exp(mm_nt(jnp.where(head_lanes[h], q_rows, 0), k[keys, columns])).astype(bf16)
        if probs_rows is not None:
            probs[h, probs_rows, keys] = prob
        return mm(prob, vaug[pair, keys, :])

    def attended_of(sums, rows):
        both = jnp.where(first_head, sums[0], sums[1])
        inverse = 1.0 / both[:, 128:256]
        attended = both[:, 0:128] * inverse
        if rows is not None:
            att[rows, :] = attended
            inv[rows, :] = inverse
        return attended.astype(bf16)

    every = pl.ds(0, 1024)
    early = pl.ds(pl.multiple_of(512 * x, 512), 512)
    late = pl.ds(pl.multiple_of(512 * (1 - x), 512), 512)
    pairs = [(me + d) % 4 for d in range(4)]
    own_rows, far_rows = rows_of(x, c), rows_of(1 - x, c)
    own_half = pl.ds(pl.multiple_of(256 * x, 256), 256)
    far_half = pl.ds(pl.multiple_of(256 * (1 - x), 256), 256)

    def pair_columns(pair):
        return pl.ds(pl.multiple_of(128 * pair, 128), 128)

    def early_part(d, h):
        sums[d, h] = attend(qt[own_half, pair_columns(pairs[d])], pairs[d], h, early, own_rows if d == 0 else None)

    project(x, c, True)
    for i, h in in_turn:
        arrived(half(xb.at[x, 2 * (1 - c) + i], h), NUM["core_own"] + 2 * i + h)
    project(x, 1 - c, False)
    for at, (i, h) in enumerate(in_turn):
        early_part(at, 0)
        early_part(at, 1)
        block = half(xb.at[1 - x, 2 * c + i], h)
        arrived(block, NUM["xn"] + 2 * i + h)
        number = NUM["core_far"] + 2 * i + h
        send(block, block, number, number, core_dev)
    project(1 - x, c, True)
    for i, h in in_turn:
        arrived(half(xb.at[1 - x, 2 * (1 - c) + i], h), NUM["core_far"] + 2 * i + h)
    project(1 - x, 1 - c, False)
    def forward_cot(i):
        @pl.when(2 * c + i != z)
        def _():
            arrived(cotb.at[x, i], NUM["cot"] + i)

        @pl.when(2 * c + i == z)
        def _():
            self_cot.wait()

        send(cotb.at[x, i], cotb.at[x, i], NUM["cot_x"] + i, NUM["cot_x"] + i, x_dev)


    for d in range(4):
        sums_all = [sums[d, h] + attend(qt[own_half, pair_columns(pairs[d])], pairs[d], h, late,
                                        own_rows if d == 0 else None) for h in range(2)]
        abuf[own_half, pair_columns(pairs[d])] = attended_of(sums_all, own_rows if d == 0 else None)
    forward_cot(first)
    for d in range(4):
        sums_all = [attend(qt[far_half, pair_columns(pairs[d])], pairs[d], h, every,
                           far_rows if d == 0 else None) for h in range(2)]
        abuf[far_half, pair_columns(pairs[d])] = attended_of(sums_all, far_rows if d == 0 else None)
        if d == 1:
            forward_cot(1 - first)

    def other_probs(xx):
        rows = rows_of(xx, 1 - c)
        attended_of([attend(q[rows, :], me, h, every, rows) for h in range(2)], rows)

    def norm(hidden):
        centred = hidden - jnp.mean(hidden, axis=-1, keepdims=True)
        scale = lax.rsqrt(jnp.mean(centred * centred, axis=-1, keepdims=True) + eps_norm)
        return centred * scale, scale

    def norm_back(grad, normalized, scale, gain):
        e = grad * gain
        return scale * (
            e - jnp.mean(e, axis=-1, keepdims=True)
            - normalized * jnp.mean(e * normalized, axis=-1, keepdims=True)
        )

    def column_sum(values):
        return jnp.sum(values, axis=0, keepdims=True)

    once = jnp.where(x == 0, 1.0, 0.0)
    land(wait_ffn)
    s1_parts = []
    for xx in (0, 1):
        there = pl.ds(256 * xx, 256)

        start_x = xb[xx, pl.ds(2 * c, 2)].reshape(256, 512).astype(f32) + pair_row
        normalized, s1 = norm(start_x + (mm(abuf[there, :], wo[...]) + ob[...]))
        s1_parts.append(s1)
        n1[there, :] = normalized
        normed = normalized * g1[...] + b1[...]
        low = normed.astype(bf16)
        normed_low[there, :] = low
        ffn = jnp.zeros((256, 512), f32)
        for j in range(4):
            cols = pl.ds(512 * j, 512)
            pre = mm(low, wup[:, cols]) + ub[:, cols]
            cdf = 0.5 * (1.0 + lax.erf(pre * 0.7071067811865476))
            gelu_grad[there, cols] = cdf + pre * (jnp.exp(-0.5 * pre * pre) * 0.3989422804014327)
            act_low = (pre * cdf).astype(bf16)
            act[there, cols] = act_low
            ffn = ffn + mm(act_low, wdn[cols, :])
        normalized, s2 = norm((ffn + db[...]) + normed + start_x)
        n2[there, :] = normalized
        s2b[there, :] = jnp.broadcast_to(s2, (256, 128))
    lob[...] = (n2[own_half, :] * g2[...] + b2[...]).astype(bf16).reshape(2, 128, 512)

    def give_back(block, out, name):
        for i in (0, 1):
            send(block.at[i], out.at[z % 2], NUM[name] + i, NUM[name] + z % 2, peer(i), when=2 * c + i != z)

        @pl.when(jnp.logical_not(crossing))
        def _():
            out[z % 2] = block[z % 2]

    give_back(lob, lo_out, "lo")
    for turn, (xx, there) in enumerate(((x, own_half), (1 - x, far_half))):
        if turn == 1:
            for i in (0, 1):
                arrived(cotb.at[1 - x, i], NUM["cot_x"] + i)
        g = cotb[xx].reshape(256, 512).astype(f32)
        normalized = n2[there, :]
        gain_part, bias_part = column_sum(g * normalized), column_sum(g)
        grad = norm_back(g, normalized, s2b[there, 0:1], g2[...])
        second[there, :] = grad
        low = grad.astype(bf16)
        ffn_grad[there, :] = low
        down_part = column_sum(low.astype(f32))
        for at, part in ((14, gain_part), (15, bias_part), (13, down_part)):
            vecb[at : at + 1, :] = part * once if turn == 0 else vecb[at : at + 1, :] + part * once

    def number(n, step):
        return NUM["lane"] + 12 * n + step

    def add_up(target, parts, result=None):
        value = target[...].astype(f32)
        for part in parts:
            value = value + part[...].astype(f32)
        (target if result is None else result)[...] = value.astype(bf16)

    def travel(mine, r1, r3, whole, number_of, scatter, order):
        stages = []

        def scatter_stages(axis, last):
            def part(zz):
                return mine.at[y, zz] if last else mine.at[:, zz]

            def slot(d):
                return r3.at[d, 0] if last else r3.at[d]

            result = whole.at[x, c, y, z] if last else None
            if axis == "y":
                box = r1.at[0] if last else r1

                def start():
                    send(mine.at[1 - y, z] if last else mine.at[1 - y], box, number_of(1), number_of(1), y_dev)

                def finish():
                    arrived(box, number_of(1))
                    add_up(mine.at[y, z] if last else mine.at[y], [box], result)

                stages.append((start, finish))
            elif axis == "z":
                def start():
                    for d in (1, 2, 3):
                        send(part((z + d) % 4), slot(3 - d), number_of(1 + d), number_of(5 - d), z_devs[d - 1])

                def finish():
                    for d in (1, 2, 3):
                        arrived(slot(d - 1), number_of(1 + d))
                    add_up(part(z), [slot(d) for d in range(3)], result)

                stages.append((start, finish))
            else:
                def start():
                    send(part(3 - z_near), slot(0), number_of(2), number_of(2), near_dev)

                def finish():
                    arrived(slot(0), number_of(2))
                    add_up(part(3 - z), [slot(0)])

                def start_two():
                    send(part(3 - z), slot(1), number_of(3), number_of(3), mirror_dev)
                    send(part(z_near), slot(2), number_of(4), number_of(4), near_dev)

                def finish_two():
                    arrived(slot(1), number_of(3))
                    arrived(slot(2), number_of(4))
                    add_up(part(z), [slot(1), slot(2)], result)

                stages.append((start, finish))
                stages.append((start_two, finish_two))

        def region(done, **other):
            place = dict(x=x, y=y, z=z) | other
            at = {axis: slice(None) if axis in done else place[axis] for axis in "xyz"}
            return whole.at[at["x"], c, at["y"], at["z"]]

        def gather_stages(axis, done):
            part = region(done)
            if axis == "z":
                def start():
                    for d in (1, 2, 3):
                        send(part, part, number_of(4 + d), number_of(8 - d), z_devs[d - 1])

                def finish():
                    for d in (1, 2, 3):
                        arrived(region(done, z=(z + d) % 4), number_of(4 + d))

                stages.append((start, finish))
            elif axis == "w":
                def start():
                    send(part, part, number_of(6), number_of(6), mirror_dev)
                    send(part, part, number_of(5), number_of(5), near_dev)

                def finish():
                    arrived(region(done, z=z_near), number_of(5))
                    arrived(region(done, z=3 - z), number_of(6))

                def start_two():
                    passed = region(done, z=3 - z)
                    send(passed, passed, number_of(7), number_of(7), near_dev)

                def finish_two():
                    arrived(region(done, z=3 - z_near), number_of(7))

                stages.append((start, finish))
                stages.append((start_two, finish_two))
            else:
                at, device, there = {"x": (9, x_dev, dict(x=1 - x)), "y": (8, y_dev, dict(y=1 - y))}[axis]

                def start():
                    send(part, part, number_of(at), number_of(at), device)

                def finish():
                    arrived(region(done, **there), number_of(at))

                stages.append((start, finish))

        scatter_stages(scatter[0], False)
        scatter_stages(scatter[1], True)
        for at, axis in enumerate(order):
            gather_stages(axis, order[:at].replace("w", "z"))

        def start():
            send(whole.at[:, c], whole.at[:, c], number_of(10), number_of(10), core_dev)

        def finish():
            arrived(whole.at[:, 1 - c], number_of(10))

        stages.append((start, finish))
        return stages

    lane_stages = [
        travel(own.at[n, c], r1.at[n], r3.at[n], full.at[n], functools.partial(number, n), SCATTER[n], GATHER[n])
        for n in range(LANES)
    ]

    def lane_step(n, step):
        if step == 0:
            arrived(r0.at[n], number(n, 0))
            add_up(own.at[n, c], [r0.at[n]])
        else:
            lane_stages[n][step - 1][1]()
        if step < len(lane_stages[n]):
            lane_stages[n][step][0]()

    own_columns = pl.ds(pl.multiple_of(256 * x, 256), 256)

    def lane_fill(n):
        if n < 4:
            value = mm_tn(act[:, pl.ds(pl.multiple_of(512 * n + 256 * x, 256), 256)], ffn_grad[...])
        elif n < 8:
            value = mm_tn(normed_low[:, own_columns], pre_grad[:, pl.ds(512 * (n - 4), 512)])
        else:
            value = mm_tn(abuf[:, own_columns], attn_grad[...])
        own[n] = value.astype(bf16).reshape(2, 2, 4, 16, 512)
        send(own.at[n, 1 - c], r0.at[n], number(n, 0), number(n, 0), core_dev)

    def ffn_back(j):
        cols = pl.ds(512 * j, 512)
        for xx in (0, 1):
            there = pl.ds(256 * xx, 256)
            grad = (mm_nt(ffn_grad[there, :], wdn[cols, :]) * gelu_grad[there, cols]).astype(bf16)
            pre_grad[there, cols] = grad
            part = column_sum(grad.astype(f32)) * once
            vecb[16 + j : 17 + j, :] = part if xx == 0 else vecb[16 + j : 17 + j, :] + part
            term = mm_nt(grad, wup[:, cols])
            normed_grad[there, :] = (second if j == 0 else normed_grad)[there, :] + term

    def first_back():
        for xx in (0, 1):
            there = pl.ds(256 * xx, 256)
            grad, normalized = normed_grad[there, :], n1[there, :]
            first_grad = norm_back(grad, normalized, s1_parts[xx], g1[...])
            low = first_grad.astype(bf16)
            attn_grad[there, :] = low
            for at, part in ((11, column_sum(grad * normalized)), (12, column_sum(grad)),
                             (10, column_sum(low.astype(f32)))):
                vecb[at : at + 1, :] = part * once if xx == 0 else vecb[at : at + 1, :] + part * once
            second[there, :] = second[there, :] + first_grad
        res[...] = second[own_half, :]
        low = attn_grad[...]

        def heads(cc):
            return pl.ds(pl.multiple_of(128 * (2 * x + cc), 128), 128)

        dob[...] = mm_nt(low, wo[heads(1 - c), :]).astype(bf16)
        send(dob, dor.at[c], NUM["do"], NUM["do"], core_dev)
        dor[c] = mm_nt(low, wo[heads(c), :]).astype(bf16)

    turns = ((0, c), (1, c), (0, 1 - c), (1, 1 - c))

    def attention_back(turn):
        xx, cc = turns[turn]
        if turn == 2:
            arrived(dor.at[cc], NUM["do"])
        rows = rows_of(xx, cc)
        d_out = dor[cc, 256 * xx : 256 * xx + 256, :].astype(f32)
        numer_grad = d_out * inv[rows, :]
        product = numer_grad.astype(bf16).astype(f32) * att[rows, :]
        q_rows = q[rows, :]
        dq_rows = jnp.zeros((256, 128), f32)
        for h in range(2):
            total = -jnp.sum(jnp.where(head_lanes[h], product, 0.0), axis=1, keepdims=True)
            high = total.astype(bf16).astype(f32)
            edge = 64 * (1 - h)
            rest = jnp.where(lane == edge, high, jnp.where(lane == edge + 1, total - high, 0.0))
            grad_low = jnp.where(head_lanes[h], numer_grad, rest).astype(bf16)
            prob = probs[h, rows, :]
            score_grad = (prob.astype(f32) * mm_nt(grad_low, vback[h])).astype(bf16)
            dq_rows = dq_rows + jnp.where(head_lanes[h], mm(score_grad, k[:, mine]), 0.0)
            part = slice(64 * h, 64 * h + 64)
            dk_part = mm(jnp.transpose(q_rows)[part, :], score_grad)
            dv_part = mm(jnp.transpose(grad_low)[part, :], prob)
            dkt[part, :] = dk_part if turn == 0 else dkt[part, :] + dk_part
            dvt[part, :] = dv_part if turn == 0 else dvt[part, :] + dv_part
        dqkv[rows, 0:128] = (dq_rows * 0.125).astype(bf16)

    def projection_grads():
        for xx in (0, 1):
            for cc in (0, 1):
                rows = pl.ds(512 * xx + 256 * cc, 256)
                dqkv[rows, 128:256] = jnp.transpose(dkt[:, rows]).astype(bf16)
                dqkv[rows, 256:384] = jnp.where(usable_rows(xx, cc), jnp.transpose(dvt[:, rows]), 0.0).astype(bf16)

    def qnumber(t, step):
        return NUM["qkv"] + 12 * t + step

    part_stages = [
        travel(qown.at[t], qr1.at[t], qr3.at[t], qfull.at[t], functools.partial(qnumber, t), QSCATTER[t], QGATHER[t])
        for t in range(3)
    ]

    def projection_weights(t):
        value = mm_tn(lowb[...], dqkv[:, 128 * t : 128 * t + 128])
        qown[t] = value.astype(bf16).reshape(2, 4, 64, 128)
        part_stages[t][0][0]()

    def projection_step(t, step):
        part_stages[t][step][1]()
        if step + 1 < len(part_stages[t]):
            part_stages[t][step + 1][0]()

    def input_back(step):
        xx, cc = ((1 - x, 1 - c), (x, 1 - c), (1 - x, c), (x, c))[step]
        block = mm_nt(dqkv[rows_of(xx, cc), :], wq[...])
        vecb[20:21, :] = column_sum(block) if step == 0 else vecb[20:21, :] + column_sum(block)
        if step < 2:
            dxb[step] = block.astype(bf16)
            send(dxb.at[step], dxr0.at[step], NUM["dx_core"] + step, NUM["dx_core"] + step, core_dev)
        elif step == 2:
            arrived(dxr0.at[0], NUM["dx_core"])
            dxb[2] = (block + dxr0[0].astype(f32)).astype(bf16)
            send(dxb.at[2], dxr1, NUM["dx_x"], NUM["dx_x"], x_dev)
        else:
            arrived(dxr0.at[1], NUM["dx_core"] + 1)
            dxo[...] = block + dxr0[1].astype(f32) + res[...]

    def input_out():
        arrived(dxr1, NUM["dx_x"])
        igb[...] = (dxo[...] + dxr1[...].astype(f32)).astype(bf16).reshape(2, 128, 512)
        give_back(igb, ig_out, "ig")

    def vectors(step):
        if step == 0:
            group_iota = lax.broadcasted_iota(jnp.int32, (8, 512), 0).astype(f32)
            column_total = vecb[20:21, :] + column_sum(res[...])
            vecb[0:8, :] = jnp.where(group_iota == group_row, column_total, 0.0)
            vecb[8:10, :] = jnp.zeros((2, 512), f32)
            vecb[8:9, mine] = column_sum(dqkv[:, 0:128].astype(f32))
            vecb[9:10, mine] = column_sum(dqkv[:, 256:384].astype(f32))
            vecb[20:24, :] = jnp.zeros((4, 512), f32)
            send(vecb, vecr.at[0], NUM["vec"], NUM["vec"], core_dev)
        else:
            level = step - 1
            arrived(vecr.at[level], NUM["vec"] + level)
            value = (vecb if level == 0 else vecr.at[4 + level])[...] + vecr[level]
            if level < 4:
                vecr[5 + level] = value
                send(vecr.at[5 + level], vecr.at[level + 1], NUM["vec"] + level + 1, NUM["vec"] + level + 1,
                     (x_dev, y_dev, near_dev, mirror_dev)[level])
            else:
                vec_out[...] = value

    tasks = {(NORM, 0, 0): first_back, (SPLIT, 0, 0): projection_grads, (RETURN, 0, 0): input_out}
    for kind, task, count in (
        (FILL, lane_fill, LANES), (FFN, ffn_back, 4), (ATTN, attention_back, 4), (PROBS, other_probs, 2), (WEIGHT, projection_weights, 3),
        (INPUT, input_back, 4), (SMALL, vectors, 6),
    ):
        for at in range(count):
            tasks[kind, at, 0] = functools.partial(task, at)
    for n in range(LANES):
        for step in range(len(lane_stages[n]) + 1):
            tasks[LANE, n, step] = functools.partial(lane_step, n, step)
    for t in range(3):
        for step in range(len(part_stages[t])):
            tasks[PART, t, step] = functools.partial(projection_step, t, step)
    for at, entry in enumerate(ORDER):
        tasks.pop(entry)()
    assert not tasks

    for name, out in (("lo", lo_out), ("ig", ig_out)):
        for i in (0, 1):
            @pl.when(2 * c + i != z)
            def _():
                arrived(out.at[i], NUM[name] + i)
    land([copy for copy in local_copies if copy is not None])
    for copy, when in pending:
        if when is None:
            copy.wait_send()
        else:
            pl.when(when)(copy.wait_send)


VECTOR_ROWS = (8, 9, 10, 11, 12, 13, 14, 15)


def finish(lo, ig, full, qfull, vec, *refs):
    lo_out, ig_out, down_out, up_out, out_out, qkv_out, pair_out = refs[:7]
    vector_outs, up_bias_out = refs[7:15], refs[15]
    lo_wide, ig_wide, full_wide, qkv_wide, rows, up_bias, sems = *refs[16:20], refs[20:28], refs[28], refs[29]
    writes = []

    def write(src, dst):
        made = pltpu.make_async_copy(src, dst, sems.at[len(writes)])
        made.start()
        writes.append(made)

    for n in range(LANES):
        for half in range(2):
            at = pl.ds(256 * half, 256)
            full_wide[n, at, :] = full[n, half].reshape(256, 512).astype(f32)
            if n < 4:
                write(full_wide.at[n, at], down_out.at[pl.ds(512 * n + 256 * half, 256)])
            elif n < 8:
                write(full_wide.at[n, at], up_out.at[at, pl.ds(512 * (n - 4), 512)])
            else:
                write(full_wide.at[n, at], out_out.at[at])
    for t in range(3):
        for h in range(4):
            columns = pl.ds(512 * t + 128 * h, 128)
            qkv_wide[:, columns] = qfull[t, h // 2, h % 2].reshape(512, 128).astype(f32)
        columns = pl.ds(512 * t, 512)
        write(qkv_wide.at[:, columns], qkv_out.at[:, columns])
    for block, wide, out in ((lo, lo_wide, lo_out), (ig, ig_wide, ig_out)):
        wide[...] = block[...].astype(f32)
        write(wide, out)
    write(vec.at[pl.ds(0, 8)], pair_out)
    for at, row, out in zip(VECTOR_ROWS, rows, vector_outs):
        row[...] = vec[at : at + 1, :]
        write(row, out)
    for j in range(4):
        up_bias[:, 512 * j : 512 * j + 512] = vec[16 + j : 17 + j, :]
    write(up_bias, up_bias_out)
    for made in writes:
        made.wait()


def pair_plan(mesh):
    return dict(mesh.shape) == {"batch": 4, "seq": 8}


def fused_local(
    block_input, cotangent, groups, lengths, pair_table, qkv_weight, q_bias, v_bias, out_weight,
    out_bias, norm1_gain, norm1_bias, up_weight, up_bias, down_weight, down_bias, norm2_gain, norm2_bias,
):
    any_spec, smem = pl.BlockSpec(memory_space=pl.ANY), pl.BlockSpec(memory_space=pltpu.SMEM)

    def row(vector):
        return vector[None, :]

    operands = (
        block_input, cotangent, groups, lengths, pair_table, qkv_weight, row(q_bias), row(v_bias),
        out_weight, row(out_bias), row(norm1_gain), row(norm1_bias), up_weight, row(up_bias),
        down_weight, row(down_bias), row(norm2_gain), row(norm2_bias),
    )
    in_specs = [smem if i in (2, 3) else any_spec for i in range(len(operands))]
    vmem = pl.BlockSpec(memory_space=pltpu.VMEM)
    out_shape = [
        pltpu.VMEM(shape, dtype)
        for shape, dtype in (
            ((2, 128, 512), bf16), ((2, 128, 512), bf16), ((LANES, 2, 2, 2, 4, 16, 512), bf16),
            ((3, 2, 2, 2, 4, 64, 128), bf16), ((24, 512), f32),
        )
    ]
    scratch = [
        pltpu.VMEM(shape, dtype)
        for shape, dtype in (
            ((2, 4, 128, 512), bf16), ((1024, 512), bf16), ((2, 2, 128, 512), bf16),
            ((8, 512), f32), ((8, 512), f32), ((8, 512), f32),
            ((512, 1536), bf16), ((512, 384), bf16), ((512, 512), bf16), ((512, 2048), bf16), ((2048, 512), bf16),
            ((1, 512), f32), ((1, 512), f32), ((1, 512), f32), ((1, 512), f32), ((1, 512), f32),
            ((1, 2048), f32), ((1, 512), f32), ((1, 512), f32), ((1, 512), f32),
            ((512, 512), bf16), ((1024, 128), bf16), ((1024, 512), bf16),
            ((4, 1024, 256), bf16), ((2, 1024, 128), bf16),
            ((1024, 128), f32), ((1024, 128), f32),
            ((4, 2, 256, 256), f32), ((512, 512), bf16),
            ((512, 2048), f32), ((512, 2048), bf16), ((512, 2048), bf16),
            ((256, 512), f32), ((2, 128, 512), bf16), ((2, 128, 512), bf16),
            ((512, 512), f32), ((512, 512), f32), ((512, 128), f32), ((512, 512), bf16),
            ((512, 512), bf16), ((512, 512), bf16), ((512, 512), f32), ((512, 512), f32),
            ((512, 128), bf16), ((2, 512, 128), bf16), ((2, 1024, 1024), bf16),
            ((128, 1024), f32), ((128, 1024), f32), ((1024, 384), bf16),
            ((3, 256, 512), bf16), ((2, 256, 512), bf16), ((256, 512), bf16), ((256, 512), f32),
            ((24, 512), f32), ((9, 24, 512), f32),
            ((LANES, 2, 2, 4, 16, 512), bf16), ((LANES, 2, 4, 16, 512), bf16), ((LANES, 4, 16, 512), bf16),
            ((LANES, 3, 2, 16, 512), bf16),
            ((3, 2, 4, 64, 128), bf16), ((3, 4, 64, 128), bf16), ((3, 3, 2, 64, 128), bf16),
        )
    ] + [
        pltpu.SemaphoreType.DMA((NUM.count,)),
        pltpu.SemaphoreType.DMA((NUM.count,)),
        pltpu.SemaphoreType.DMA((LOCAL,)),
    ]
    results = pl.pallas_call(
        fused,
        out_shape=out_shape,
        in_specs=in_specs,
        out_specs=[vmem] * len(out_shape),
        scratch_shapes=scratch,
        compiler_params=pltpu.CompilerParams(
            collective_id=0, has_side_effects=True, vmem_limit_bytes=54 * 2**20
        ),
    )(*operands)
    shapes = [(2, 128, 512)] * 2 + [(2048, 512), (512, 2048), (512, 512), (512, 1536), (8, 512)]
    shapes += [(1, 512)] * 8 + [(1, 2048)]
    scratch_sizes = [(2, 128, 512)] * 2 + [(LANES, 512, 512), (512, 1536)] + [(1, 512)] * 8 + [(1, 2048)]
    results = pl.pallas_call(
        finish,
        out_shape=[jax.ShapeDtypeStruct(shape, f32) for shape in shapes],
        in_specs=[vmem] * 5,
        out_specs=[any_spec] * len(shapes),
        scratch_shapes=[pltpu.VMEM(shape, f32) for shape in scratch_sizes] + [pltpu.SemaphoreType.DMA((40,))],
        compiler_params=pltpu.CompilerParams(vmem_limit_bytes=40 * 2**20),
    )(*results)
    layer_out, input_grad, down_grad, up_grad, out_grad, qkv_grad, pair_grad = results[:7]
    q_grad, v_grad, ob_grad, g1_grad, b1_grad, db_grad, g2_grad, b2_grad = [r.reshape(512) for r in results[7:15]]
    return (
        layer_out, input_grad, pair_grad, qkv_grad, q_grad, v_grad,
        out_grad, ob_grad, g1_grad, b1_grad, up_grad, results[15].reshape(2048), down_grad, db_grad, g2_grad, b2_grad,
    )


def solution(mesh):
    in_specs = (
        P("batch", "seq", None),
        P("batch", "seq", None),
        P("batch"),
        P("batch"),
        P(),
        P(),
        P(),
        P(),
        P(),
        P(),
        P(),
        P(),
        P(),
        P(),
        P(),
        P(),
        P(),
        P(),
    )
    out_specs = (
        P("batch", "seq", None),
        P("batch", "seq", None),
        P(),
        P(),
        P(),
        P(),
        P(),
        P(),
        P(),
        P(),
        P(),
        P(),
        P(),
        P(),
        P(),
        P(),
    )
    return jax.shard_map(fused_local if pair_plan(mesh) else local, mesh=mesh, in_specs=in_specs, out_specs=out_specs, check_vma=False)
```

```python
import functools

import jax
import jax.numpy as jnp
from jax import lax
from jax.experimental import pallas as pl
from jax.experimental.pallas import tpu as pltpu
from jax.sharding import PartitionSpec as P

HEADS = 8


highest = lax.Precision.HIGHEST
eps_norm = 1e-05


def layer_norm(hidden, norm_gain, norm_shift):
    row_mean = jnp.mean(hidden, axis=-1, keepdims=True)
    centred = hidden - row_mean
    spread = jnp.mean(centred * centred, axis=-1, keepdims=True)
    return centred * lax.rsqrt(spread + eps_norm) * norm_gain + norm_shift


def exact_gelu(pre_act):
    return jax.nn.gelu(pre_act, approximate=False)


def block_size():
    return 512


def to_heads(flat_rows, head_count):
    return flat_rows.reshape(
        flat_rows.shape[0], flat_rows.shape[1], head_count, flat_rows.shape[2] // head_count
    )


def masked_exp(query_block, key_block, key_first, row_lengths, score_scale):
    scores = (
        jnp.einsum("rihd,rjhd->rhij", query_block, key_block, preferred_element_type=jnp.float32)
        * score_scale
    )
    places = key_first + jnp.arange(key_block.shape[1], dtype=jnp.int32)
    usable = places[None, :] < row_lengths[:, None]
    return jnp.where(usable[:, None, None, :], jnp.exp(scores), 0.0)


def forward_piece(
    running, key_piece, value_piece, query_heads, row_lengths, score_scale, head_count
):
    piece_len = key_piece.shape[1]
    block_len = block_size()
    key_all = to_heads(key_piece, head_count)
    value_all = to_heads(value_piece, head_count)

    def forward_one_block(block_index, partial_sums):
        numerator, denominator = partial_sums
        block_first = block_index * block_len
        key_block = lax.dynamic_slice_in_dim(key_all, block_first, block_len, 1)
        value_block = lax.dynamic_slice_in_dim(value_all, block_first, block_len, 1)
        exp_scores = masked_exp(query_heads, key_block, block_first, row_lengths, score_scale)
        denominator = denominator + jnp.sum(exp_scores, axis=-1)
        numerator = numerator + jnp.einsum(
            "rhij,rjhd->rihd",
            exp_scores.astype(jnp.bfloat16),
            value_block,
            preferred_element_type=jnp.float32,
        )
        return (numerator, denominator)

    return lax.fori_loop(0, piece_len // block_len, forward_one_block, running)


def key_side(
    running,
    query_piece,
    grad_piece,
    total_piece,
    key_heads,
    value_heads,
    key_first,
    row_lengths,
    score_scale,
    head_count,
):
    piece_len = query_piece.shape[1]
    block_len = block_size()
    query_all = to_heads(query_piece.astype(jnp.bfloat16), head_count)
    grad_all = to_heads(grad_piece, head_count)
    value_wide = value_heads.astype(jnp.float32)

    def key_one_block(block_index, partial_grads):
        key_grad, value_grad = partial_grads
        block_first = block_index * block_len
        query_block = lax.dynamic_slice_in_dim(query_all, block_first, block_len, 1)
        grad_block = lax.dynamic_slice_in_dim(grad_all, block_first, block_len, 1)
        total_block = lax.dynamic_slice_in_dim(total_piece, block_first, block_len, 1)
        exp_scores = masked_exp(query_block, key_heads, key_first, row_lengths, score_scale)
        prob_grad = jnp.einsum(
            "rihd,rjhd->rhij",
            grad_block,
            value_wide,
            precision=highest,
            preferred_element_type=jnp.float32,
        )
        shift_grad = jnp.transpose(total_block, (0, 2, 1))[..., None]
        score_grad = (exp_scores * (prob_grad + shift_grad)).astype(jnp.bfloat16)
        key_grad = (
            key_grad
            + jnp.einsum(
                "rhij,rihd->rjhd", score_grad, query_block, preferred_element_type=jnp.float32
            )
            * score_scale
        )
        exp_low = exp_scores.astype(jnp.bfloat16).astype(jnp.float32)
        value_grad = value_grad + jnp.einsum(
            "rhij,rihd->rjhd",
            exp_low,
            grad_block,
            precision=highest,
            preferred_element_type=jnp.float32,
        )
        return (key_grad, value_grad)

    return lax.fori_loop(0, piece_len // block_len, key_one_block, running)


def query_side(
    running,
    key_piece,
    value_piece,
    query_heads,
    grad_heads,
    total_here,
    row_lengths,
    score_scale,
    head_count,
):
    piece_len = key_piece.shape[1]
    block_len = block_size()
    key_all = to_heads(key_piece, head_count)
    value_all = to_heads(value_piece, head_count)

    def query_one_block(block_index, query_grad):
        block_first = block_index * block_len
        key_block = lax.dynamic_slice_in_dim(key_all, block_first, block_len, 1)
        value_block = lax.dynamic_slice_in_dim(value_all, block_first, block_len, 1)
        exp_scores = masked_exp(query_heads, key_block, block_first, row_lengths, score_scale)
        prob_grad = jnp.einsum(
            "rihd,rjhd->rhij",
            grad_heads,
            value_block.astype(jnp.float32),
            precision=highest,
            preferred_element_type=jnp.float32,
        )
        score_grad = (exp_scores * (prob_grad + total_here[..., None])).astype(jnp.bfloat16)
        return (
            query_grad
            + jnp.einsum(
                "rhij,rjhd->rihd", score_grad, key_block, preferred_element_type=jnp.float32
            )
            * score_scale
        )

    return lax.fori_loop(0, piece_len // block_len, query_one_block, running)


def local(
    block_input,
    cotangent,
    groups,
    lengths,
    pair_table,
    qkv_weight,
    q_bias,
    v_bias,
    out_weight,
    out_bias,
    norm1_gain,
    norm1_bias,
    up_weight,
    up_bias,
    down_weight,
    down_bias,
    norm2_gain,
    norm2_bias,
):
    row_count, shard_len, model_width = block_input.shape
    head_count = HEADS
    head_size = model_width // head_count
    score_scale = head_size ** (-0.5)
    key_offset = lax.axis_index("seq") * shard_len
    pair_onehot = (
        groups[:, None] == jnp.arange(pair_table.shape[0], dtype=jnp.int32)[None, :]
    ).astype(jnp.float32)
    lifted = jnp.dot(pair_onehot, pair_table, precision=highest)
    start_x = block_input.astype(jnp.float32) + lifted[:, None, :]
    lowered = start_x.astype(jnp.bfloat16)
    projected = jnp.einsum("rtd,de->rte", lowered, qkv_weight, preferred_element_type=jnp.float32)
    query_rows = (projected[:, :, :model_width] + q_bias).astype(jnp.bfloat16)
    key_rows = projected[:, :, model_width : 2 * model_width].astype(jnp.bfloat16)
    value_rows = (projected[:, :, 2 * model_width :] + v_bias).astype(jnp.bfloat16)
    query_heads = to_heads(query_rows, head_count)
    key_heads = to_heads(key_rows, head_count)
    value_heads = to_heads(value_rows, head_count)
    zero_heads = jnp.zeros((row_count, shard_len, head_count, head_size), jnp.float32)
    zero_totals = jnp.zeros((row_count, head_count, shard_len), jnp.float32)
    incoming = (
        lax.all_gather(key_rows, "seq", axis=1, tiled=True),
        lax.all_gather(value_rows, "seq", axis=1, tiled=True),
    )
    numerator, denominator = forward_piece(
        (zero_heads, zero_totals),
        incoming[0],
        incoming[1],
        query_heads,
        lengths,
        score_scale,
        head_count,
    )
    inverse = 1.0 / jnp.transpose(denominator, (0, 2, 1))[..., None]
    attended = numerator * inverse
    attended_low = attended.reshape(row_count, shard_len, model_width).astype(jnp.bfloat16)
    attn_out = (
        jnp.einsum("rtd,de->rte", attended_low, out_weight, preferred_element_type=jnp.float32)
        + out_bias
    )
    normed, norm1_back = jax.vjp(layer_norm, start_x + attn_out, norm1_gain, norm1_bias)
    normed_low = normed.astype(jnp.bfloat16)
    pre_act = (
        jnp.einsum("rtd,df->rtf", normed_low, up_weight, preferred_element_type=jnp.float32)
        + up_bias
    )
    activated, gelu_back = jax.vjp(exact_gelu, pre_act)
    activated_low = activated.astype(jnp.bfloat16)
    ffn_out = (
        jnp.einsum("rtf,fd->rtd", activated_low, down_weight, preferred_element_type=jnp.float32)
        + down_bias
    )
    layer_out, norm2_back = jax.vjp(layer_norm, ffn_out + normed + start_x, norm2_gain, norm2_bias)
    second_grad, norm2_gain_grad, norm2_bias_grad = norm2_back(cotangent.astype(jnp.float32))
    ffn_grad = second_grad.astype(jnp.bfloat16)
    down_bias_grad = jnp.sum(ffn_grad.astype(jnp.float32), axis=(0, 1))
    down_weight_grad = jnp.einsum(
        "rtf,rtd->fd", activated_low, ffn_grad, preferred_element_type=jnp.float32
    )
    act_grad = jnp.einsum("rtd,fd->rtf", ffn_grad, down_weight, preferred_element_type=jnp.float32)
    pre_grad = gelu_back(act_grad)[0].astype(jnp.bfloat16)
    up_bias_grad = jnp.sum(pre_grad.astype(jnp.float32), axis=(0, 1))
    up_weight_grad = jnp.einsum(
        "rtd,rtf->df", normed_low, pre_grad, preferred_element_type=jnp.float32
    )
    normed_grad = second_grad + jnp.einsum(
        "rtf,df->rtd", pre_grad, up_weight, preferred_element_type=jnp.float32
    )
    first_grad, norm1_gain_grad, norm1_bias_grad = norm1_back(normed_grad)
    attn_grad = first_grad.astype(jnp.bfloat16)
    out_bias_grad = jnp.sum(attn_grad.astype(jnp.float32), axis=(0, 1))
    out_weight_grad = jnp.einsum(
        "rtd,rte->de", attended_low, attn_grad, preferred_element_type=jnp.float32
    )
    attended_grad = to_heads(
        jnp.einsum("rte,de->rtd", attn_grad, out_weight, preferred_element_type=jnp.float32),
        head_count,
    )
    numer_grad = attended_grad * inverse
    total_grad = -jnp.sum(attended_grad * attended, axis=-1) * inverse[..., 0]
    grad_rows = numer_grad.reshape(row_count, shard_len, model_width)
    total_here = jnp.transpose(total_grad, (0, 2, 1))
    incoming = (
        lax.all_gather(query_rows.astype(jnp.float32), "seq", axis=1, tiled=True),
        lax.all_gather(grad_rows, "seq", axis=1, tiled=True),
        lax.all_gather(total_grad, "seq", axis=1, tiled=True),
    )
    key_grad, value_grad = key_side(
        (zero_heads, zero_heads),
        incoming[0],
        incoming[1],
        incoming[2],
        key_heads,
        value_heads,
        key_offset,
        lengths,
        score_scale,
        head_count,
    )
    incoming = (
        lax.all_gather(key_rows, "seq", axis=1, tiled=True),
        lax.all_gather(value_rows, "seq", axis=1, tiled=True),
    )
    query_grad = query_side(
        zero_heads,
        incoming[0],
        incoming[1],
        query_heads,
        numer_grad,
        total_here,
        lengths,
        score_scale,
        head_count,
    )
    flat_shape = (row_count, shard_len, model_width)
    query_low = query_grad.reshape(flat_shape).astype(jnp.bfloat16)
    key_low = key_grad.reshape(flat_shape).astype(jnp.bfloat16)
    value_low = value_grad.reshape(flat_shape).astype(jnp.bfloat16)
    qkv_grad = jnp.concatenate([query_low, key_low, value_low], axis=-1)
    qkv_weight_grad = jnp.einsum(
        "rtd,rte->de", lowered, qkv_grad, preferred_element_type=jnp.float32
    )
    q_bias_grad = jnp.sum(query_low.astype(jnp.float32), axis=(0, 1))
    v_bias_grad = jnp.sum(value_low.astype(jnp.float32), axis=(0, 1))
    input_grad = (
        jnp.einsum("rte,de->rtd", qkv_grad, qkv_weight, preferred_element_type=jnp.float32)
        + first_grad
        + second_grad
    )
    pair_table_grad = jnp.dot(
        jnp.transpose(pair_onehot), jnp.sum(input_grad, axis=1), precision=highest
    )
    summed = lax.psum(
        (
            pair_table_grad,
            qkv_weight_grad,
            q_bias_grad,
            v_bias_grad,
            out_weight_grad,
            out_bias_grad,
            norm1_gain_grad,
            norm1_bias_grad,
            up_weight_grad,
            up_bias_grad,
            down_weight_grad,
            down_bias_grad,
            norm2_gain_grad,
            norm2_bias_grad,
        ),
        ("batch", "seq"),
    )
    return (
        layer_out,
        input_grad,
        summed[0],
        summed[1],
        summed[2],
        summed[3],
        summed[4],
        summed[5],
        summed[6],
        summed[7],
        summed[8],
        summed[9],
        summed[10],
        summed[11],
        summed[12],
        summed[13],
    )


MESH = pl.DeviceIdType.MESH
f32, bf16 = jnp.float32, jnp.bfloat16
LANES = 9
PIECES, PIECE = 4, 32


def mm(a, b):
    return jnp.dot(a, b, preferred_element_type=f32)


def mm_nt(a, b):
    return lax.dot_general(a, b, (((1,), (1,)), ((), ())), preferred_element_type=f32)


def mm_tn(a, b):
    return lax.dot_general(a, b, (((0,), (0,)), ((), ())), preferred_element_type=f32)


class Numbers:
    def __init__(self):
        self.count = 0
        self.first = {}

    def take(self, name, size=1):
        self.first[name] = self.count
        self.count += size

    def __getitem__(self, name):
        return self.first[name]


def semaphore_numbers():
    numbers = Numbers()
    for name, size in (
        ("x", 2 * PIECES), ("cot", 2), ("lo", 2), ("ig", 2), ("cot_x", 2),
        ("xn", 2 * PIECES), ("core_own", 2 * PIECES), ("core_far", 2 * PIECES), ("meta", 1),
        ("do", 1), ("dx_core", 2), ("dx_x", 1), ("vec", 6),
        ("lane", LANES * 12), ("qkv", 3 * 12),
    ):
        numbers.take(name, size)
    return numbers


NUM = semaphore_numbers()
LOCAL = 19

SCATTER = ('yz', 'yz', 'yz', 'yz', 'yw', 'yw', 'yw', 'yw', 'yw')
GATHER = ('wxy', 'wxy', 'wyx', 'wyx', 'wyx', 'zyx', 'zxy', 'zxy', 'zyx')
QSCATTER = ('yw', 'yw', 'yw')
QGATHER = ('zxy', 'zyx', 'wxy')
FILL, LANE, FFN, NORM, ATTN, SPLIT, WEIGHT, PART, INPUT, RETURN, SMALL, PROBS, SUMS = range(13)
ORDER = (
    (RETURN, 1, 0), (FILL, 0, 0), (FFN, 0, 0), (FILL, 3, 0), (FILL, 2, 0), (LANE, 0, 0), (FILL, 1, 0),
    (FFN, 1, 0), (LANE, 3, 0), (LANE, 2, 0), (FFN, 2, 0), (LANE, 1, 0), (FFN, 3, 0), (FILL, 5, 0),
    (FILL, 7, 0), (PROBS, 1, 0), (LANE, 0, 1), (NORM, 0, 0), (FILL, 6, 0), (LANE, 5, 0), (LANE, 3, 1),
    (ATTN, 0, 0), (FILL, 4, 0), (LANE, 2, 1), (ATTN, 1, 0), (LANE, 6, 0), (LANE, 4, 0), (LANE, 1, 1),
    (PROBS, 0, 0), (ATTN, 2, 0), (LANE, 5, 1), (LANE, 7, 0), (LANE, 0, 2), (LANE, 3, 2), (ATTN, 3, 0),
    (SPLIT, 0, 0), (INPUT, 0, 0), (LANE, 2, 2), (FILL, 8, 0), (WEIGHT, 0, 0), (LANE, 6, 1), (LANE, 5, 2),
    (INPUT, 1, 0), (SUMS, 0, 0), (INPUT, 2, 0), (LANE, 8, 0), (LANE, 1, 2), (SUMS, 1, 0), (LANE, 0, 3),
    (LANE, 4, 1), (WEIGHT, 2, 0), (LANE, 3, 3), (WEIGHT, 1, 0), (INPUT, 3, 0), (LANE, 6, 2), (LANE, 2, 3),
    (PART, 0, 0), (LANE, 5, 3), (LANE, 0, 4), (SMALL, 0, 0), (LANE, 1, 3), (LANE, 3, 4), (LANE, 7, 1),
    (SMALL, 1, 0), (PART, 2, 0), (LANE, 8, 1), (PART, 0, 1), (LANE, 4, 2), (LANE, 2, 4), (LANE, 1, 4),
    (LANE, 6, 3), (LANE, 5, 4), (PART, 2, 1), (LANE, 3, 5), (LANE, 0, 5), (LANE, 8, 2), (SMALL, 2, 0),
    (PART, 0, 2), (PART, 1, 0), (LANE, 6, 4), (LANE, 4, 3), (PART, 2, 2), (LANE, 7, 2), (LANE, 5, 5),
    (LANE, 1, 5), (LANE, 8, 3), (PART, 1, 1), (PART, 0, 3), (LANE, 6, 5), (PART, 2, 3), (LANE, 4, 4),
    (LANE, 2, 5), (LANE, 7, 3), (LANE, 8, 4), (PART, 1, 2), (LANE, 0, 6), (LANE, 4, 5), (PART, 2, 4),
    (PART, 0, 4), (SMALL, 3, 0), (LANE, 7, 4), (RETURN, 0, 0), (LANE, 8, 5), (LANE, 3, 6), (LANE, 4, 6),
    (SMALL, 4, 0), (PART, 1, 3), (LANE, 6, 6), (LANE, 7, 5), (LANE, 2, 6), (LANE, 5, 6), (PART, 0, 5),
    (PART, 1, 4), (PART, 0, 6), (PART, 2, 5), (LANE, 8, 6), (LANE, 7, 6), (LANE, 4, 7), (LANE, 7, 7),
    (LANE, 6, 7), (LANE, 4, 8), (LANE, 1, 6), (LANE, 8, 7), (PART, 2, 6), (SMALL, 5, 0), (LANE, 3, 7),
    (LANE, 0, 7), (PART, 1, 5), (LANE, 1, 7), (LANE, 2, 7), (LANE, 5, 7), (PART, 2, 7), (PART, 1, 6),
)


def fused(
    x_in, cot_in, groups, lengths, table_in, wqkv_in, qb_in, vb_in, wo_in, ob_in, g1_in, b1_in,
    wup_in, ub_in, wdn_in, db_in, g2_in, b2_in,
    lo_out, ig_out, full, qfull, vec_out,
    x_here, cot_here, xb, lowb, cotb, table, meta, meta_far, wqkv, wq, wo, wup, wdn, qb, vb, ob, g1, b1, ub, db, g2, b2,
    qt, q, k, vaug, vback, att, inv, sums, abuf, before, act, pre_grad, res, lob, igb, n1, n2, s1b, s2b, attn_grad,
    normed_low, ffn_grad, second, normed_grad, dob, dor, probs, dkt, dvt, dqkv, dxb, dxr0, dxr1, dxo,
    vecb, vecr,
    own, r0, r1, r3, qown, qr1, qr3,
    ssem, rsem, lsem,
):
    b_index, s_index = lax.axis_index("batch"), lax.axis_index("seq")
    x, z = s_index % 2, s_index // 2
    y, c = b_index // 2, b_index % 2
    me = 2 * x + c

    def dev(x, y, z, c):
        return (2 * y + c, 2 * z + x)

    core_dev = dev(x, y, z, 1 - c)
    x_dev = dev(1 - x, y, z, c)
    y_dev = dev(x, 1 - y, z, c)
    z_devs = [dev(x, y, (z + d) % 4, c) for d in (1, 2, 3)]
    z_near = z + 1 - 2 * (z % 2)
    near_dev, mirror_dev = dev(x, y, z_near, c), dev(x, y, 3 - z, c)
    crossing = c != z // 2

    pending = []

    def send(src, dst, s_number, r_number, device, when=None):
        copy = pltpu.make_async_remote_copy(
            src_ref=src, dst_ref=dst, send_sem=ssem.at[s_number], recv_sem=rsem.at[r_number],
            device_id=device, device_id_type=MESH,
        )
        if when is None:
            copy.start()
        else:
            pl.when(when)(copy.start)
        pending.append((copy, when))

    def arrived(dst, number):
        pltpu.make_async_remote_copy(
            src_ref=dst, dst_ref=dst, send_sem=ssem.at[number], recv_sem=rsem.at[number],
            device_id=core_dev, device_id_type=MESH,
        ).wait_recv()

    local_copies = []

    def fetch(src, dst):
        copy = pltpu.make_async_copy(src, dst, lsem.at[len(local_copies)])
        copy.start()
        local_copies.append(copy)
        return copy

    def land(copies):
        for copy in copies:
            copy.wait()
            local_copies[[entry is copy for entry in local_copies].index(True)] = None

    wait_table = fetch(table_in, table)
    wait_tokens = [fetch(x_in, x_here), fetch(cot_in, cot_here)]

    barrier = pltpu.get_barrier_semaphore()
    near = [core_dev, x_dev, y_dev] + z_devs
    for device in near:
        pl.semaphore_signal(barrier, inc=1, device_id=device, device_id_type=MESH)

    def greet(devices):
        for device in devices:
            pl.semaphore_signal(barrier, inc=1, device_id=device, device_id_type=MESH)
        pl.semaphore_wait(barrier, len(near) + len(devices))

    @pl.when(crossing)
    def _():
        greet([dev(xx, y, 2 * c + i, z // 2) for i in range(2) for xx in (x, 1 - x)])

    @pl.when(jnp.logical_not(crossing))
    def _():
        greet([dev(1 - x, y, z_near, c)])

    def half(ref, h):
        return ref.at[pl.ds(PIECE * h, PIECE)]

    def peer(i):
        return dev(x, y, 2 * c + i, z // 2)

    land(wait_tokens)
    first = jnp.where(crossing, 1 - c, z % 2)
    in_turn = [(i, h) for i in (first, 1 - first) for h in range(PIECES)]
    for i, h in in_turn:
        send(half(x_here.at[i], h), half(xb.at[x, z], h), NUM["x"] + PIECES * i + h, NUM["x"] + PIECES * (z % 2) + h,
             peer(i), when=2 * c + i != z)
    def send_cot():
        for i in (first, 1 - first):
            send(cot_here.at[i], cotb.at[x, z % 2], NUM["cot"] + i, NUM["cot"] + z % 2, peer(i), when=2 * c + i != z)
        for i in (first, 1 - first):
            send(cot_here.at[i], cotb.at[x, z % 2], NUM["cot_x"] + i, NUM["cot_x"] + z % 2,
                 dev(1 - x, y, 2 * c + i, z // 2))

    send_cot()
    @pl.when(jnp.logical_not(crossing))
    def _():
        xb[x, z] = x_here[z % 2]
        cotb[x, z % 2] = cot_here[z % 2]

    wait_qkv = [fetch(qb_in, qb), fetch(vb_in, vb)]
    for t in range(3):
        columns = pl.ds(pl.multiple_of(512 * t + 128 * me, 128), 128)
        wait_qkv.append(fetch(wqkv_in.at[:, columns], wq.at[:, pl.ds(128 * t, 128)]))
    wait_qkv.append(fetch(wqkv_in, wqkv))
    wait_ffn = [
        fetch(a, b)
        for a, b in ((wo_in, wo), (ob_in, ob), (g1_in, g1), (b1_in, b1), (wup_in, wup), (ub_in, ub),
                     (wdn_in, wdn), (db_in, db), (g2_in, g2), (b2_in, b2))
    ]

    land([wait_table])
    slot = z % 2
    group, length = groups[slot], lengths[slot]
    meta[0:1, :] = table[pl.ds(group, 1), :]
    meta[1:2, :] = jnp.full((1, 512), length.astype(f32))
    meta[2:3, :] = jnp.full((1, 512), group.astype(f32))
    meta[3:8, :] = jnp.zeros((5, 512), f32)
    send(meta, meta_far, NUM["meta"], NUM["meta"], core_dev)

    for i, h in in_turn:
        block = half(xb.at[x, 2 * c + i], h)

        @pl.when(2 * c + i != z)
        def _():
            arrived(block, NUM["x"] + PIECES * i + h)

        number = NUM["xn"] + PIECES * i + h
        send(block, block, number, number, x_dev)
        number = NUM["core_own"] + PIECES * i + h
        send(block, block, number, number, core_dev)

    land(wait_qkv)
    arrived(meta_far, NUM["meta"])
    facts = jnp.where(crossing, meta_far[...], meta[...])
    pair_row, length_row, group_row = facts[0:1, :], facts[1:2, :], facts[2:3, :]
    row_length = length_row[:, 0:1]

    lane = lax.broadcasted_iota(jnp.int32, (1, 128), 1)
    head_lanes = [lane < 64, lane >= 64]
    row = lax.broadcasted_iota(jnp.int32, (256, 1), 0)

    def rows_of(xx, cc):
        return pl.ds(pl.multiple_of(512 * xx + 256 * cc, 256), 256)

    def usable_rows(xx, cc):
        place = 128 * (4 * cc + xx) + row + jnp.where(row >= 128, 128, 0)
        return place.astype(f32) < row_length

    mine = pl.ds(pl.multiple_of(128 * me, 128), 128)
    all_lanes = lax.broadcasted_iota(jnp.int32, (1, 256), 1)
    first_head = all_lanes % 128 < 64

    def project(xx, cc, ours):
        low = (xb[xx, pl.ds(2 * cc, 2)].reshape(256, 512).astype(f32) + pair_row).astype(bf16)
        rows = rows_of(xx, cc)
        lowb[rows, :] = low
        usable = usable_rows(xx, cc)
        eighth = jnp.asarray(0.125, bf16)
        if ours:
            there = pl.ds(pl.multiple_of(256 * xx, 256), 256)
            qt[there, :] = (mm(low, wqkv[:, 0:512]) + qb[...]).astype(bf16) * eighth
            q[rows, :] = qt[there, mine]
        else:
            q[rows, :] = (mm(low, wq[:, 0:128]) + qb[:, mine]).astype(bf16) * eighth
        k[rows, :] = jnp.where(usable, mm(low, wqkv[:, 512:1024]), 0.0).astype(bf16)
        value = jnp.where(usable, mm(low, wqkv[:, 1024:1536]) + vb[...], 0.0).astype(bf16)
        one = jnp.broadcast_to(jnp.where(usable, 1.0, 0.0), (256, 128))
        for pair in range(4):
            vaug[pair, rows, 0:128] = value[:, 128 * pair : 128 * pair + 128]
            vaug[pair, rows, 128:256] = one.astype(bf16)
        own_value = vaug[me, rows, 0:128].astype(f32)
        for h in range(2):
            edge = 64 * (1 - h)
            extra = jnp.where((lane == edge) | (lane == edge + 1), one, 0.0)
            vback[h, rows, :] = jnp.where(head_lanes[h], own_value, extra).astype(bf16)

    def attend(q_rows, pair, h, keys, probs_rows):
        columns = pl.ds(pl.multiple_of(128 * pair, 128), 128)
        prob = jnp.exp(mm_nt(jnp.where(head_lanes[h], q_rows, 0), k[keys, columns])).astype(bf16)
        for at, rows in enumerate(probs_rows):
            probs[h, rows, keys] = prob[256 * at : 256 * at + 256]
        return mm(prob, vaug[pair, keys, :])

    def attended_of(parts, rows):
        both = jnp.where(first_head, parts[0], parts[1])
        inverse = 1.0 / both[:, 128:256]
        attended = both[:, 0:128] * inverse
        if rows is not None:
            att[rows, :] = attended
            inv[rows, :] = inverse
        return attended.astype(bf16)

    every = pl.ds(0, 1024)
    early = pl.ds(pl.multiple_of(512 * x, 512), 512)
    pairs = [(me + d) % 4 for d in range(4)]
    own_rows, far_rows = rows_of(x, c), rows_of(1 - x, c)
    own_half = pl.ds(pl.multiple_of(256 * x, 256), 256)
    far_half = pl.ds(pl.multiple_of(256 * (1 - x), 256), 256)

    def pair_columns(pair):
        return pl.ds(pl.multiple_of(128 * pair, 128), 128)

    def own_early(d, h):
        keep = [own_rows] if d == 0 else []
        sums[d, h, own_half, :] = attend(qt[own_half, pair_columns(pairs[d])], pairs[d], h, early, keep)

    def far_early(d, h):
        keep = [far_rows] if d == 0 else []
        sums[d, h, far_half, :] = attend(qt[far_half, pair_columns(pairs[d])], pairs[d], h, early, keep)

    def all_late(d, h, keys):
        keep = [rows_of(0, c), rows_of(1, c)] if d == 0 else []
        return sums[d, h] + attend(qt[:, pair_columns(pairs[d])], pairs[d], h, keys, keep)

    project(x, c, True)
    for i, h in in_turn:
        arrived(half(xb.at[x, 2 * (1 - c) + i], h), NUM["core_own"] + PIECES * i + h)
    project(x, 1 - c, False)
    for at, (i, h) in enumerate(in_turn):
        if at % (PIECES // 2) == 0:
            own_early(at // (PIECES // 2), 0)
            own_early(at // (PIECES // 2), 1)
        block = half(xb.at[1 - x, 2 * c + i], h)
        arrived(block, NUM["xn"] + PIECES * i + h)
        number = NUM["core_far"] + PIECES * i + h
        send(block, block, number, number, core_dev)
    project(1 - x, c, True)
    for d in range(4):
        for h in range(2):
            far_early(d, h)
            sums[d, h] = all_late(d, h, far_rows)
    for i, h in in_turn:
        arrived(half(xb.at[1 - x, 2 * (1 - c) + i], h), NUM["core_far"] + PIECES * i + h)
    project(1 - x, 1 - c, False)

    for d in range(4):
        parts = [all_late(d, h, rows_of(1 - x, 1 - c)) for h in range(2)]
        for xx in (0, 1):
            there = pl.ds(256 * xx, 256)
            abuf[there, pair_columns(pairs[d])] = attended_of(
                [part[256 * xx : 256 * xx + 256] for part in parts], rows_of(xx, c) if d == 0 else None
            )

    def other_probs(xx):
        rows = rows_of(xx, 1 - c)
        attended_of([attend(q[rows, :], me, h, every, [rows]) for h in range(2)], rows)

    def norm(hidden):
        centred = hidden - jnp.mean(hidden, axis=-1, keepdims=True)
        scale = lax.rsqrt(jnp.mean(centred * centred, axis=-1, keepdims=True) + eps_norm)
        return centred * scale, scale

    def norm_back(grad, normalized, scale, gain):
        e = grad * gain
        return scale * (
            e - jnp.mean(e, axis=-1, keepdims=True)
            - normalized * jnp.mean(e * normalized, axis=-1, keepdims=True)
        )

    def column_sum(values):
        return jnp.sum(values, axis=0, keepdims=True)

    once = jnp.where(x == 0, 1.0, 0.0)
    land(wait_ffn)
    for xx in (0, 1):
        there = pl.ds(256 * xx, 256)
        start_x = xb[xx, pl.ds(2 * c, 2)].reshape(256, 512).astype(f32) + pair_row
        normalized, s1 = norm(start_x + (mm(abuf[there, :], wo[...]) + ob[...]))
        s1b[there, :] = jnp.broadcast_to(s1, (256, 128))
        n1[there, :] = normalized
        normed = normalized * g1[...] + b1[...]
        normed_low[there, :] = normed.astype(bf16)
        normed_grad[there, :] = normed + start_x
    for j in range(4):
        cols = pl.ds(512 * j, 512)
        pre = mm(normed_low[...], wup[:, cols]) + ub[:, cols]
        before[:, cols] = pre
        act_low = (pre * (0.5 * (1.0 + lax.erf(pre * 0.7071067811865476)))).astype(bf16)
        act[:, cols] = act_low
        term = mm(act_low, wdn[cols, :])
        second[...] = term if j == 0 else second[...] + term
    for xx in (0, 1):
        there = pl.ds(256 * xx, 256)
        normalized, s2 = norm((second[there, :] + db[...]) + normed_grad[there, :])
        n2[there, :] = normalized
        s2b[there, :] = jnp.broadcast_to(s2, (256, 128))
    def give_back(block, out, name):
        for i in (0, 1):
            send(block.at[i], out.at[z % 2], NUM[name] + i, NUM[name] + z % 2, peer(i), when=2 * c + i != z)

        @pl.when(jnp.logical_not(crossing))
        def _():
            out[z % 2] = block[z % 2]

    def layer_back():
        lob[...] = (n2[own_half, :] * g2[...] + b2[...]).astype(bf16).reshape(2, 128, 512)
        give_back(lob, lo_out, "lo")

    for i in (0, 1):
        @pl.when(2 * c + i != z)
        def _():
            arrived(cotb.at[x, i], NUM["cot"] + i)
    for turn, (xx, there) in enumerate(((x, own_half), (1 - x, far_half))):
        if turn == 1:
            for i in (0, 1):
                arrived(cotb.at[1 - x, i], NUM["cot_x"] + i)
        g = cotb[xx].reshape(256, 512).astype(f32)
        normalized = n2[there, :]
        grad = norm_back(g, normalized, s2b[there, 0:1], g2[...])
        second[there, :] = grad
        low = grad.astype(bf16)
        ffn_grad[there, :] = low

    def number(n, step):
        return NUM["lane"] + 12 * n + step

    def add_up(target, parts, result=None):
        value = target[...].astype(f32)
        for part in parts:
            value = value + part[...].astype(f32)
        (target if result is None else result)[...] = value.astype(bf16)

    def travel(mine, r1, r3, whole, number_of, scatter, order):
        stages = []

        def scatter_stages(axis, last):
            def part(zz):
                return mine.at[y, zz] if last else mine.at[:, zz]

            def slot(d):
                return r3.at[d, 0] if last else r3.at[d]

            result = whole.at[x, c, y, z] if last else None
            if axis == "y":
                box = r1.at[0] if last else r1

                def start():
                    send(mine.at[1 - y, z] if last else mine.at[1 - y], box, number_of(1), number_of(1), y_dev)

                def finish():
                    arrived(box, number_of(1))
                    add_up(mine.at[y, z] if last else mine.at[y], [box], result)

                stages.append((start, finish))
            elif axis == "z":
                def start():
                    for d in (1, 2, 3):
                        send(part((z + d) % 4), slot(3 - d), number_of(1 + d), number_of(5 - d), z_devs[d - 1])

                def finish():
                    for d in (1, 2, 3):
                        arrived(slot(d - 1), number_of(1 + d))
                    add_up(part(z), [slot(d) for d in range(3)], result)

                stages.append((start, finish))
            else:
                def start():
                    send(part(3 - z_near), slot(0), number_of(2), number_of(2), near_dev)

                def finish():
                    arrived(slot(0), number_of(2))
                    add_up(part(3 - z), [slot(0)])

                def start_two():
                    send(part(3 - z), slot(1), number_of(3), number_of(3), mirror_dev)
                    send(part(z_near), slot(2), number_of(4), number_of(4), near_dev)

                def finish_two():
                    arrived(slot(1), number_of(3))
                    arrived(slot(2), number_of(4))
                    add_up(part(z), [slot(1), slot(2)], result)

                stages.append((start, finish))
                stages.append((start_two, finish_two))

        def region(done, **other):
            place = dict(x=x, y=y, z=z) | other
            at = {axis: slice(None) if axis in done else place[axis] for axis in "xyz"}
            return whole.at[at["x"], c, at["y"], at["z"]]

        def gather_stages(axis, done):
            part = region(done)
            if axis == "z":
                def start():
                    for d in (1, 2, 3):
                        send(part, part, number_of(4 + d), number_of(8 - d), z_devs[d - 1])

                def finish():
                    for d in (1, 2, 3):
                        arrived(region(done, z=(z + d) % 4), number_of(4 + d))

                stages.append((start, finish))
            elif axis == "w":
                def start():
                    send(part, part, number_of(6), number_of(6), mirror_dev)
                    send(part, part, number_of(5), number_of(5), near_dev)

                def finish():
                    arrived(region(done, z=z_near), number_of(5))
                    arrived(region(done, z=3 - z), number_of(6))

                def start_two():
                    passed = region(done, z=3 - z)
                    send(passed, passed, number_of(7), number_of(7), near_dev)

                def finish_two():
                    arrived(region(done, z=3 - z_near), number_of(7))

                stages.append((start, finish))
                stages.append((start_two, finish_two))
            else:
                at, device, there = {"x": (9, x_dev, dict(x=1 - x)), "y": (8, y_dev, dict(y=1 - y))}[axis]

                def start():
                    send(part, part, number_of(at), number_of(at), device)

                def finish():
                    arrived(region(done, **there), number_of(at))

                stages.append((start, finish))

        scatter_stages(scatter[0], False)
        scatter_stages(scatter[1], True)
        for at, axis in enumerate(order):
            gather_stages(axis, order[:at].replace("w", "z"))

        def start():
            send(whole.at[:, c], whole.at[:, c], number_of(10), number_of(10), core_dev)

        def finish():
            arrived(whole.at[:, 1 - c], number_of(10))

        stages.append((start, finish))
        return stages

    lane_stages = [
        travel(own.at[n, c], r1.at[n], r3.at[n], full.at[n], functools.partial(number, n), SCATTER[n], GATHER[n])
        for n in range(LANES)
    ]

    def lane_step(n, step):
        if step == 0:
            arrived(r0.at[n], number(n, 0))
            add_up(own.at[n, c], [r0.at[n]])
        else:
            lane_stages[n][step - 1][1]()
        if step < len(lane_stages[n]):
            lane_stages[n][step][0]()

    own_columns = pl.ds(pl.multiple_of(256 * x, 256), 256)

    def lane_fill(n):
        if n < 4:
            value = mm_tn(act[:, pl.ds(pl.multiple_of(512 * n + 256 * x, 256), 256)], ffn_grad[...])
        elif n < 8:
            value = mm_tn(normed_low[:, own_columns], pre_grad[:, pl.ds(512 * (n - 4), 512)])
        else:
            value = mm_tn(abuf[:, own_columns], attn_grad[...])
        own[n] = value.astype(bf16).reshape(2, 2, 4, 16, 512)
        send(own.at[n, 1 - c], r0.at[n], number(n, 0), number(n, 0), core_dev)

    def ffn_back(j):
        cols = pl.ds(512 * j, 512)
        pre = before[:, cols]
        cdf = 0.5 * (1.0 + lax.erf(pre * 0.7071067811865476))
        slope = cdf + pre * (jnp.exp(-0.5 * pre * pre) * 0.3989422804014327)
        grad = (mm_nt(ffn_grad[...], wdn[cols, :]) * slope).astype(bf16)
        pre_grad[:, cols] = grad
        vecb[16 + j : 17 + j, :] = column_sum(grad.astype(f32)) * once
        normed_grad[...] = (second if j == 0 else normed_grad)[...] + mm_nt(grad, wup[:, cols])

    def first_back():
        for xx in (0, 1):
            there = pl.ds(256 * xx, 256)
            grad, normalized = normed_grad[there, :], n1[there, :]
            first_grad = norm_back(grad, normalized, s1b[there, 0:1], g1[...])
            low = first_grad.astype(bf16)
            attn_grad[there, :] = low
            second[there, :] = second[there, :] + first_grad
        res[...] = second[own_half, :]
        low = attn_grad[...]

        def heads(cc):
            return pl.ds(pl.multiple_of(128 * (2 * x + cc), 128), 128)

        dob[...] = mm_nt(low, wo[heads(1 - c), :]).astype(bf16)
        send(dob, dor.at[c], NUM["do"], NUM["do"], core_dev)
        dor[c] = mm_nt(low, wo[heads(c), :]).astype(bf16)

    def norm_sums(which):
        if which == 0:
            grad, normalized, low, at = cotb[...].reshape(512, 512).astype(f32), n2[...], ffn_grad[...], 13
        else:
            grad, normalized, low, at = normed_grad[...], n1[...], attn_grad[...], 10
        vecb[at : at + 1, :] = column_sum(low.astype(f32)) * once
        vecb[at + 1 : at + 2, :] = column_sum(grad * normalized) * once
        vecb[at + 2 : at + 3, :] = column_sum(grad) * once

    turns = ((0, c), (1, c), (0, 1 - c), (1, 1 - c))

    def attention_back(turn):
        xx, cc = turns[turn]
        if turn == 2:
            arrived(dor.at[cc], NUM["do"])
        rows = rows_of(xx, cc)
        d_out = dor[cc, 256 * xx : 256 * xx + 256, :].astype(f32)
        numer_grad = d_out * inv[rows, :]
        product = numer_grad.astype(bf16).astype(f32) * att[rows, :]
        q_rows = q[rows, :]
        dq_rows = jnp.zeros((256, 128), f32)
        for h in range(2):
            total = -jnp.sum(jnp.where(head_lanes[h], product, 0.0), axis=1, keepdims=True)
            high = total.astype(bf16).astype(f32)
            edge = 64 * (1 - h)
            rest = jnp.where(lane == edge, high, jnp.where(lane == edge + 1, total - high, 0.0))
            grad_low = jnp.where(head_lanes[h], numer_grad, rest).astype(bf16)
            prob = probs[h, rows, :]
            score_grad = (prob.astype(f32) * mm_nt(grad_low, vback[h])).astype(bf16)
            dq_rows = dq_rows + jnp.where(head_lanes[h], mm(score_grad, k[:, mine]), 0.0)
            part = slice(64 * h, 64 * h + 64)
            dk_part = mm(jnp.transpose(q_rows)[part, :], score_grad)
            dv_part = mm(jnp.transpose(grad_low)[part, :], prob)
            dkt[part, :] = dk_part if turn == 0 else dkt[part, :] + dk_part
            dvt[part, :] = dv_part if turn == 0 else dvt[part, :] + dv_part
        dqkv[rows, 0:128] = (dq_rows * 0.125).astype(bf16)

    def projection_grads():
        for xx in (0, 1):
            for cc in (0, 1):
                rows = pl.ds(512 * xx + 256 * cc, 256)
                dqkv[rows, 128:256] = jnp.transpose(dkt[:, rows]).astype(bf16)
                dqkv[rows, 256:384] = jnp.where(usable_rows(xx, cc), jnp.transpose(dvt[:, rows]), 0.0).astype(bf16)

    def qnumber(t, step):
        return NUM["qkv"] + 12 * t + step

    part_stages = [
        travel(qown.at[t], qr1.at[t], qr3.at[t], qfull.at[t], functools.partial(qnumber, t), QSCATTER[t], QGATHER[t])
        for t in range(3)
    ]

    def projection_weights(t):
        value = mm_tn(lowb[...], dqkv[:, 128 * t : 128 * t + 128])
        qown[t] = value.astype(bf16).reshape(2, 4, 64, 128)
        part_stages[t][0][0]()

    def projection_step(t, step):
        part_stages[t][step][1]()
        if step + 1 < len(part_stages[t]):
            part_stages[t][step + 1][0]()

    def input_back(step):
        xx, cc = ((1 - x, 1 - c), (x, 1 - c), (1 - x, c), (x, c))[step]
        block = mm_nt(dqkv[rows_of(xx, cc), :], wq[...])
        vecb[20:21, :] = column_sum(block) if step == 0 else vecb[20:21, :] + column_sum(block)
        if step < 2:
            dxb[step] = block.astype(bf16)
            send(dxb.at[step], dxr0.at[step], NUM["dx_core"] + step, NUM["dx_core"] + step, core_dev)
        elif step == 2:
            arrived(dxr0.at[0], NUM["dx_core"])
            dxb[2] = (block + dxr0[0].astype(f32)).astype(bf16)
            send(dxb.at[2], dxr1, NUM["dx_x"], NUM["dx_x"], x_dev)
        else:
            arrived(dxr0.at[1], NUM["dx_core"] + 1)
            dxo[...] = block + dxr0[1].astype(f32) + res[...]

    def input_out():
        arrived(dxr1, NUM["dx_x"])
        igb[...] = (dxo[...] + dxr1[...].astype(f32)).astype(bf16).reshape(2, 128, 512)
        give_back(igb, ig_out, "ig")

    def vectors(step):
        if step == 0:
            group_iota = lax.broadcasted_iota(jnp.int32, (8, 512), 0).astype(f32)
            column_total = vecb[20:21, :] + column_sum(res[...])
            vecb[0:8, :] = jnp.where(group_iota == group_row, column_total, 0.0)
            vecb[8:10, :] = jnp.zeros((2, 512), f32)
            vecb[8:9, mine] = column_sum(dqkv[:, 0:128].astype(f32))
            vecb[9:10, mine] = column_sum(dqkv[:, 256:384].astype(f32))
            vecb[20:24, :] = jnp.zeros((4, 512), f32)
            send(vecb, vecr.at[0], NUM["vec"], NUM["vec"], core_dev)
        else:
            level = step - 1
            arrived(vecr.at[level], NUM["vec"] + level)
            value = (vecb if level == 0 else vecr.at[4 + level])[...] + vecr[level]
            if level < 4:
                vecr[5 + level] = value
                send(vecr.at[5 + level], vecr.at[level + 1], NUM["vec"] + level + 1, NUM["vec"] + level + 1,
                     (x_dev, y_dev, near_dev, mirror_dev)[level])
            else:
                vec_out[...] = value

    tasks = {(NORM, 0, 0): first_back, (SPLIT, 0, 0): projection_grads, (RETURN, 0, 0): input_out, (RETURN, 1, 0): layer_back}
    for kind, task, count in (
        (FILL, lane_fill, LANES), (FFN, ffn_back, 4), (ATTN, attention_back, 4), (PROBS, other_probs, 2), (WEIGHT, projection_weights, 3),
        (INPUT, input_back, 4), (SMALL, vectors, 6), (SUMS, norm_sums, 2),
    ):
        for at in range(count):
            tasks[kind, at, 0] = functools.partial(task, at)
    for n in range(LANES):
        for step in range(len(lane_stages[n]) + 1):
            tasks[LANE, n, step] = functools.partial(lane_step, n, step)
    for t in range(3):
        for step in range(len(part_stages[t])):
            tasks[PART, t, step] = functools.partial(projection_step, t, step)
    for at, entry in enumerate(ORDER):
        tasks.pop(entry)()
    assert not tasks

    for name, out in (("lo", lo_out), ("ig", ig_out)):
        for i in (0, 1):
            @pl.when(2 * c + i != z)
            def _():
                arrived(out.at[i], NUM[name] + i)
    land([copy for copy in local_copies if copy is not None])
    for copy, when in pending:
        if when is None:
            copy.wait_send()
        else:
            pl.when(when)(copy.wait_send)


VECTOR_ROWS = (8, 9, 10, 11, 12, 13, 14, 15)


def finish(lo, ig, full, qfull, vec, *refs):
    lo_out, ig_out, down_out, up_out, out_out, qkv_out, pair_out = refs[:7]
    vector_outs, up_bias_out = refs[7:15], refs[15]
    lo_wide, ig_wide, full_wide, qkv_wide, rows, up_bias, sems = *refs[16:20], refs[20:28], refs[28], refs[29]
    writes = []

    def write(src, dst):
        made = pltpu.make_async_copy(src, dst, sems.at[len(writes)])
        made.start()
        writes.append(made)

    for n in range(LANES):
        for half in range(2):
            at = pl.ds(256 * half, 256)
            full_wide[n, at, :] = full[n, half].reshape(256, 512).astype(f32)
            if n < 4:
                write(full_wide.at[n, at], down_out.at[pl.ds(512 * n + 256 * half, 256)])
            elif n < 8:
                write(full_wide.at[n, at], up_out.at[at, pl.ds(512 * (n - 4), 512)])
            else:
                write(full_wide.at[n, at], out_out.at[at])
    for t in range(3):
        for h in range(4):
            columns = pl.ds(512 * t + 128 * h, 128)
            qkv_wide[:, columns] = qfull[t, h // 2, h % 2].reshape(512, 128).astype(f32)
        columns = pl.ds(512 * t, 512)
        write(qkv_wide.at[:, columns], qkv_out.at[:, columns])
    for block, wide, out in ((lo, lo_wide, lo_out), (ig, ig_wide, ig_out)):
        wide[...] = block[...].astype(f32)
        write(wide, out)
    write(vec.at[pl.ds(0, 8)], pair_out)
    for at, row, out in zip(VECTOR_ROWS, rows, vector_outs):
        row[...] = vec[at : at + 1, :]
        write(row, out)
    for j in range(4):
        up_bias[:, 512 * j : 512 * j + 512] = vec[16 + j : 17 + j, :]
    write(up_bias, up_bias_out)
    for made in writes:
        made.wait()


def pair_plan(mesh):
    return dict(mesh.shape) == {"batch": 4, "seq": 8}


def fused_local(
    block_input, cotangent, groups, lengths, pair_table, qkv_weight, q_bias, v_bias, out_weight,
    out_bias, norm1_gain, norm1_bias, up_weight, up_bias, down_weight, down_bias, norm2_gain, norm2_bias,
):
    any_spec, smem = pl.BlockSpec(memory_space=pl.ANY), pl.BlockSpec(memory_space=pltpu.SMEM)

    def row(vector):
        return vector[None, :]

    operands = (
        block_input, cotangent, groups, lengths, pair_table, qkv_weight, row(q_bias), row(v_bias),
        out_weight, row(out_bias), row(norm1_gain), row(norm1_bias), up_weight, row(up_bias),
        down_weight, row(down_bias), row(norm2_gain), row(norm2_bias),
    )
    in_specs = [smem if i in (2, 3) else any_spec for i in range(len(operands))]
    vmem = pl.BlockSpec(memory_space=pltpu.VMEM)
    out_shape = [
        pltpu.VMEM(shape, dtype)
        for shape, dtype in (
            ((2, 128, 512), bf16), ((2, 128, 512), bf16), ((LANES, 2, 2, 2, 4, 16, 512), bf16),
            ((3, 2, 2, 2, 4, 64, 128), bf16), ((24, 512), f32),
        )
    ]
    scratch = [
        pltpu.VMEM(shape, dtype)
        for shape, dtype in (
            ((2, 128, 512), bf16), ((2, 128, 512), bf16),
            ((2, 4, 128, 512), bf16), ((1024, 512), bf16), ((2, 2, 128, 512), bf16),
            ((8, 512), f32), ((8, 512), f32), ((8, 512), f32),
            ((512, 1536), bf16), ((512, 384), bf16), ((512, 512), bf16), ((512, 2048), bf16), ((2048, 512), bf16),
            ((1, 512), f32), ((1, 512), f32), ((1, 512), f32), ((1, 512), f32), ((1, 512), f32),
            ((1, 2048), f32), ((1, 512), f32), ((1, 512), f32), ((1, 512), f32),
            ((512, 512), bf16), ((1024, 128), bf16), ((1024, 512), bf16),
            ((4, 1024, 256), bf16), ((2, 1024, 128), bf16),
            ((1024, 128), f32), ((1024, 128), f32),
            ((4, 2, 512, 256), f32), ((512, 512), bf16),
            ((512, 2048), f32), ((512, 2048), bf16), ((512, 2048), bf16),
            ((256, 512), f32), ((2, 128, 512), bf16), ((2, 128, 512), bf16),
            ((512, 512), f32), ((512, 512), f32), ((512, 128), f32), ((512, 128), f32),
            ((512, 512), bf16),
            ((512, 512), bf16), ((512, 512), bf16), ((512, 512), f32), ((512, 512), f32),
            ((512, 128), bf16), ((2, 512, 128), bf16), ((2, 1024, 1024), bf16),
            ((128, 1024), f32), ((128, 1024), f32), ((1024, 384), bf16),
            ((3, 256, 512), bf16), ((2, 256, 512), bf16), ((256, 512), bf16), ((256, 512), f32),
            ((24, 512), f32), ((9, 24, 512), f32),
            ((LANES, 2, 2, 4, 16, 512), bf16), ((LANES, 2, 4, 16, 512), bf16), ((LANES, 4, 16, 512), bf16),
            ((LANES, 3, 2, 16, 512), bf16),
            ((3, 2, 4, 64, 128), bf16), ((3, 4, 64, 128), bf16), ((3, 3, 2, 64, 128), bf16),
        )
    ] + [
        pltpu.SemaphoreType.DMA((NUM.count,)),
        pltpu.SemaphoreType.DMA((NUM.count,)),
        pltpu.SemaphoreType.DMA((LOCAL,)),
    ]
    results = pl.pallas_call(
        fused,
        out_shape=out_shape,
        in_specs=in_specs,
        out_specs=[vmem] * len(out_shape),
        scratch_shapes=scratch,
        compiler_params=pltpu.CompilerParams(
            collective_id=0, has_side_effects=True, vmem_limit_bytes=54 * 2**20
        ),
    )(*operands)
    shapes = [(2, 128, 512)] * 2 + [(2048, 512), (512, 2048), (512, 512), (512, 1536), (8, 512)]
    shapes += [(1, 512)] * 8 + [(1, 2048)]
    scratch_sizes = [(2, 128, 512)] * 2 + [(LANES, 512, 512), (512, 1536)] + [(1, 512)] * 8 + [(1, 2048)]
    results = pl.pallas_call(
        finish,
        out_shape=[jax.ShapeDtypeStruct(shape, f32) for shape in shapes],
        in_specs=[vmem] * 5,
        out_specs=[any_spec] * len(shapes),
        scratch_shapes=[pltpu.VMEM(shape, f32) for shape in scratch_sizes] + [pltpu.SemaphoreType.DMA((40,))],
        compiler_params=pltpu.CompilerParams(vmem_limit_bytes=40 * 2**20),
    )(*results)
    layer_out, input_grad, down_grad, up_grad, out_grad, qkv_grad, pair_grad = results[:7]
    q_grad, v_grad, ob_grad, g1_grad, b1_grad, db_grad, g2_grad, b2_grad = [r.reshape(512) for r in results[7:15]]
    return (
        layer_out, input_grad, pair_grad, qkv_grad, q_grad, v_grad,
        out_grad, ob_grad, g1_grad, b1_grad, up_grad, results[15].reshape(2048), down_grad, db_grad, g2_grad, b2_grad,
    )


def solution(mesh):
    in_specs = (
        P("batch", "seq", None),
        P("batch", "seq", None),
        P("batch"),
        P("batch"),
        P(),
        P(),
        P(),
        P(),
        P(),
        P(),
        P(),
        P(),
        P(),
        P(),
        P(),
        P(),
        P(),
        P(),
    )
    out_specs = (
        P("batch", "seq", None),
        P("batch", "seq", None),
        P(),
        P(),
        P(),
        P(),
        P(),
        P(),
        P(),
        P(),
        P(),
        P(),
        P(),
        P(),
        P(),
        P(),
    )
    return jax.shard_map(fused_local if pair_plan(mesh) else local, mesh=mesh, in_specs=in_specs, out_specs=out_specs, check_vma=False)
```

```python
import functools

import jax
import jax.numpy as jnp
from jax import lax
from jax.experimental import pallas as pl
from jax.experimental.pallas import tpu as pltpu
from jax.sharding import PartitionSpec as P

HEADS = 8


highest = lax.Precision.HIGHEST
eps_norm = 1e-05


def layer_norm(hidden, norm_gain, norm_shift):
    row_mean = jnp.mean(hidden, axis=-1, keepdims=True)
    centred = hidden - row_mean
    spread = jnp.mean(centred * centred, axis=-1, keepdims=True)
    return centred * lax.rsqrt(spread + eps_norm) * norm_gain + norm_shift


def exact_gelu(pre_act):
    return jax.nn.gelu(pre_act, approximate=False)


def block_size():
    return 512


def to_heads(flat_rows, head_count):
    return flat_rows.reshape(
        flat_rows.shape[0], flat_rows.shape[1], head_count, flat_rows.shape[2] // head_count
    )


def masked_exp(query_block, key_block, key_first, row_lengths, score_scale):
    scores = (
        jnp.einsum("rihd,rjhd->rhij", query_block, key_block, preferred_element_type=jnp.float32)
        * score_scale
    )
    places = key_first + jnp.arange(key_block.shape[1], dtype=jnp.int32)
    usable = places[None, :] < row_lengths[:, None]
    return jnp.where(usable[:, None, None, :], jnp.exp(scores), 0.0)


def forward_piece(
    running, key_piece, value_piece, query_heads, row_lengths, score_scale, head_count
):
    piece_len = key_piece.shape[1]
    block_len = block_size()
    key_all = to_heads(key_piece, head_count)
    value_all = to_heads(value_piece, head_count)

    def forward_one_block(block_index, partial_sums):
        numerator, denominator = partial_sums
        block_first = block_index * block_len
        key_block = lax.dynamic_slice_in_dim(key_all, block_first, block_len, 1)
        value_block = lax.dynamic_slice_in_dim(value_all, block_first, block_len, 1)
        exp_scores = masked_exp(query_heads, key_block, block_first, row_lengths, score_scale)
        denominator = denominator + jnp.sum(exp_scores, axis=-1)
        numerator = numerator + jnp.einsum(
            "rhij,rjhd->rihd",
            exp_scores.astype(jnp.bfloat16),
            value_block,
            preferred_element_type=jnp.float32,
        )
        return (numerator, denominator)

    return lax.fori_loop(0, piece_len // block_len, forward_one_block, running)


def key_side(
    running,
    query_piece,
    grad_piece,
    total_piece,
    key_heads,
    value_heads,
    key_first,
    row_lengths,
    score_scale,
    head_count,
):
    piece_len = query_piece.shape[1]
    block_len = block_size()
    query_all = to_heads(query_piece.astype(jnp.bfloat16), head_count)
    grad_all = to_heads(grad_piece, head_count)
    value_wide = value_heads.astype(jnp.float32)

    def key_one_block(block_index, partial_grads):
        key_grad, value_grad = partial_grads
        block_first = block_index * block_len
        query_block = lax.dynamic_slice_in_dim(query_all, block_first, block_len, 1)
        grad_block = lax.dynamic_slice_in_dim(grad_all, block_first, block_len, 1)
        total_block = lax.dynamic_slice_in_dim(total_piece, block_first, block_len, 1)
        exp_scores = masked_exp(query_block, key_heads, key_first, row_lengths, score_scale)
        prob_grad = jnp.einsum(
            "rihd,rjhd->rhij",
            grad_block,
            value_wide,
            precision=highest,
            preferred_element_type=jnp.float32,
        )
        shift_grad = jnp.transpose(total_block, (0, 2, 1))[..., None]
        score_grad = (exp_scores * (prob_grad + shift_grad)).astype(jnp.bfloat16)
        key_grad = (
            key_grad
            + jnp.einsum(
                "rhij,rihd->rjhd", score_grad, query_block, preferred_element_type=jnp.float32
            )
            * score_scale
        )
        exp_low = exp_scores.astype(jnp.bfloat16).astype(jnp.float32)
        value_grad = value_grad + jnp.einsum(
            "rhij,rihd->rjhd",
            exp_low,
            grad_block,
            precision=highest,
            preferred_element_type=jnp.float32,
        )
        return (key_grad, value_grad)

    return lax.fori_loop(0, piece_len // block_len, key_one_block, running)


def query_side(
    running,
    key_piece,
    value_piece,
    query_heads,
    grad_heads,
    total_here,
    row_lengths,
    score_scale,
    head_count,
):
    piece_len = key_piece.shape[1]
    block_len = block_size()
    key_all = to_heads(key_piece, head_count)
    value_all = to_heads(value_piece, head_count)

    def query_one_block(block_index, query_grad):
        block_first = block_index * block_len
        key_block = lax.dynamic_slice_in_dim(key_all, block_first, block_len, 1)
        value_block = lax.dynamic_slice_in_dim(value_all, block_first, block_len, 1)
        exp_scores = masked_exp(query_heads, key_block, block_first, row_lengths, score_scale)
        prob_grad = jnp.einsum(
            "rihd,rjhd->rhij",
            grad_heads,
            value_block.astype(jnp.float32),
            precision=highest,
            preferred_element_type=jnp.float32,
        )
        score_grad = (exp_scores * (prob_grad + total_here[..., None])).astype(jnp.bfloat16)
        return (
            query_grad
            + jnp.einsum(
                "rhij,rjhd->rihd", score_grad, key_block, preferred_element_type=jnp.float32
            )
            * score_scale
        )

    return lax.fori_loop(0, piece_len // block_len, query_one_block, running)


def local(
    block_input,
    cotangent,
    groups,
    lengths,
    pair_table,
    qkv_weight,
    q_bias,
    v_bias,
    out_weight,
    out_bias,
    norm1_gain,
    norm1_bias,
    up_weight,
    up_bias,
    down_weight,
    down_bias,
    norm2_gain,
    norm2_bias,
):
    row_count, shard_len, model_width = block_input.shape
    head_count = HEADS
    head_size = model_width // head_count
    score_scale = head_size ** (-0.5)
    key_offset = lax.axis_index("seq") * shard_len
    pair_onehot = (
        groups[:, None] == jnp.arange(pair_table.shape[0], dtype=jnp.int32)[None, :]
    ).astype(jnp.float32)
    lifted = jnp.dot(pair_onehot, pair_table, precision=highest)
    start_x = block_input.astype(jnp.float32) + lifted[:, None, :]
    lowered = start_x.astype(jnp.bfloat16)
    projected = jnp.einsum("rtd,de->rte", lowered, qkv_weight, preferred_element_type=jnp.float32)
    query_rows = (projected[:, :, :model_width] + q_bias).astype(jnp.bfloat16)
    key_rows = projected[:, :, model_width : 2 * model_width].astype(jnp.bfloat16)
    value_rows = (projected[:, :, 2 * model_width :] + v_bias).astype(jnp.bfloat16)
    query_heads = to_heads(query_rows, head_count)
    key_heads = to_heads(key_rows, head_count)
    value_heads = to_heads(value_rows, head_count)
    zero_heads = jnp.zeros((row_count, shard_len, head_count, head_size), jnp.float32)
    zero_totals = jnp.zeros((row_count, head_count, shard_len), jnp.float32)
    incoming = (
        lax.all_gather(key_rows, "seq", axis=1, tiled=True),
        lax.all_gather(value_rows, "seq", axis=1, tiled=True),
    )
    numerator, denominator = forward_piece(
        (zero_heads, zero_totals),
        incoming[0],
        incoming[1],
        query_heads,
        lengths,
        score_scale,
        head_count,
    )
    inverse = 1.0 / jnp.transpose(denominator, (0, 2, 1))[..., None]
    attended = numerator * inverse
    attended_low = attended.reshape(row_count, shard_len, model_width).astype(jnp.bfloat16)
    attn_out = (
        jnp.einsum("rtd,de->rte", attended_low, out_weight, preferred_element_type=jnp.float32)
        + out_bias
    )
    normed, norm1_back = jax.vjp(layer_norm, start_x + attn_out, norm1_gain, norm1_bias)
    normed_low = normed.astype(jnp.bfloat16)
    pre_act = (
        jnp.einsum("rtd,df->rtf", normed_low, up_weight, preferred_element_type=jnp.float32)
        + up_bias
    )
    activated, gelu_back = jax.vjp(exact_gelu, pre_act)
    activated_low = activated.astype(jnp.bfloat16)
    ffn_out = (
        jnp.einsum("rtf,fd->rtd", activated_low, down_weight, preferred_element_type=jnp.float32)
        + down_bias
    )
    layer_out, norm2_back = jax.vjp(layer_norm, ffn_out + normed + start_x, norm2_gain, norm2_bias)
    second_grad, norm2_gain_grad, norm2_bias_grad = norm2_back(cotangent.astype(jnp.float32))
    ffn_grad = second_grad.astype(jnp.bfloat16)
    down_bias_grad = jnp.sum(ffn_grad.astype(jnp.float32), axis=(0, 1))
    down_weight_grad = jnp.einsum(
        "rtf,rtd->fd", activated_low, ffn_grad, preferred_element_type=jnp.float32
    )
    act_grad = jnp.einsum("rtd,fd->rtf", ffn_grad, down_weight, preferred_element_type=jnp.float32)
    pre_grad = gelu_back(act_grad)[0].astype(jnp.bfloat16)
    up_bias_grad = jnp.sum(pre_grad.astype(jnp.float32), axis=(0, 1))
    up_weight_grad = jnp.einsum(
        "rtd,rtf->df", normed_low, pre_grad, preferred_element_type=jnp.float32
    )
    normed_grad = second_grad + jnp.einsum(
        "rtf,df->rtd", pre_grad, up_weight, preferred_element_type=jnp.float32
    )
    first_grad, norm1_gain_grad, norm1_bias_grad = norm1_back(normed_grad)
    attn_grad = first_grad.astype(jnp.bfloat16)
    out_bias_grad = jnp.sum(attn_grad.astype(jnp.float32), axis=(0, 1))
    out_weight_grad = jnp.einsum(
        "rtd,rte->de", attended_low, attn_grad, preferred_element_type=jnp.float32
    )
    attended_grad = to_heads(
        jnp.einsum("rte,de->rtd", attn_grad, out_weight, preferred_element_type=jnp.float32),
        head_count,
    )
    numer_grad = attended_grad * inverse
    total_grad = -jnp.sum(attended_grad * attended, axis=-1) * inverse[..., 0]
    grad_rows = numer_grad.reshape(row_count, shard_len, model_width)
    total_here = jnp.transpose(total_grad, (0, 2, 1))
    incoming = (
        lax.all_gather(query_rows.astype(jnp.float32), "seq", axis=1, tiled=True),
        lax.all_gather(grad_rows, "seq", axis=1, tiled=True),
        lax.all_gather(total_grad, "seq", axis=1, tiled=True),
    )
    key_grad, value_grad = key_side(
        (zero_heads, zero_heads),
        incoming[0],
        incoming[1],
        incoming[2],
        key_heads,
        value_heads,
        key_offset,
        lengths,
        score_scale,
        head_count,
    )
    incoming = (
        lax.all_gather(key_rows, "seq", axis=1, tiled=True),
        lax.all_gather(value_rows, "seq", axis=1, tiled=True),
    )
    query_grad = query_side(
        zero_heads,
        incoming[0],
        incoming[1],
        query_heads,
        numer_grad,
        total_here,
        lengths,
        score_scale,
        head_count,
    )
    flat_shape = (row_count, shard_len, model_width)
    query_low = query_grad.reshape(flat_shape).astype(jnp.bfloat16)
    key_low = key_grad.reshape(flat_shape).astype(jnp.bfloat16)
    value_low = value_grad.reshape(flat_shape).astype(jnp.bfloat16)
    qkv_grad = jnp.concatenate([query_low, key_low, value_low], axis=-1)
    qkv_weight_grad = jnp.einsum(
        "rtd,rte->de", lowered, qkv_grad, preferred_element_type=jnp.float32
    )
    q_bias_grad = jnp.sum(query_low.astype(jnp.float32), axis=(0, 1))
    v_bias_grad = jnp.sum(value_low.astype(jnp.float32), axis=(0, 1))
    input_grad = (
        jnp.einsum("rte,de->rtd", qkv_grad, qkv_weight, preferred_element_type=jnp.float32)
        + first_grad
        + second_grad
    )
    pair_table_grad = jnp.dot(
        jnp.transpose(pair_onehot), jnp.sum(input_grad, axis=1), precision=highest
    )
    summed = lax.psum(
        (
            pair_table_grad,
            qkv_weight_grad,
            q_bias_grad,
            v_bias_grad,
            out_weight_grad,
            out_bias_grad,
            norm1_gain_grad,
            norm1_bias_grad,
            up_weight_grad,
            up_bias_grad,
            down_weight_grad,
            down_bias_grad,
            norm2_gain_grad,
            norm2_bias_grad,
        ),
        ("batch", "seq"),
    )
    return (
        layer_out,
        input_grad,
        summed[0],
        summed[1],
        summed[2],
        summed[3],
        summed[4],
        summed[5],
        summed[6],
        summed[7],
        summed[8],
        summed[9],
        summed[10],
        summed[11],
        summed[12],
        summed[13],
    )


MESH = pl.DeviceIdType.MESH
f32, bf16 = jnp.float32, jnp.bfloat16
LANES = 9
PIECES, PIECE = 4, 32


def mm(a, b):
    return jnp.dot(a, b, preferred_element_type=f32)


def mm_nt(a, b):
    return lax.dot_general(a, b, (((1,), (1,)), ((), ())), preferred_element_type=f32)


def mm_tn(a, b):
    return lax.dot_general(a, b, (((0,), (0,)), ((), ())), preferred_element_type=f32)


class Numbers:
    def __init__(self):
        self.count = 0
        self.first = {}

    def take(self, name, size=1):
        self.first[name] = self.count
        self.count += size

    def __getitem__(self, name):
        return self.first[name]


def semaphore_numbers():
    numbers = Numbers()
    for name, size in (
        ("x", 2 * PIECES), ("cot", 2), ("lo", 2), ("ig", 2), ("cot_x", 2),
        ("xn", 2 * PIECES), ("core_own", 2 * PIECES), ("core_far", 2 * PIECES), ("meta", 1),
        ("do", 1), ("dx_core", 2), ("dx_x", 1), ("vec", 6),
        ("lane", LANES * 12), ("qkv", 3 * 12),
    ):
        numbers.take(name, size)
    return numbers


NUM = semaphore_numbers()
LOCAL = 19

SCATTER = ('yz', 'yz', 'yz', 'yz', 'yw', 'yw', 'yw', 'yw', 'yw')
GATHER = ('wyx', 'wxy', 'zxy', 'wyx', 'wxy', 'zyx', 'zyx', 'zxy', 'zyx')
QSCATTER = ('yw', 'yw', 'yw')
QGATHER = ('wxy', 'zxy', 'zyx')
FILL, LANE, FFN, NORM, ATTN, SPLIT, WEIGHT, PART, INPUT, RETURN, SMALL, PROBS, SUMS = range(13)
ORDER = (
    (RETURN, 1, 0), (FILL, 2, 0), (FILL, 1, 0), (FFN, 0, 0), (FILL, 0, 0), (LANE, 2, 0), (LANE, 1, 0),
    (FFN, 1, 0), (PROBS, 1, 0), (FILL, 4, 0), (FILL, 5, 0), (LANE, 0, 0), (FFN, 2, 0), (FFN, 3, 0),
    (FILL, 3, 0), (LANE, 2, 1), (LANE, 4, 0), (NORM, 0, 0), (FILL, 8, 0), (LANE, 1, 1), (LANE, 5, 0),
    (PROBS, 0, 0), (FILL, 6, 0), (FILL, 7, 0), (LANE, 8, 0), (LANE, 0, 1), (LANE, 3, 0), (ATTN, 0, 0),
    (LANE, 7, 0), (LANE, 4, 1), (LANE, 2, 2), (ATTN, 1, 0), (LANE, 5, 1), (LANE, 6, 0), (LANE, 1, 2),
    (ATTN, 2, 0), (LANE, 8, 1), (LANE, 0, 2), (LANE, 4, 2), (ATTN, 3, 0), (SPLIT, 0, 0), (LANE, 5, 2),
    (INPUT, 0, 0), (LANE, 2, 3), (LANE, 3, 1), (WEIGHT, 0, 0), (INPUT, 1, 0), (LANE, 7, 1), (INPUT, 2, 0),
    (WEIGHT, 1, 0), (WEIGHT, 2, 0), (INPUT, 3, 0), (LANE, 1, 3), (LANE, 0, 3), (LANE, 8, 2), (LANE, 4, 3),
    (SUMS, 0, 0), (PART, 0, 0), (LANE, 5, 3), (LANE, 3, 2), (LANE, 0, 4), (LANE, 7, 2), (LANE, 2, 4),
    (LANE, 1, 4), (SUMS, 1, 0), (LANE, 6, 1), (SMALL, 0, 0), (PART, 0, 1), (SMALL, 1, 0), (LANE, 4, 4),
    (LANE, 8, 3), (PART, 1, 0), (LANE, 0, 5), (LANE, 5, 4), (PART, 2, 0), (LANE, 6, 2), (LANE, 7, 3),
    (LANE, 1, 5), (LANE, 3, 3), (PART, 0, 2), (LANE, 4, 5), (PART, 2, 1), (LANE, 8, 4), (LANE, 5, 5),
    (PART, 1, 1), (SMALL, 2, 0), (LANE, 6, 3), (LANE, 3, 4), (LANE, 7, 4), (LANE, 4, 6), (PART, 0, 3),
    (LANE, 8, 5), (PART, 2, 2), (PART, 1, 2), (PART, 0, 4), (LANE, 6, 4), (LANE, 0, 6), (SMALL, 3, 0),
    (LANE, 2, 5), (LANE, 1, 6), (LANE, 5, 6), (LANE, 7, 5), (LANE, 0, 7), (LANE, 3, 5), (RETURN, 0, 0),
    (PART, 2, 3), (LANE, 4, 7), (LANE, 4, 8), (PART, 1, 3), (LANE, 8, 6), (LANE, 2, 6), (LANE, 8, 7),
    (SMALL, 4, 0), (PART, 0, 5), (LANE, 6, 5), (PART, 1, 4), (LANE, 3, 6), (PART, 2, 4), (LANE, 7, 6),
    (PART, 0, 6), (LANE, 6, 6), (LANE, 5, 7), (LANE, 7, 7), (LANE, 3, 7), (PART, 1, 5), (LANE, 6, 7),
    (PART, 0, 7), (PART, 2, 5), (LANE, 1, 7), (PART, 1, 6), (SMALL, 5, 0), (PART, 2, 6),
)


def fused(
    x_in, cot_in, groups, lengths, table_in, wqkv_in, qb_in, vb_in, wo_in, ob_in, g1_in, b1_in,
    wup_in, ub_in, wdn_in, db_in, g2_in, b2_in,
    lo_out, ig_out, full, qfull, vec_out,
    x_here, cot_here, xb, lowb, cotb, table, meta, meta_far, wqkv, wq, wo, wup, wdn, qb, vb, ob, g1, b1, ub, db, g2, b2,
    qt, q, k, vaug, vback, att, inv, sums, abuf, before, act, pre_grad, res, lob, igb, n1, n2, s1b, s2b, attn_grad,
    normed_low, ffn_grad, second, normed_grad, dob, dor, probs, dkt, dvt, dqkv, dxb, dxr0, dxr1, dxo,
    vecb, vecr,
    own, r0, r1, r3, qown, qr1, qr3,
    ssem, rsem, lsem,
):
    b_index, s_index = lax.axis_index("batch"), lax.axis_index("seq")
    x, z = s_index % 2, s_index // 2
    y, c = b_index // 2, b_index % 2
    me = 2 * x + c

    def dev(x, y, z, c):
        return (2 * y + c, 2 * z + x)

    core_dev = dev(x, y, z, 1 - c)
    x_dev = dev(1 - x, y, z, c)
    y_dev = dev(x, 1 - y, z, c)
    z_devs = [dev(x, y, (z + d) % 4, c) for d in (1, 2, 3)]
    z_near = z + 1 - 2 * (z % 2)
    near_dev, mirror_dev = dev(x, y, z_near, c), dev(x, y, 3 - z, c)
    crossing = c != z // 2

    pending = []

    def send(src, dst, s_number, r_number, device, when=None):
        copy = pltpu.make_async_remote_copy(
            src_ref=src, dst_ref=dst, send_sem=ssem.at[s_number], recv_sem=rsem.at[r_number],
            device_id=device, device_id_type=MESH,
        )
        if when is None:
            copy.start()
        else:
            pl.when(when)(copy.start)
        pending.append((copy, when))

    def arrived(dst, number):
        pltpu.make_async_remote_copy(
            src_ref=dst, dst_ref=dst, send_sem=ssem.at[number], recv_sem=rsem.at[number],
            device_id=core_dev, device_id_type=MESH,
        ).wait_recv()

    local_copies = []

    def fetch(src, dst):
        copy = pltpu.make_async_copy(src, dst, lsem.at[len(local_copies)])
        copy.start()
        local_copies.append(copy)
        return copy

    def land(copies):
        for copy in copies:
            copy.wait()
            local_copies[[entry is copy for entry in local_copies].index(True)] = None

    wait_table = fetch(table_in, table)
    wait_tokens = [fetch(x_in, x_here), fetch(cot_in, cot_here)]

    barrier = pltpu.get_barrier_semaphore()
    near = [core_dev, x_dev, y_dev] + z_devs
    for device in near:
        pl.semaphore_signal(barrier, inc=1, device_id=device, device_id_type=MESH)

    def greet(devices):
        for device in devices:
            pl.semaphore_signal(barrier, inc=1, device_id=device, device_id_type=MESH)
        pl.semaphore_wait(barrier, len(near) + len(devices))

    @pl.when(crossing)
    def _():
        greet([dev(xx, y, 2 * c + i, z // 2) for i in range(2) for xx in (x, 1 - x)])

    @pl.when(jnp.logical_not(crossing))
    def _():
        greet([dev(1 - x, y, z_near, c)])

    def half(ref, h):
        return ref.at[pl.ds(PIECE * h, PIECE)]

    def peer(i):
        return dev(x, y, 2 * c + i, z // 2)

    land(wait_tokens)
    first = jnp.where(crossing, 1 - c, z % 2)
    in_turn = [(i, h) for i in (first, 1 - first) for h in range(PIECES)]
    for i, h in in_turn:
        send(half(x_here.at[i], h), half(xb.at[x, z], h), NUM["x"] + PIECES * i + h, NUM["x"] + PIECES * (z % 2) + h,
             peer(i), when=2 * c + i != z)
    def send_cot():
        for i in (first, 1 - first):
            send(cot_here.at[i], cotb.at[x, z % 2], NUM["cot"] + i, NUM["cot"] + z % 2, peer(i), when=2 * c + i != z)
        for i in (first, 1 - first):
            send(cot_here.at[i], cotb.at[x, z % 2], NUM["cot_x"] + i, NUM["cot_x"] + z % 2,
                 dev(1 - x, y, 2 * c + i, z // 2))

    send_cot()
    @pl.when(jnp.logical_not(crossing))
    def _():
        xb[x, z] = x_here[z % 2]
        cotb[x, z % 2] = cot_here[z % 2]

    wait_qkv = [fetch(qb_in, qb), fetch(vb_in, vb)]
    for t in range(3):
        columns = pl.ds(pl.multiple_of(512 * t + 128 * me, 128), 128)
        wait_qkv.append(fetch(wqkv_in.at[:, columns], wq.at[:, pl.ds(128 * t, 128)]))
    wait_qkv.append(fetch(wqkv_in, wqkv))
    wait_ffn = [
        fetch(a, b)
        for a, b in ((wo_in, wo), (ob_in, ob), (g1_in, g1), (b1_in, b1), (wup_in, wup), (ub_in, ub),
                     (wdn_in, wdn), (db_in, db), (g2_in, g2), (b2_in, b2))
    ]

    land([wait_table])
    slot = z % 2
    group, length = groups[slot], lengths[slot]
    meta[0:1, :] = table[pl.ds(group, 1), :]
    meta[1:2, :] = jnp.full((1, 512), length.astype(f32))
    meta[2:3, :] = jnp.full((1, 512), group.astype(f32))
    meta[3:8, :] = jnp.zeros((5, 512), f32)
    send(meta, meta_far, NUM["meta"], NUM["meta"], core_dev)

    for i, h in in_turn:
        block = half(xb.at[x, 2 * c + i], h)

        @pl.when(2 * c + i != z)
        def _():
            arrived(block, NUM["x"] + PIECES * i + h)

        number = NUM["xn"] + PIECES * i + h
        send(block, block, number, number, x_dev)
        number = NUM["core_own"] + PIECES * i + h
        send(block, block, number, number, core_dev)

    land(wait_qkv)
    arrived(meta_far, NUM["meta"])
    facts = jnp.where(crossing, meta_far[...], meta[...])
    pair_row, length_row, group_row = facts[0:1, :], facts[1:2, :], facts[2:3, :]
    row_length = length_row[:, 0:1]

    lane = lax.broadcasted_iota(jnp.int32, (1, 128), 1)
    head_lanes = [lane < 64, lane >= 64]
    row = lax.broadcasted_iota(jnp.int32, (256, 1), 0)

    def rows_of(xx, cc):
        return pl.ds(pl.multiple_of(512 * xx + 256 * cc, 256), 256)

    def usable_rows(xx, cc):
        place = 128 * (4 * cc + xx) + row + jnp.where(row >= 128, 128, 0)
        return place.astype(f32) < row_length

    mine = pl.ds(pl.multiple_of(128 * me, 128), 128)
    all_lanes = lax.broadcasted_iota(jnp.int32, (1, 256), 1)
    first_head = all_lanes % 128 < 64

    def project(xx, cc, ours):
        low = (xb[xx, pl.ds(2 * cc, 2)].reshape(256, 512).astype(f32) + pair_row).astype(bf16)
        rows = rows_of(xx, cc)
        lowb[rows, :] = low
        usable = usable_rows(xx, cc)
        eighth = jnp.asarray(0.125, bf16)
        if ours:
            there = pl.ds(pl.multiple_of(256 * xx, 256), 256)
            qt[there, :] = (mm(low, wqkv[:, 0:512]) + qb[...]).astype(bf16) * eighth
            q[rows, :] = qt[there, mine]
        else:
            q[rows, :] = (mm(low, wq[:, 0:128]) + qb[:, mine]).astype(bf16) * eighth
        k[rows, :] = jnp.where(usable, mm(low, wqkv[:, 512:1024]), 0.0).astype(bf16)
        value = jnp.where(usable, mm(low, wqkv[:, 1024:1536]) + vb[...], 0.0).astype(bf16)
        one = jnp.broadcast_to(jnp.where(usable, 1.0, 0.0), (256, 128))
        for pair in range(4):
            vaug[pair, rows, 0:128] = value[:, 128 * pair : 128 * pair + 128]
            vaug[pair, rows, 128:256] = one.astype(bf16)
        own_value = vaug[me, rows, 0:128].astype(f32)
        for h in range(2):
            edge = 64 * (1 - h)
            extra = jnp.where((lane == edge) | (lane == edge + 1), one, 0.0)
            vback[h, rows, :] = jnp.where(head_lanes[h], own_value, extra).astype(bf16)

    def attend(q_rows, pair, h, keys, probs_rows):
        columns = pl.ds(pl.multiple_of(128 * pair, 128), 128)
        prob = jnp.exp(mm_nt(jnp.where(head_lanes[h], q_rows, 0), k[keys, columns])).astype(bf16)
        for at, rows in enumerate(probs_rows):
            probs[h, rows, keys] = prob[256 * at : 256 * at + 256]
        return mm(prob, vaug[pair, keys, :])

    def attended_of(parts, rows):
        both = jnp.where(first_head, parts[0], parts[1])
        inverse = 1.0 / both[:, 128:256]
        attended = both[:, 0:128] * inverse
        if rows is not None:
            att[rows, :] = attended
            inv[rows, :] = inverse
        return attended.astype(bf16)

    every = pl.ds(0, 1024)
    early = pl.ds(pl.multiple_of(512 * x, 512), 512)
    pairs = [(me + d) % 4 for d in range(4)]
    own_rows, far_rows = rows_of(x, c), rows_of(1 - x, c)
    own_half = pl.ds(pl.multiple_of(256 * x, 256), 256)
    far_half = pl.ds(pl.multiple_of(256 * (1 - x), 256), 256)

    def pair_columns(pair):
        return pl.ds(pl.multiple_of(128 * pair, 128), 128)

    def own_early(d, h):
        keep = [own_rows] if d == 0 else []
        sums[d, h, own_half, :] = attend(qt[own_half, pair_columns(pairs[d])], pairs[d], h, early, keep)

    def far_early(d, h):
        keep = [far_rows] if d == 0 else []
        sums[d, h, far_half, :] = attend(qt[far_half, pair_columns(pairs[d])], pairs[d], h, early, keep)

    def all_late(d, h, keys):
        keep = [rows_of(0, c), rows_of(1, c)] if d == 0 else []
        return sums[d, h] + attend(qt[:, pair_columns(pairs[d])], pairs[d], h, keys, keep)

    project(x, c, True)
    for i, h in in_turn:
        arrived(half(xb.at[x, 2 * (1 - c) + i], h), NUM["core_own"] + PIECES * i + h)
    project(x, 1 - c, False)
    for at, (i, h) in enumerate(in_turn):
        if at % (PIECES // 2) == 0:
            own_early(at // (PIECES // 2), 0)
            own_early(at // (PIECES // 2), 1)
        block = half(xb.at[1 - x, 2 * c + i], h)
        arrived(block, NUM["xn"] + PIECES * i + h)
        number = NUM["core_far"] + PIECES * i + h
        send(block, block, number, number, core_dev)
    project(1 - x, c, True)
    for d in range(4):
        for h in range(2):
            far_early(d, h)
            sums[d, h] = all_late(d, h, far_rows)
    for i, h in in_turn:
        arrived(half(xb.at[1 - x, 2 * (1 - c) + i], h), NUM["core_far"] + PIECES * i + h)
    project(1 - x, 1 - c, False)

    for d in range(4):
        parts = [all_late(d, h, rows_of(1 - x, 1 - c)) for h in range(2)]
        for xx in (0, 1):
            there = pl.ds(256 * xx, 256)
            abuf[there, pair_columns(pairs[d])] = attended_of(
                [part[256 * xx : 256 * xx + 256] for part in parts], rows_of(xx, c) if d == 0 else None
            )

    def other_probs(xx):
        rows = rows_of(xx, 1 - c)
        attended_of([attend(q[rows, :], me, h, every, [rows]) for h in range(2)], rows)

    def norm(hidden):
        centred = hidden - jnp.mean(hidden, axis=-1, keepdims=True)
        scale = lax.rsqrt(jnp.mean(centred * centred, axis=-1, keepdims=True) + eps_norm)
        return centred * scale, scale

    def norm_back(grad, normalized, scale, gain):
        e = grad * gain
        return scale * (
            e - jnp.mean(e, axis=-1, keepdims=True)
            - normalized * jnp.mean(e * normalized, axis=-1, keepdims=True)
        )

    def column_sum(values):
        return jnp.sum(values, axis=0, keepdims=True)

    once = jnp.where(x == 0, 1.0, 0.0)
    land(wait_ffn)
    for xx in (0, 1):
        there = pl.ds(256 * xx, 256)
        start_x = xb[xx, pl.ds(2 * c, 2)].reshape(256, 512).astype(f32) + pair_row
        normalized, s1 = norm(start_x + (mm(abuf[there, :], wo[...]) + ob[...]))
        s1b[there, :] = jnp.broadcast_to(s1, (256, 128))
        n1[there, :] = normalized
        normed = normalized * g1[...] + b1[...]
        normed_low[there, :] = normed.astype(bf16)
        normed_grad[there, :] = normed + start_x
    for j in range(4):
        cols = pl.ds(512 * j, 512)
        pre = mm(normed_low[...], wup[:, cols]) + ub[:, cols]
        before[:, cols] = pre
        act_low = (pre * (0.5 * (1.0 + lax.erf(pre * 0.7071067811865476)))).astype(bf16)
        act[:, cols] = act_low
        term = mm(act_low, wdn[cols, :])
        second[...] = term if j == 0 else second[...] + term
    for xx in (0, 1):
        there = pl.ds(256 * xx, 256)
        normalized, s2 = norm((second[there, :] + db[...]) + normed_grad[there, :])
        n2[there, :] = normalized
        s2b[there, :] = jnp.broadcast_to(s2, (256, 128))
    def give_back(block, out, name):
        for i in (0, 1):
            send(block.at[i], out.at[z % 2], NUM[name] + i, NUM[name] + z % 2, peer(i), when=2 * c + i != z)

        @pl.when(jnp.logical_not(crossing))
        def _():
            out[z % 2] = block[z % 2]

    def layer_back():
        lob[...] = (n2[own_half, :] * g2[...] + b2[...]).astype(bf16).reshape(2, 128, 512)
        give_back(lob, lo_out, "lo")

    for i in (0, 1):
        @pl.when(2 * c + i != z)
        def _():
            arrived(cotb.at[x, i], NUM["cot"] + i)
    for turn, (xx, there) in enumerate(((x, own_half), (1 - x, far_half))):
        if turn == 1:
            for i in (0, 1):
                arrived(cotb.at[1 - x, i], NUM["cot_x"] + i)
        g = cotb[xx].reshape(256, 512).astype(f32)
        normalized = n2[there, :]
        grad = norm_back(g, normalized, s2b[there, 0:1], g2[...])
        second[there, :] = grad
        low = grad.astype(bf16)
        ffn_grad[there, :] = low

    def number(n, step):
        return NUM["lane"] + 12 * n + step

    def add_up(target, parts, result=None):
        value = target[...].astype(f32)
        for part in parts:
            value = value + part[...].astype(f32)
        (target if result is None else result)[...] = value.astype(bf16)

    def travel(mine, r1, r3, whole, number_of, scatter, order):
        stages = []

        def scatter_stages(axis, last):
            def part(zz):
                return mine.at[y, zz] if last else mine.at[:, zz]

            def slot(d):
                return r3.at[d, 0] if last else r3.at[d]

            result = whole.at[x, c, y, z] if last else None
            if axis == "y":
                box = r1.at[0] if last else r1

                def start():
                    send(mine.at[1 - y, z] if last else mine.at[1 - y], box, number_of(1), number_of(1), y_dev)

                def finish():
                    arrived(box, number_of(1))
                    add_up(mine.at[y, z] if last else mine.at[y], [box], result)

                stages.append((start, finish))
            elif axis == "z":
                def start():
                    for d in (1, 2, 3):
                        send(part((z + d) % 4), slot(3 - d), number_of(1 + d), number_of(5 - d), z_devs[d - 1])

                def finish():
                    for d in (1, 2, 3):
                        arrived(slot(d - 1), number_of(1 + d))
                    add_up(part(z), [slot(d) for d in range(3)], result)

                stages.append((start, finish))
            else:
                def start():
                    send(part(3 - z_near), slot(0), number_of(2), number_of(2), near_dev)

                def finish():
                    arrived(slot(0), number_of(2))
                    add_up(part(3 - z), [slot(0)])

                def start_two():
                    send(part(3 - z), slot(1), number_of(3), number_of(3), mirror_dev)
                    send(part(z_near), slot(2), number_of(4), number_of(4), near_dev)

                def finish_two():
                    arrived(slot(1), number_of(3))
                    arrived(slot(2), number_of(4))
                    add_up(part(z), [slot(1), slot(2)], result)

                stages.append((start, finish))
                stages.append((start_two, finish_two))

        def region(done, **other):
            place = dict(x=x, y=y, z=z) | other
            at = {axis: slice(None) if axis in done else place[axis] for axis in "xyz"}
            return whole.at[at["x"], c, at["y"], at["z"]]

        def gather_stages(axis, done):
            part = region(done)
            if axis == "z":
                def start():
                    for d in (1, 2, 3):
                        send(part, part, number_of(4 + d), number_of(8 - d), z_devs[d - 1])

                def finish():
                    for d in (1, 2, 3):
                        arrived(region(done, z=(z + d) % 4), number_of(4 + d))

                stages.append((start, finish))
            elif axis == "w":
                def start():
                    send(part, part, number_of(6), number_of(6), mirror_dev)
                    send(part, part, number_of(5), number_of(5), near_dev)

                def finish():
                    arrived(region(done, z=z_near), number_of(5))
                    arrived(region(done, z=3 - z), number_of(6))

                def start_two():
                    passed = region(done, z=3 - z)
                    send(passed, passed, number_of(7), number_of(7), near_dev)

                def finish_two():
                    arrived(region(done, z=3 - z_near), number_of(7))

                stages.append((start, finish))
                stages.append((start_two, finish_two))
            else:
                at, device, there = {"x": (9, x_dev, dict(x=1 - x)), "y": (8, y_dev, dict(y=1 - y))}[axis]

                def start():
                    send(part, part, number_of(at), number_of(at), device)

                def finish():
                    arrived(region(done, **there), number_of(at))

                stages.append((start, finish))

        scatter_stages(scatter[0], False)
        scatter_stages(scatter[1], True)
        for at, axis in enumerate(order):
            gather_stages(axis, order[:at].replace("w", "z"))

        def start():
            send(whole.at[:, c], whole.at[:, c], number_of(10), number_of(10), core_dev)

        def finish():
            arrived(whole.at[:, 1 - c], number_of(10))

        stages.append((start, finish))
        return stages

    lane_stages = [
        travel(own.at[n, c], r1.at[n], r3.at[n], full.at[n], functools.partial(number, n), SCATTER[n], GATHER[n])
        for n in range(LANES)
    ]

    def lane_step(n, step):
        if step == 0:
            arrived(r0.at[n], number(n, 0))
            add_up(own.at[n, c], [r0.at[n]])
        else:
            lane_stages[n][step - 1][1]()
        if step < len(lane_stages[n]):
            lane_stages[n][step][0]()

    own_columns = pl.ds(pl.multiple_of(256 * x, 256), 256)

    def lane_fill(n):
        if n < 4:
            value = mm_tn(act[:, pl.ds(pl.multiple_of(512 * n + 256 * x, 256), 256)], ffn_grad[...])
        elif n < 8:
            value = mm_tn(normed_low[:, own_columns], pre_grad[:, pl.ds(512 * (n - 4), 512)])
        else:
            value = mm_tn(abuf[:, own_columns], attn_grad[...])
        own[n] = value.astype(bf16).reshape(2, 2, 4, 16, 512)
        send(own.at[n, 1 - c], r0.at[n], number(n, 0), number(n, 0), core_dev)

    def ffn_back(j):
        cols = pl.ds(512 * j, 512)
        pre = before[:, cols]
        cdf = 0.5 * (1.0 + lax.erf(pre * 0.7071067811865476))
        slope = cdf + pre * (jnp.exp(-0.5 * pre * pre) * 0.3989422804014327)
        grad = (mm_nt(ffn_grad[...], wdn[cols, :]) * slope).astype(bf16)
        pre_grad[:, cols] = grad
        vecb[16 + j : 17 + j, :] = column_sum(grad.astype(f32)) * once
        normed_grad[...] = (second if j == 0 else normed_grad)[...] + mm_nt(grad, wup[:, cols])

    def first_back():
        for xx in (0, 1):
            there = pl.ds(256 * xx, 256)
            grad, normalized = normed_grad[there, :], n1[there, :]
            first_grad = norm_back(grad, normalized, s1b[there, 0:1], g1[...])
            low = first_grad.astype(bf16)
            attn_grad[there, :] = low
            second[there, :] = second[there, :] + first_grad
        res[...] = second[own_half, :]
        low = attn_grad[...]

        def heads(cc):
            return pl.ds(pl.multiple_of(128 * (2 * x + cc), 128), 128)

        dob[...] = mm_nt(low, wo[heads(1 - c), :]).astype(bf16)
        send(dob, dor.at[c], NUM["do"], NUM["do"], core_dev)
        dor[c] = mm_nt(low, wo[heads(c), :]).astype(bf16)

    def norm_sums(which):
        if which == 0:
            grad, normalized, low, at = cotb[...].reshape(512, 512).astype(f32), n2[...], ffn_grad[...], 13
        else:
            grad, normalized, low, at = normed_grad[...], n1[...], attn_grad[...], 10
        vecb[at : at + 1, :] = column_sum(low.astype(f32)) * once
        vecb[at + 1 : at + 2, :] = column_sum(grad * normalized) * once
        vecb[at + 2 : at + 3, :] = column_sum(grad) * once

    turns = ((0, c), (1, c), (0, 1 - c), (1, 1 - c))

    def attention_back(turn):
        xx, cc = turns[turn]
        if turn == 2:
            arrived(dor.at[cc], NUM["do"])
        rows = rows_of(xx, cc)
        d_out = dor[cc, 256 * xx : 256 * xx + 256, :].astype(f32)
        numer_grad = d_out * inv[rows, :]
        product = numer_grad.astype(bf16).astype(f32) * att[rows, :]
        q_rows = q[rows, :]
        dq_rows = jnp.zeros((256, 128), f32)
        for h in range(2):
            total = -jnp.sum(jnp.where(head_lanes[h], product, 0.0), axis=1, keepdims=True)
            high = total.astype(bf16).astype(f32)
            edge = 64 * (1 - h)
            rest = jnp.where(lane == edge, high, jnp.where(lane == edge + 1, total - high, 0.0))
            grad_low = jnp.where(head_lanes[h], numer_grad, rest).astype(bf16)
            prob = probs[h, rows, :]
            score_grad = (prob.astype(f32) * mm_nt(grad_low, vback[h])).astype(bf16)
            dq_rows = dq_rows + jnp.where(head_lanes[h], mm(score_grad, k[:, mine]), 0.0)
            part = slice(64 * h, 64 * h + 64)
            dk_part = mm(jnp.transpose(q_rows)[part, :], score_grad)
            dv_part = mm(jnp.transpose(grad_low)[part, :], prob)
            dkt[part, :] = dk_part if turn == 0 else dkt[part, :] + dk_part
            dvt[part, :] = dv_part if turn == 0 else dvt[part, :] + dv_part
        dqkv[rows, 0:128] = (dq_rows * 0.125).astype(bf16)

    def projection_grads():
        for xx in (0, 1):
            for cc in (0, 1):
                rows = pl.ds(512 * xx + 256 * cc, 256)
                dqkv[rows, 128:256] = jnp.transpose(dkt[:, rows]).astype(bf16)
                dqkv[rows, 256:384] = jnp.where(usable_rows(xx, cc), jnp.transpose(dvt[:, rows]), 0.0).astype(bf16)

    def qnumber(t, step):
        return NUM["qkv"] + 12 * t + step

    part_stages = [
        travel(qown.at[t], qr1.at[t], qr3.at[t], qfull.at[t], functools.partial(qnumber, t), QSCATTER[t], QGATHER[t])
        for t in range(3)
    ]

    def projection_weights(t):
        value = mm_tn(lowb[...], dqkv[:, 128 * t : 128 * t + 128])
        qown[t] = value.astype(bf16).reshape(2, 4, 64, 128)
        part_stages[t][0][0]()

    def projection_step(t, step):
        part_stages[t][step][1]()
        if step + 1 < len(part_stages[t]):
            part_stages[t][step + 1][0]()

    def input_back(step):
        xx, cc = ((1 - x, 1 - c), (x, 1 - c), (1 - x, c), (x, c))[step]
        block = mm_nt(dqkv[rows_of(xx, cc), :], wq[...])
        vecb[20:21, :] = column_sum(block) if step == 0 else vecb[20:21, :] + column_sum(block)
        if step < 2:
            dxb[step] = block.astype(bf16)
            send(dxb.at[step], dxr0.at[step], NUM["dx_core"] + step, NUM["dx_core"] + step, core_dev)
        elif step == 2:
            arrived(dxr0.at[0], NUM["dx_core"])
            dxb[2] = (block + dxr0[0].astype(f32)).astype(bf16)
            send(dxb.at[2], dxr1, NUM["dx_x"], NUM["dx_x"], x_dev)
        else:
            arrived(dxr0.at[1], NUM["dx_core"] + 1)
            dxo[...] = block + dxr0[1].astype(f32) + res[...]

    def input_out():
        arrived(dxr1, NUM["dx_x"])
        igb[...] = (dxo[...] + dxr1[...].astype(f32)).astype(bf16).reshape(2, 128, 512)
        give_back(igb, ig_out, "ig")

    def vectors(step):
        if step == 0:
            group_iota = lax.broadcasted_iota(jnp.int32, (8, 512), 0).astype(f32)
            column_total = vecb[20:21, :] + column_sum(res[...])
            vecb[0:8, :] = jnp.where(group_iota == group_row, column_total, 0.0)
            vecb[8:10, :] = jnp.zeros((2, 512), f32)
            vecb[8:9, mine] = column_sum(dqkv[:, 0:128].astype(f32))
            vecb[9:10, mine] = column_sum(dqkv[:, 256:384].astype(f32))
            vecb[20:24, :] = jnp.zeros((4, 512), f32)
            send(vecb, vecr.at[0], NUM["vec"], NUM["vec"], core_dev)
        else:
            level = step - 1
            arrived(vecr.at[level], NUM["vec"] + level)
            value = (vecb if level == 0 else vecr.at[4 + level])[...] + vecr[level]
            if level < 4:
                vecr[5 + level] = value
                send(vecr.at[5 + level], vecr.at[level + 1], NUM["vec"] + level + 1, NUM["vec"] + level + 1,
                     (x_dev, y_dev, near_dev, mirror_dev)[level])
            else:
                vec_out[...] = value

    tasks = {(NORM, 0, 0): first_back, (SPLIT, 0, 0): projection_grads, (RETURN, 0, 0): input_out, (RETURN, 1, 0): layer_back}
    for kind, task, count in (
        (FILL, lane_fill, LANES), (FFN, ffn_back, 4), (ATTN, attention_back, 4), (PROBS, other_probs, 2), (WEIGHT, projection_weights, 3),
        (INPUT, input_back, 4), (SMALL, vectors, 6), (SUMS, norm_sums, 2),
    ):
        for at in range(count):
            tasks[kind, at, 0] = functools.partial(task, at)
    for n in range(LANES):
        for step in range(len(lane_stages[n]) + 1):
            tasks[LANE, n, step] = functools.partial(lane_step, n, step)
    for t in range(3):
        for step in range(len(part_stages[t])):
            tasks[PART, t, step] = functools.partial(projection_step, t, step)
    for at, entry in enumerate(ORDER):
        tasks.pop(entry)()
    assert not tasks

    for name, out in (("lo", lo_out), ("ig", ig_out)):
        for i in (0, 1):
            @pl.when(2 * c + i != z)
            def _():
                arrived(out.at[i], NUM[name] + i)
    land([copy for copy in local_copies if copy is not None])
    for copy, when in pending:
        if when is None:
            copy.wait_send()
        else:
            pl.when(when)(copy.wait_send)


VECTOR_ROWS = (8, 9, 10, 11, 12, 13, 14, 15)


def finish(lo, ig, full, qfull, vec, *refs):
    lo_out, ig_out, down_out, up_out, out_out, qkv_out, pair_out = refs[:7]
    vector_outs, up_bias_out = refs[7:15], refs[15]
    lo_wide, ig_wide, full_wide, qkv_wide, rows, up_bias, sems = *refs[16:20], refs[20:28], refs[28], refs[29]
    writes = []

    def write(src, dst):
        made = pltpu.make_async_copy(src, dst, sems.at[len(writes)])
        made.start()
        writes.append(made)

    for n in range(LANES):
        for half in range(2):
            at = pl.ds(256 * half, 256)
            full_wide[n, at, :] = full[n, half].reshape(256, 512).astype(f32)
            if n < 4:
                write(full_wide.at[n, at], down_out.at[pl.ds(512 * n + 256 * half, 256)])
            elif n < 8:
                write(full_wide.at[n, at], up_out.at[at, pl.ds(512 * (n - 4), 512)])
            else:
                write(full_wide.at[n, at], out_out.at[at])
    for t in range(3):
        for h in range(4):
            columns = pl.ds(512 * t + 128 * h, 128)
            qkv_wide[:, columns] = qfull[t, h // 2, h % 2].reshape(512, 128).astype(f32)
        columns = pl.ds(512 * t, 512)
        write(qkv_wide.at[:, columns], qkv_out.at[:, columns])
    for block, wide, out in ((lo, lo_wide, lo_out), (ig, ig_wide, ig_out)):
        wide[...] = block[...].astype(f32)
        write(wide, out)
    write(vec.at[pl.ds(0, 8)], pair_out)
    for at, row, out in zip(VECTOR_ROWS, rows, vector_outs):
        row[...] = vec[at : at + 1, :]
        write(row, out)
    for j in range(4):
        up_bias[:, 512 * j : 512 * j + 512] = vec[16 + j : 17 + j, :]
    write(up_bias, up_bias_out)
    for made in writes:
        made.wait()


def pair_plan(mesh):
    return dict(mesh.shape) == {"batch": 4, "seq": 8}


def fused_local(
    block_input, cotangent, groups, lengths, pair_table, qkv_weight, q_bias, v_bias, out_weight,
    out_bias, norm1_gain, norm1_bias, up_weight, up_bias, down_weight, down_bias, norm2_gain, norm2_bias,
):
    any_spec, smem = pl.BlockSpec(memory_space=pl.ANY), pl.BlockSpec(memory_space=pltpu.SMEM)

    def row(vector):
        return vector[None, :]

    operands = (
        block_input, cotangent, groups, lengths, pair_table, qkv_weight, row(q_bias), row(v_bias),
        out_weight, row(out_bias), row(norm1_gain), row(norm1_bias), up_weight, row(up_bias),
        down_weight, row(down_bias), row(norm2_gain), row(norm2_bias),
    )
    in_specs = [smem if i in (2, 3) else any_spec for i in range(len(operands))]
    vmem = pl.BlockSpec(memory_space=pltpu.VMEM)
    out_shape = [
        pltpu.VMEM(shape, dtype)
        for shape, dtype in (
            ((2, 128, 512), bf16), ((2, 128, 512), bf16), ((LANES, 2, 2, 2, 4, 16, 512), bf16),
            ((3, 2, 2, 2, 4, 64, 128), bf16), ((24, 512), f32),
        )
    ]
    scratch = [
        pltpu.VMEM(shape, dtype)
        for shape, dtype in (
            ((2, 128, 512), bf16), ((2, 128, 512), bf16),
            ((2, 4, 128, 512), bf16), ((1024, 512), bf16), ((2, 2, 128, 512), bf16),
            ((8, 512), f32), ((8, 512), f32), ((8, 512), f32),
            ((512, 1536), bf16), ((512, 384), bf16), ((512, 512), bf16), ((512, 2048), bf16), ((2048, 512), bf16),
            ((1, 512), f32), ((1, 512), f32), ((1, 512), f32), ((1, 512), f32), ((1, 512), f32),
            ((1, 2048), f32), ((1, 512), f32), ((1, 512), f32), ((1, 512), f32),
            ((512, 512), bf16), ((1024, 128), bf16), ((1024, 512), bf16),
            ((4, 1024, 256), bf16), ((2, 1024, 128), bf16),
            ((1024, 128), f32), ((1024, 128), f32),
            ((4, 2, 512, 256), f32), ((512, 512), bf16),
            ((512, 2048), f32), ((512, 2048), bf16), ((512, 2048), bf16),
            ((256, 512), f32), ((2, 128, 512), bf16), ((2, 128, 512), bf16),
            ((512, 512), f32), ((512, 512), f32), ((512, 128), f32), ((512, 128), f32),
            ((512, 512), bf16),
            ((512, 512), bf16), ((512, 512), bf16), ((512, 512), f32), ((512, 512), f32),
            ((512, 128), bf16), ((2, 512, 128), bf16), ((2, 1024, 1024), bf16),
            ((128, 1024), f32), ((128, 1024), f32), ((1024, 384), bf16),
            ((3, 256, 512), bf16), ((2, 256, 512), bf16), ((256, 512), bf16), ((256, 512), f32),
            ((24, 512), f32), ((9, 24, 512), f32),
            ((LANES, 2, 2, 4, 16, 512), bf16), ((LANES, 2, 4, 16, 512), bf16), ((LANES, 4, 16, 512), bf16),
            ((LANES, 3, 2, 16, 512), bf16),
            ((3, 2, 4, 64, 128), bf16), ((3, 4, 64, 128), bf16), ((3, 3, 2, 64, 128), bf16),
        )
    ] + [
        pltpu.SemaphoreType.DMA((NUM.count,)),
        pltpu.SemaphoreType.DMA((NUM.count,)),
        pltpu.SemaphoreType.DMA((LOCAL,)),
    ]
    results = pl.pallas_call(
        fused,
        out_shape=out_shape,
        in_specs=in_specs,
        out_specs=[vmem] * len(out_shape),
        scratch_shapes=scratch,
        compiler_params=pltpu.CompilerParams(
            collective_id=0, has_side_effects=True, vmem_limit_bytes=54 * 2**20
        ),
    )(*operands)
    shapes = [(2, 128, 512)] * 2 + [(2048, 512), (512, 2048), (512, 512), (512, 1536), (8, 512)]
    shapes += [(1, 512)] * 8 + [(1, 2048)]
    scratch_sizes = [(2, 128, 512)] * 2 + [(LANES, 512, 512), (512, 1536)] + [(1, 512)] * 8 + [(1, 2048)]
    results = pl.pallas_call(
        finish,
        out_shape=[jax.ShapeDtypeStruct(shape, f32) for shape in shapes],
        in_specs=[vmem] * 5,
        out_specs=[any_spec] * len(shapes),
        scratch_shapes=[pltpu.VMEM(shape, f32) for shape in scratch_sizes] + [pltpu.SemaphoreType.DMA((40,))],
        compiler_params=pltpu.CompilerParams(vmem_limit_bytes=40 * 2**20),
    )(*results)
    layer_out, input_grad, down_grad, up_grad, out_grad, qkv_grad, pair_grad = results[:7]
    q_grad, v_grad, ob_grad, g1_grad, b1_grad, db_grad, g2_grad, b2_grad = [r.reshape(512) for r in results[7:15]]
    return (
        layer_out, input_grad, pair_grad, qkv_grad, q_grad, v_grad,
        out_grad, ob_grad, g1_grad, b1_grad, up_grad, results[15].reshape(2048), down_grad, db_grad, g2_grad, b2_grad,
    )


def solution(mesh):
    in_specs = (
        P("batch", "seq", None),
        P("batch", "seq", None),
        P("batch"),
        P("batch"),
        P(),
        P(),
        P(),
        P(),
        P(),
        P(),
        P(),
        P(),
        P(),
        P(),
        P(),
        P(),
        P(),
        P(),
    )
    out_specs = (
        P("batch", "seq", None),
        P("batch", "seq", None),
        P(),
        P(),
        P(),
        P(),
        P(),
        P(),
        P(),
        P(),
        P(),
        P(),
        P(),
        P(),
        P(),
        P(),
    )
    return jax.shard_map(fused_local if pair_plan(mesh) else local, mesh=mesh, in_specs=in_specs, out_specs=out_specs, check_vma=False)
```

```python
import functools

import jax
import jax.numpy as jnp
from jax import lax
from jax.experimental import pallas as pl
from jax.experimental.pallas import tpu as pltpu
from jax.sharding import PartitionSpec as P

HEADS = 8


highest = lax.Precision.HIGHEST
eps_norm = 1e-05


def layer_norm(hidden, norm_gain, norm_shift):
    row_mean = jnp.mean(hidden, axis=-1, keepdims=True)
    centred = hidden - row_mean
    spread = jnp.mean(centred * centred, axis=-1, keepdims=True)
    return centred * lax.rsqrt(spread + eps_norm) * norm_gain + norm_shift


def exact_gelu(pre_act):
    return jax.nn.gelu(pre_act, approximate=False)


def block_size():
    return 512


def to_heads(flat_rows, head_count):
    return flat_rows.reshape(
        flat_rows.shape[0], flat_rows.shape[1], head_count, flat_rows.shape[2] // head_count
    )


def masked_exp(query_block, key_block, key_first, row_lengths, score_scale):
    scores = (
        jnp.einsum("rihd,rjhd->rhij", query_block, key_block, preferred_element_type=jnp.float32)
        * score_scale
    )
    places = key_first + jnp.arange(key_block.shape[1], dtype=jnp.int32)
    usable = places[None, :] < row_lengths[:, None]
    return jnp.where(usable[:, None, None, :], jnp.exp(scores), 0.0)


def forward_piece(
    running, key_piece, value_piece, query_heads, row_lengths, score_scale, head_count
):
    piece_len = key_piece.shape[1]
    block_len = block_size()
    key_all = to_heads(key_piece, head_count)
    value_all = to_heads(value_piece, head_count)

    def forward_one_block(block_index, partial_sums):
        numerator, denominator = partial_sums
        block_first = block_index * block_len
        key_block = lax.dynamic_slice_in_dim(key_all, block_first, block_len, 1)
        value_block = lax.dynamic_slice_in_dim(value_all, block_first, block_len, 1)
        exp_scores = masked_exp(query_heads, key_block, block_first, row_lengths, score_scale)
        denominator = denominator + jnp.sum(exp_scores, axis=-1)
        numerator = numerator + jnp.einsum(
            "rhij,rjhd->rihd",
            exp_scores.astype(jnp.bfloat16),
            value_block,
            preferred_element_type=jnp.float32,
        )
        return (numerator, denominator)

    return lax.fori_loop(0, piece_len // block_len, forward_one_block, running)


def key_side(
    running,
    query_piece,
    grad_piece,
    total_piece,
    key_heads,
    value_heads,
    key_first,
    row_lengths,
    score_scale,
    head_count,
):
    piece_len = query_piece.shape[1]
    block_len = block_size()
    query_all = to_heads(query_piece.astype(jnp.bfloat16), head_count)
    grad_all = to_heads(grad_piece, head_count)
    value_wide = value_heads.astype(jnp.float32)

    def key_one_block(block_index, partial_grads):
        key_grad, value_grad = partial_grads
        block_first = block_index * block_len
        query_block = lax.dynamic_slice_in_dim(query_all, block_first, block_len, 1)
        grad_block = lax.dynamic_slice_in_dim(grad_all, block_first, block_len, 1)
        total_block = lax.dynamic_slice_in_dim(total_piece, block_first, block_len, 1)
        exp_scores = masked_exp(query_block, key_heads, key_first, row_lengths, score_scale)
        prob_grad = jnp.einsum(
            "rihd,rjhd->rhij",
            grad_block,
            value_wide,
            precision=highest,
            preferred_element_type=jnp.float32,
        )
        shift_grad = jnp.transpose(total_block, (0, 2, 1))[..., None]
        score_grad = (exp_scores * (prob_grad + shift_grad)).astype(jnp.bfloat16)
        key_grad = (
            key_grad
            + jnp.einsum(
                "rhij,rihd->rjhd", score_grad, query_block, preferred_element_type=jnp.float32
            )
            * score_scale
        )
        exp_low = exp_scores.astype(jnp.bfloat16).astype(jnp.float32)
        value_grad = value_grad + jnp.einsum(
            "rhij,rihd->rjhd",
            exp_low,
            grad_block,
            precision=highest,
            preferred_element_type=jnp.float32,
        )
        return (key_grad, value_grad)

    return lax.fori_loop(0, piece_len // block_len, key_one_block, running)


def query_side(
    running,
    key_piece,
    value_piece,
    query_heads,
    grad_heads,
    total_here,
    row_lengths,
    score_scale,
    head_count,
):
    piece_len = key_piece.shape[1]
    block_len = block_size()
    key_all = to_heads(key_piece, head_count)
    value_all = to_heads(value_piece, head_count)

    def query_one_block(block_index, query_grad):
        block_first = block_index * block_len
        key_block = lax.dynamic_slice_in_dim(key_all, block_first, block_len, 1)
        value_block = lax.dynamic_slice_in_dim(value_all, block_first, block_len, 1)
        exp_scores = masked_exp(query_heads, key_block, block_first, row_lengths, score_scale)
        prob_grad = jnp.einsum(
            "rihd,rjhd->rhij",
            grad_heads,
            value_block.astype(jnp.float32),
            precision=highest,
            preferred_element_type=jnp.float32,
        )
        score_grad = (exp_scores * (prob_grad + total_here[..., None])).astype(jnp.bfloat16)
        return (
            query_grad
            + jnp.einsum(
                "rhij,rjhd->rihd", score_grad, key_block, preferred_element_type=jnp.float32
            )
            * score_scale
        )

    return lax.fori_loop(0, piece_len // block_len, query_one_block, running)


def local(
    block_input,
    cotangent,
    groups,
    lengths,
    pair_table,
    qkv_weight,
    q_bias,
    v_bias,
    out_weight,
    out_bias,
    norm1_gain,
    norm1_bias,
    up_weight,
    up_bias,
    down_weight,
    down_bias,
    norm2_gain,
    norm2_bias,
):
    row_count, shard_len, model_width = block_input.shape
    head_count = HEADS
    head_size = model_width // head_count
    score_scale = head_size ** (-0.5)
    key_offset = lax.axis_index("seq") * shard_len
    pair_onehot = (
        groups[:, None] == jnp.arange(pair_table.shape[0], dtype=jnp.int32)[None, :]
    ).astype(jnp.float32)
    lifted = jnp.dot(pair_onehot, pair_table, precision=highest)
    start_x = block_input.astype(jnp.float32) + lifted[:, None, :]
    lowered = start_x.astype(jnp.bfloat16)
    projected = jnp.einsum("rtd,de->rte", lowered, qkv_weight, preferred_element_type=jnp.float32)
    query_rows = (projected[:, :, :model_width] + q_bias).astype(jnp.bfloat16)
    key_rows = projected[:, :, model_width : 2 * model_width].astype(jnp.bfloat16)
    value_rows = (projected[:, :, 2 * model_width :] + v_bias).astype(jnp.bfloat16)
    query_heads = to_heads(query_rows, head_count)
    key_heads = to_heads(key_rows, head_count)
    value_heads = to_heads(value_rows, head_count)
    zero_heads = jnp.zeros((row_count, shard_len, head_count, head_size), jnp.float32)
    zero_totals = jnp.zeros((row_count, head_count, shard_len), jnp.float32)
    incoming = (
        lax.all_gather(key_rows, "seq", axis=1, tiled=True),
        lax.all_gather(value_rows, "seq", axis=1, tiled=True),
    )
    numerator, denominator = forward_piece(
        (zero_heads, zero_totals),
        incoming[0],
        incoming[1],
        query_heads,
        lengths,
        score_scale,
        head_count,
    )
    inverse = 1.0 / jnp.transpose(denominator, (0, 2, 1))[..., None]
    attended = numerator * inverse
    attended_low = attended.reshape(row_count, shard_len, model_width).astype(jnp.bfloat16)
    attn_out = (
        jnp.einsum("rtd,de->rte", attended_low, out_weight, preferred_element_type=jnp.float32)
        + out_bias
    )
    normed, norm1_back = jax.vjp(layer_norm, start_x + attn_out, norm1_gain, norm1_bias)
    normed_low = normed.astype(jnp.bfloat16)
    pre_act = (
        jnp.einsum("rtd,df->rtf", normed_low, up_weight, preferred_element_type=jnp.float32)
        + up_bias
    )
    activated, gelu_back = jax.vjp(exact_gelu, pre_act)
    activated_low = activated.astype(jnp.bfloat16)
    ffn_out = (
        jnp.einsum("rtf,fd->rtd", activated_low, down_weight, preferred_element_type=jnp.float32)
        + down_bias
    )
    layer_out, norm2_back = jax.vjp(layer_norm, ffn_out + normed + start_x, norm2_gain, norm2_bias)
    second_grad, norm2_gain_grad, norm2_bias_grad = norm2_back(cotangent.astype(jnp.float32))
    ffn_grad = second_grad.astype(jnp.bfloat16)
    down_bias_grad = jnp.sum(ffn_grad.astype(jnp.float32), axis=(0, 1))
    down_weight_grad = jnp.einsum(
        "rtf,rtd->fd", activated_low, ffn_grad, preferred_element_type=jnp.float32
    )
    act_grad = jnp.einsum("rtd,fd->rtf", ffn_grad, down_weight, preferred_element_type=jnp.float32)
    pre_grad = gelu_back(act_grad)[0].astype(jnp.bfloat16)
    up_bias_grad = jnp.sum(pre_grad.astype(jnp.float32), axis=(0, 1))
    up_weight_grad = jnp.einsum(
        "rtd,rtf->df", normed_low, pre_grad, preferred_element_type=jnp.float32
    )
    normed_grad = second_grad + jnp.einsum(
        "rtf,df->rtd", pre_grad, up_weight, preferred_element_type=jnp.float32
    )
    first_grad, norm1_gain_grad, norm1_bias_grad = norm1_back(normed_grad)
    attn_grad = first_grad.astype(jnp.bfloat16)
    out_bias_grad = jnp.sum(attn_grad.astype(jnp.float32), axis=(0, 1))
    out_weight_grad = jnp.einsum(
        "rtd,rte->de", attended_low, attn_grad, preferred_element_type=jnp.float32
    )
    attended_grad = to_heads(
        jnp.einsum("rte,de->rtd", attn_grad, out_weight, preferred_element_type=jnp.float32),
        head_count,
    )
    numer_grad = attended_grad * inverse
    total_grad = -jnp.sum(attended_grad * attended, axis=-1) * inverse[..., 0]
    grad_rows = numer_grad.reshape(row_count, shard_len, model_width)
    total_here = jnp.transpose(total_grad, (0, 2, 1))
    incoming = (
        lax.all_gather(query_rows.astype(jnp.float32), "seq", axis=1, tiled=True),
        lax.all_gather(grad_rows, "seq", axis=1, tiled=True),
        lax.all_gather(total_grad, "seq", axis=1, tiled=True),
    )
    key_grad, value_grad = key_side(
        (zero_heads, zero_heads),
        incoming[0],
        incoming[1],
        incoming[2],
        key_heads,
        value_heads,
        key_offset,
        lengths,
        score_scale,
        head_count,
    )
    incoming = (
        lax.all_gather(key_rows, "seq", axis=1, tiled=True),
        lax.all_gather(value_rows, "seq", axis=1, tiled=True),
    )
    query_grad = query_side(
        zero_heads,
        incoming[0],
        incoming[1],
        query_heads,
        numer_grad,
        total_here,
        lengths,
        score_scale,
        head_count,
    )
    flat_shape = (row_count, shard_len, model_width)
    query_low = query_grad.reshape(flat_shape).astype(jnp.bfloat16)
    key_low = key_grad.reshape(flat_shape).astype(jnp.bfloat16)
    value_low = value_grad.reshape(flat_shape).astype(jnp.bfloat16)
    qkv_grad = jnp.concatenate([query_low, key_low, value_low], axis=-1)
    qkv_weight_grad = jnp.einsum(
        "rtd,rte->de", lowered, qkv_grad, preferred_element_type=jnp.float32
    )
    q_bias_grad = jnp.sum(query_low.astype(jnp.float32), axis=(0, 1))
    v_bias_grad = jnp.sum(value_low.astype(jnp.float32), axis=(0, 1))
    input_grad = (
        jnp.einsum("rte,de->rtd", qkv_grad, qkv_weight, preferred_element_type=jnp.float32)
        + first_grad
        + second_grad
    )
    pair_table_grad = jnp.dot(
        jnp.transpose(pair_onehot), jnp.sum(input_grad, axis=1), precision=highest
    )
    summed = lax.psum(
        (
            pair_table_grad,
            qkv_weight_grad,
            q_bias_grad,
            v_bias_grad,
            out_weight_grad,
            out_bias_grad,
            norm1_gain_grad,
            norm1_bias_grad,
            up_weight_grad,
            up_bias_grad,
            down_weight_grad,
            down_bias_grad,
            norm2_gain_grad,
            norm2_bias_grad,
        ),
        ("batch", "seq"),
    )
    return (
        layer_out,
        input_grad,
        summed[0],
        summed[1],
        summed[2],
        summed[3],
        summed[4],
        summed[5],
        summed[6],
        summed[7],
        summed[8],
        summed[9],
        summed[10],
        summed[11],
        summed[12],
        summed[13],
    )


MESH = pl.DeviceIdType.MESH
f32, bf16 = jnp.float32, jnp.bfloat16
LANES = 9
PIECES, PIECE = 4, 32


def mm(a, b):
    return jnp.dot(a, b, preferred_element_type=f32)


def mm_nt(a, b):
    return lax.dot_general(a, b, (((1,), (1,)), ((), ())), preferred_element_type=f32)


def mm_tn(a, b):
    return lax.dot_general(a, b, (((0,), (0,)), ((), ())), preferred_element_type=f32)


class Numbers:
    def __init__(self):
        self.count = 0
        self.first = {}

    def take(self, name, size=1):
        self.first[name] = self.count
        self.count += size

    def __getitem__(self, name):
        return self.first[name]


def semaphore_numbers():
    numbers = Numbers()
    for name, size in (
        ("x", 2 * PIECES), ("cot", 2), ("lo", 2), ("ig", 2), ("cot_x", 2),
        ("xn", 2 * PIECES), ("core_own", 2 * PIECES), ("core_far", 2 * PIECES), ("meta", 1),
        ("do", 1), ("dx_core", 2), ("dx_x", 1), ("vec", 6),
        ("lane", LANES * 12), ("qkv", 3 * 12),
    ):
        numbers.take(name, size)
    return numbers


NUM = semaphore_numbers()
LOCAL = 19

SCATTER = ('yz', 'yz', 'yz', 'yz', 'yw', 'yw', 'yw', 'yw', 'yw')
GATHER = ('wyx', 'wxy', 'zxy', 'wyx', 'wxy', 'zyx', 'zyx', 'zxy', 'zyx')
QSCATTER = ('yw', 'yw', 'yw')
QGATHER = ('wxy', 'zxy', 'zyx')
FILL, LANE, FFN, NORM, ATTN, SPLIT, WEIGHT, PART, INPUT, RETURN, SMALL, PROBS, SUMS = range(13)
ORDER = (
    (RETURN, 1, 0), (FILL, 2, 0), (FILL, 1, 0), (FFN, 0, 0), (FILL, 0, 0), (LANE, 2, 0), (LANE, 1, 0),
    (FFN, 1, 0), (PROBS, 1, 0), (FILL, 4, 0), (FILL, 5, 0), (LANE, 0, 0), (FFN, 2, 0), (FFN, 3, 0),
    (FILL, 3, 0), (LANE, 2, 1), (LANE, 4, 0), (NORM, 0, 0), (FILL, 8, 0), (LANE, 1, 1), (LANE, 5, 0),
    (PROBS, 0, 0), (FILL, 6, 0), (FILL, 7, 0), (LANE, 8, 0), (LANE, 0, 1), (LANE, 3, 0), (ATTN, 0, 0),
    (LANE, 7, 0), (LANE, 4, 1), (LANE, 2, 2), (ATTN, 1, 0), (LANE, 5, 1), (LANE, 6, 0), (LANE, 1, 2),
    (ATTN, 2, 0), (LANE, 8, 1), (LANE, 0, 2), (LANE, 4, 2), (ATTN, 3, 0), (SPLIT, 0, 0), (LANE, 5, 2),
    (INPUT, 0, 0), (LANE, 2, 3), (LANE, 3, 1), (WEIGHT, 0, 0), (INPUT, 1, 0), (LANE, 7, 1), (INPUT, 2, 0),
    (WEIGHT, 1, 0), (WEIGHT, 2, 0), (INPUT, 3, 0), (LANE, 1, 3), (LANE, 0, 3), (LANE, 8, 2), (LANE, 4, 3),
    (SUMS, 0, 0), (PART, 0, 0), (LANE, 5, 3), (LANE, 3, 2), (LANE, 0, 4), (LANE, 7, 2), (LANE, 2, 4),
    (LANE, 1, 4), (SUMS, 1, 0), (LANE, 6, 1), (SMALL, 0, 0), (PART, 0, 1), (SMALL, 1, 0), (LANE, 4, 4),
    (LANE, 8, 3), (PART, 1, 0), (LANE, 0, 5), (LANE, 5, 4), (PART, 2, 0), (LANE, 6, 2), (LANE, 7, 3),
    (LANE, 1, 5), (LANE, 3, 3), (PART, 0, 2), (LANE, 4, 5), (PART, 2, 1), (LANE, 8, 4), (LANE, 5, 5),
    (PART, 1, 1), (SMALL, 2, 0), (LANE, 6, 3), (LANE, 3, 4), (LANE, 7, 4), (LANE, 4, 6), (PART, 0, 3),
    (LANE, 8, 5), (PART, 2, 2), (PART, 1, 2), (PART, 0, 4), (LANE, 6, 4), (LANE, 0, 6), (SMALL, 3, 0),
    (LANE, 2, 5), (LANE, 1, 6), (LANE, 5, 6), (LANE, 7, 5), (LANE, 0, 7), (LANE, 3, 5), (RETURN, 0, 0),
    (PART, 2, 3), (LANE, 4, 7), (LANE, 4, 8), (PART, 1, 3), (LANE, 8, 6), (LANE, 2, 6), (LANE, 8, 7),
    (SMALL, 4, 0), (PART, 0, 5), (LANE, 6, 5), (PART, 1, 4), (LANE, 3, 6), (PART, 2, 4), (LANE, 7, 6),
    (PART, 0, 6), (LANE, 6, 6), (LANE, 5, 7), (LANE, 7, 7), (LANE, 3, 7), (PART, 1, 5), (LANE, 6, 7),
    (PART, 0, 7), (PART, 2, 5), (LANE, 1, 7), (PART, 1, 6), (SMALL, 5, 0), (PART, 2, 6),
)


def fused(
    x_in, cot_in, groups, lengths, table_in, wqkv_in, qb_in, vb_in, wo_in, ob_in, g1_in, b1_in,
    wup_in, ub_in, wdn_in, db_in, g2_in, b2_in,
    lo_out, ig_out, full, qfull, vec_out,
    x_here, cot_here, xb, lowb, cotb, table, meta, meta_far, wqkv, wq, wo, wup, wdn, qb, vb, ob, g1, b1, ub, db, g2, b2,
    qt, q, k, vaug, vback, att, inv, sums, abuf, before, act, pre_grad, res, lob, igb, n1, n2, s1b, s2b, attn_grad,
    normed_low, ffn_grad, second, normed_grad, dob, dor, probs, dkt, dvt, dqkv, dxb, dxr0, dxr1, dxo,
    vecb, vecr,
    own, r0, r1, r3, qown, qr1, qr3,
    ssem, rsem, lsem,
):
    b_index, s_index = lax.axis_index("batch"), lax.axis_index("seq")
    x, z = s_index % 2, s_index // 2
    y, c = b_index // 2, b_index % 2
    me = 2 * x + c

    def dev(x, y, z, c):
        return (2 * y + c, 2 * z + x)

    core_dev = dev(x, y, z, 1 - c)
    x_dev = dev(1 - x, y, z, c)
    y_dev = dev(x, 1 - y, z, c)
    z_devs = [dev(x, y, (z + d) % 4, c) for d in (1, 2, 3)]
    z_near = z + 1 - 2 * (z % 2)
    near_dev, mirror_dev = dev(x, y, z_near, c), dev(x, y, 3 - z, c)
    crossing = c != z // 2

    pending = []

    def send(src, dst, s_number, r_number, device, when=None):
        copy = pltpu.make_async_remote_copy(
            src_ref=src, dst_ref=dst, send_sem=ssem.at[s_number], recv_sem=rsem.at[r_number],
            device_id=device, device_id_type=MESH,
        )
        if when is None:
            copy.start()
        else:
            pl.when(when)(copy.start)
        pending.append((copy, when))

    def arrived(dst, number):
        pltpu.make_async_remote_copy(
            src_ref=dst, dst_ref=dst, send_sem=ssem.at[number], recv_sem=rsem.at[number],
            device_id=core_dev, device_id_type=MESH,
        ).wait_recv()

    local_copies = []

    def fetch(src, dst):
        copy = pltpu.make_async_copy(src, dst, lsem.at[len(local_copies)])
        copy.start()
        local_copies.append(copy)
        return copy

    def land(copies):
        for copy in copies:
            copy.wait()
            local_copies[[entry is copy for entry in local_copies].index(True)] = None

    wait_table = fetch(table_in, table)
    wait_tokens = [fetch(x_in, x_here), fetch(cot_in, cot_here)]

    barrier = pltpu.get_barrier_semaphore()
    near = [core_dev, x_dev, y_dev] + z_devs
    for device in near:
        pl.semaphore_signal(barrier, inc=1, device_id=device, device_id_type=MESH)

    def greet(devices):
        for device in devices:
            pl.semaphore_signal(barrier, inc=1, device_id=device, device_id_type=MESH)
        pl.semaphore_wait(barrier, len(near) + len(devices))

    @pl.when(crossing)
    def _():
        greet([dev(xx, y, 2 * c + i, z // 2) for i in range(2) for xx in (x, 1 - x)])

    @pl.when(jnp.logical_not(crossing))
    def _():
        greet([dev(1 - x, y, z_near, c)])

    def half(ref, h):
        return ref.at[pl.ds(PIECE * h, PIECE)]

    def peer(i):
        return dev(x, y, 2 * c + i, z // 2)

    land(wait_tokens)
    first = jnp.where(crossing, 1 - c, z % 2)
    in_turn = [(i, h) for i in (first, 1 - first) for h in range(PIECES)]
    for i, h in in_turn:
        send(half(x_here.at[i], h), half(xb.at[x, z], h), NUM["x"] + PIECES * i + h, NUM["x"] + PIECES * (z % 2) + h,
             peer(i), when=2 * c + i != z)
    def send_cot():
        for i in (first, 1 - first):
            send(cot_here.at[i], cotb.at[x, z % 2], NUM["cot"] + i, NUM["cot"] + z % 2, peer(i), when=2 * c + i != z)
        for i in (first, 1 - first):
            send(cot_here.at[i], cotb.at[x, z % 2], NUM["cot_x"] + i, NUM["cot_x"] + z % 2,
                 dev(1 - x, y, 2 * c + i, z // 2))

    send_cot()
    @pl.when(jnp.logical_not(crossing))
    def _():
        xb[x, z] = x_here[z % 2]
        cotb[x, z % 2] = cot_here[z % 2]

    wait_qkv = [fetch(qb_in, qb), fetch(vb_in, vb)]
    for t in range(3):
        columns = pl.ds(pl.multiple_of(512 * t + 128 * me, 128), 128)
        wait_qkv.append(fetch(wqkv_in.at[:, columns], wq.at[:, pl.ds(128 * t, 128)]))
    wait_qkv.append(fetch(wqkv_in, wqkv))
    wait_ffn = [
        fetch(a, b)
        for a, b in ((wo_in, wo), (ob_in, ob), (g1_in, g1), (b1_in, b1), (wup_in, wup), (ub_in, ub),
                     (wdn_in, wdn), (db_in, db), (g2_in, g2), (b2_in, b2))
    ]

    land([wait_table])
    slot = z % 2
    group, length = groups[slot], lengths[slot]
    meta[0:1, :] = table[pl.ds(group, 1), :]
    meta[1:2, :] = jnp.full((1, 512), length.astype(f32))
    meta[2:3, :] = jnp.full((1, 512), group.astype(f32))
    meta[3:8, :] = jnp.zeros((5, 512), f32)
    send(meta, meta_far, NUM["meta"], NUM["meta"], core_dev)

    for i, h in in_turn:
        block = half(xb.at[x, 2 * c + i], h)

        @pl.when(2 * c + i != z)
        def _():
            arrived(block, NUM["x"] + PIECES * i + h)

        number = NUM["xn"] + PIECES * i + h
        send(block, block, number, number, x_dev)
        number = NUM["core_own"] + PIECES * i + h
        send(block, block, number, number, core_dev)

    land(wait_qkv)
    arrived(meta_far, NUM["meta"])
    facts = jnp.where(crossing, meta_far[...], meta[...])
    pair_row, length_row, group_row = facts[0:1, :], facts[1:2, :], facts[2:3, :]
    row_length = length_row[:, 0:1]

    lane = lax.broadcasted_iota(jnp.int32, (1, 128), 1)
    head_lanes = [lane < 64, lane >= 64]
    row = lax.broadcasted_iota(jnp.int32, (256, 1), 0)

    def rows_of(xx, cc):
        return pl.ds(pl.multiple_of(512 * xx + 256 * cc, 256), 256)

    def usable_rows(xx, cc):
        place = 128 * (4 * cc + xx) + row + jnp.where(row >= 128, 128, 0)
        return place.astype(f32) < row_length

    mine = pl.ds(pl.multiple_of(128 * me, 128), 128)
    all_lanes = lax.broadcasted_iota(jnp.int32, (1, 256), 1)
    first_head = all_lanes % 128 < 64

    def project(xx, cc, ours):
        low = (xb[xx, pl.ds(2 * cc, 2)].reshape(256, 512).astype(f32) + pair_row).astype(bf16)
        rows = rows_of(xx, cc)
        lowb[rows, :] = low
        usable = usable_rows(xx, cc)
        eighth = jnp.asarray(0.125, bf16)
        if ours:
            there = pl.ds(pl.multiple_of(256 * xx, 256), 256)
            qt[there, :] = (mm(low, wqkv[:, 0:512]) + qb[...]).astype(bf16) * eighth
            q[rows, :] = qt[there, mine]
        k[rows, :] = jnp.where(usable, mm(low, wqkv[:, 512:1024]), 0.0).astype(bf16)
        value = jnp.where(usable, mm(low, wqkv[:, 1024:1536]) + vb[...], 0.0).astype(bf16)
        one = jnp.broadcast_to(jnp.where(usable, 1.0, 0.0), (256, 128))
        for pair in range(4):
            vaug[pair, rows, 0:128] = value[:, 128 * pair : 128 * pair + 128]
            vaug[pair, rows, 128:256] = one.astype(bf16)

    def backward_values():
        for xx in (0, 1):
            for cc in (0, 1):
                rows = pl.ds(512 * xx + 256 * cc, 256)
                own_value = vaug[me, rows, 0:128].astype(f32)
                one = vaug[me, rows, 128:256].astype(f32)
                for h in range(2):
                    edge = 64 * (1 - h)
                    extra = jnp.where((lane == edge) | (lane == edge + 1), one, 0.0)
                    vback[h, rows, :] = jnp.where(head_lanes[h], own_value, extra).astype(bf16)

    def attend(q_rows, pair, h, keys, probs_rows):
        columns = pl.ds(pl.multiple_of(128 * pair, 128), 128)
        prob = jnp.exp(mm_nt(jnp.where(head_lanes[h], q_rows, 0), k[keys, columns])).astype(bf16)
        for at, rows in enumerate(probs_rows):
            probs[h, rows, keys] = prob[256 * at : 256 * at + 256]
        return mm(prob, vaug[pair, keys, :])

    def attended_of(parts, rows):
        both = jnp.where(first_head, parts[0], parts[1])
        inverse = 1.0 / both[:, 128:256]
        attended = both[:, 0:128] * inverse
        if rows is not None:
            att[rows, :] = attended
            inv[rows, :] = inverse
        return attended.astype(bf16)

    every = pl.ds(0, 1024)
    early = pl.ds(pl.multiple_of(512 * x, 512), 512)
    pairs = [(me + d) % 4 for d in range(4)]
    own_rows, far_rows = rows_of(x, c), rows_of(1 - x, c)
    own_half = pl.ds(pl.multiple_of(256 * x, 256), 256)
    far_half = pl.ds(pl.multiple_of(256 * (1 - x), 256), 256)

    def pair_columns(pair):
        return pl.ds(pl.multiple_of(128 * pair, 128), 128)

    def own_early(d, h):
        keep = [own_rows] if d == 0 else []
        sums[d, h, own_half, :] = attend(qt[own_half, pair_columns(pairs[d])], pairs[d], h, early, keep)

    def far_early(d, h):
        keep = [far_rows] if d == 0 else []
        sums[d, h, far_half, :] = attend(qt[far_half, pair_columns(pairs[d])], pairs[d], h, early, keep)

    def all_late(d, h, keys):
        keep = [rows_of(0, c), rows_of(1, c)] if d == 0 else []
        return sums[d, h] + attend(qt[:, pair_columns(pairs[d])], pairs[d], h, keys, keep)

    project(x, c, True)
    for i, h in in_turn:
        arrived(half(xb.at[x, 2 * (1 - c) + i], h), NUM["core_own"] + PIECES * i + h)
    project(x, 1 - c, False)
    for at, (i, h) in enumerate(in_turn):
        if at % (PIECES // 2) == 0:
            own_early(at // (PIECES // 2), 0)
            own_early(at // (PIECES // 2), 1)
        block = half(xb.at[1 - x, 2 * c + i], h)
        arrived(block, NUM["xn"] + PIECES * i + h)
        number = NUM["core_far"] + PIECES * i + h
        send(block, block, number, number, core_dev)
    project(1 - x, c, True)
    for d in range(4):
        for h in range(2):
            far_early(d, h)
            sums[d, h] = all_late(d, h, far_rows)
    for i, h in in_turn:
        arrived(half(xb.at[1 - x, 2 * (1 - c) + i], h), NUM["core_far"] + PIECES * i + h)
    project(1 - x, 1 - c, False)

    for d in range(4):
        parts = [all_late(d, h, rows_of(1 - x, 1 - c)) for h in range(2)]
        for xx in (0, 1):
            there = pl.ds(256 * xx, 256)
            abuf[there, pair_columns(pairs[d])] = attended_of(
                [part[256 * xx : 256 * xx + 256] for part in parts], rows_of(xx, c) if d == 0 else None
            )

    def other_probs(xx):
        rows = rows_of(xx, 1 - c)
        projected = mm(lowb[rows, :], wq[:, 0:128]) + qb[:, mine]
        q[rows, :] = projected.astype(bf16) * jnp.asarray(0.125, bf16)
        attended_of([attend(q[rows, :], me, h, every, [rows]) for h in range(2)], rows)

    def norm(hidden):
        centred = hidden - jnp.mean(hidden, axis=-1, keepdims=True)
        scale = lax.rsqrt(jnp.mean(centred * centred, axis=-1, keepdims=True) + eps_norm)
        return centred * scale, scale

    def norm_back(grad, normalized, scale, gain):
        e = grad * gain
        return scale * (
            e - jnp.mean(e, axis=-1, keepdims=True)
            - normalized * jnp.mean(e * normalized, axis=-1, keepdims=True)
        )

    def column_sum(values):
        return jnp.sum(values, axis=0, keepdims=True)

    once = jnp.where(x == 0, 1.0, 0.0)
    land(wait_ffn)
    for xx in (0, 1):
        there = pl.ds(256 * xx, 256)
        start_x = xb[xx, pl.ds(2 * c, 2)].reshape(256, 512).astype(f32) + pair_row
        normalized, s1 = norm(start_x + (mm(abuf[there, :], wo[...]) + ob[...]))
        s1b[there, :] = jnp.broadcast_to(s1, (256, 128))
        n1[there, :] = normalized
        normed = normalized * g1[...] + b1[...]
        normed_low[there, :] = normed.astype(bf16)
        normed_grad[there, :] = normed + start_x
    for j in range(4):
        cols = pl.ds(512 * j, 512)
        pre = mm(normed_low[...], wup[:, cols]) + ub[:, cols]
        before[:, cols] = pre
        act_low = (pre * (0.5 * (1.0 + lax.erf(pre * 0.7071067811865476)))).astype(bf16)
        act[:, cols] = act_low
        term = mm(act_low, wdn[cols, :])
        second[...] = term if j == 0 else second[...] + term
    for xx in (0, 1):
        there = pl.ds(256 * xx, 256)
        normalized, s2 = norm((second[there, :] + db[...]) + normed_grad[there, :])
        n2[there, :] = normalized
        s2b[there, :] = jnp.broadcast_to(s2, (256, 128))
    def give_back(block, out, name):
        for i in (0, 1):
            send(block.at[i], out.at[z % 2], NUM[name] + i, NUM[name] + z % 2, peer(i), when=2 * c + i != z)

        @pl.when(jnp.logical_not(crossing))
        def _():
            out[z % 2] = block[z % 2]

    def layer_back():
        lob[...] = (n2[own_half, :] * g2[...] + b2[...]).astype(bf16).reshape(2, 128, 512)
        give_back(lob, lo_out, "lo")

    for i in (0, 1):
        @pl.when(2 * c + i != z)
        def _():
            arrived(cotb.at[x, i], NUM["cot"] + i)
    for turn, (xx, there) in enumerate(((x, own_half), (1 - x, far_half))):
        if turn == 1:
            for i in (0, 1):
                arrived(cotb.at[1 - x, i], NUM["cot_x"] + i)
        g = cotb[xx].reshape(256, 512).astype(f32)
        normalized = n2[there, :]
        grad = norm_back(g, normalized, s2b[there, 0:1], g2[...])
        second[there, :] = grad
        low = grad.astype(bf16)
        ffn_grad[there, :] = low

    def number(n, step):
        return NUM["lane"] + 12 * n + step

    def add_up(target, parts, result=None):
        value = target[...].astype(f32)
        for part in parts:
            value = value + part[...].astype(f32)
        (target if result is None else result)[...] = value.astype(bf16)

    def travel(mine, r1, r3, whole, number_of, scatter, order):
        stages = []

        def scatter_stages(axis, last):
            def part(zz):
                return mine.at[y, zz] if last else mine.at[:, zz]

            def slot(d):
                return r3.at[d, 0] if last else r3.at[d]

            result = whole.at[x, c, y, z] if last else None
            if axis == "y":
                box = r1.at[0] if last else r1

                def start():
                    send(mine.at[1 - y, z] if last else mine.at[1 - y], box, number_of(1), number_of(1), y_dev)

                def finish():
                    arrived(box, number_of(1))
                    add_up(mine.at[y, z] if last else mine.at[y], [box], result)

                stages.append((start, finish))
            elif axis == "z":
                def start():
                    for d in (1, 2, 3):
                        send(part((z + d) % 4), slot(3 - d), number_of(1 + d), number_of(5 - d), z_devs[d - 1])

                def finish():
                    for d in (1, 2, 3):
                        arrived(slot(d - 1), number_of(1 + d))
                    add_up(part(z), [slot(d) for d in range(3)], result)

                stages.append((start, finish))
            else:
                def start():
                    send(part(3 - z_near), slot(0), number_of(2), number_of(2), near_dev)

                def finish():
                    arrived(slot(0), number_of(2))
                    add_up(part(3 - z), [slot(0)])

                def start_two():
                    send(part(3 - z), slot(1), number_of(3), number_of(3), mirror_dev)
                    send(part(z_near), slot(2), number_of(4), number_of(4), near_dev)

                def finish_two():
                    arrived(slot(1), number_of(3))
                    arrived(slot(2), number_of(4))
                    add_up(part(z), [slot(1), slot(2)], result)

                stages.append((start, finish))
                stages.append((start_two, finish_two))

        def region(done, **other):
            place = dict(x=x, y=y, z=z) | other
            at = {axis: slice(None) if axis in done else place[axis] for axis in "xyz"}
            return whole.at[at["x"], c, at["y"], at["z"]]

        def gather_stages(axis, done):
            part = region(done)
            if axis == "z":
                def start():
                    for d in (1, 2, 3):
                        send(part, part, number_of(4 + d), number_of(8 - d), z_devs[d - 1])

                def finish():
                    for d in (1, 2, 3):
                        arrived(region(done, z=(z + d) % 4), number_of(4 + d))

                stages.append((start, finish))
            elif axis == "w":
                def start():
                    send(part, part, number_of(6), number_of(6), mirror_dev)
                    send(part, part, number_of(5), number_of(5), near_dev)

                def finish():
                    arrived(region(done, z=z_near), number_of(5))
                    arrived(region(done, z=3 - z), number_of(6))

                def start_two():
                    passed = region(done, z=3 - z)
                    send(passed, passed, number_of(7), number_of(7), near_dev)

                def finish_two():
                    arrived(region(done, z=3 - z_near), number_of(7))

                stages.append((start, finish))
                stages.append((start_two, finish_two))
            else:
                at, device, there = {"x": (9, x_dev, dict(x=1 - x)), "y": (8, y_dev, dict(y=1 - y))}[axis]

                def start():
                    send(part, part, number_of(at), number_of(at), device)

                def finish():
                    arrived(region(done, **there), number_of(at))

                stages.append((start, finish))

        scatter_stages(scatter[0], False)
        scatter_stages(scatter[1], True)
        for at, axis in enumerate(order):
            gather_stages(axis, order[:at].replace("w", "z"))

        def start():
            send(whole.at[:, c], whole.at[:, c], number_of(10), number_of(10), core_dev)

        def finish():
            arrived(whole.at[:, 1 - c], number_of(10))

        stages.append((start, finish))
        return stages

    lane_stages = [
        travel(own.at[n, c], r1.at[n], r3.at[n], full.at[n], functools.partial(number, n), SCATTER[n], GATHER[n])
        for n in range(LANES)
    ]

    def lane_step(n, step):
        if step == 0:
            arrived(r0.at[n], number(n, 0))
            add_up(own.at[n, c], [r0.at[n]])
        else:
            lane_stages[n][step - 1][1]()
        if step < len(lane_stages[n]):
            lane_stages[n][step][0]()

    own_columns = pl.ds(pl.multiple_of(256 * x, 256), 256)

    def lane_fill(n):
        if n < 4:
            value = mm_tn(act[:, pl.ds(pl.multiple_of(512 * n + 256 * x, 256), 256)], ffn_grad[...])
        elif n < 8:
            value = mm_tn(normed_low[:, own_columns], pre_grad[:, pl.ds(512 * (n - 4), 512)])
        else:
            value = mm_tn(abuf[:, own_columns], attn_grad[...])
        own[n] = value.astype(bf16).reshape(2, 2, 4, 16, 512)
        send(own.at[n, 1 - c], r0.at[n], number(n, 0), number(n, 0), core_dev)

    def ffn_back(j):
        cols = pl.ds(512 * j, 512)
        pre = before[:, cols]
        cdf = 0.5 * (1.0 + lax.erf(pre * 0.7071067811865476))
        slope = cdf + pre * (jnp.exp(-0.5 * pre * pre) * 0.3989422804014327)
        grad = (mm_nt(ffn_grad[...], wdn[cols, :]) * slope).astype(bf16)
        pre_grad[:, cols] = grad
        vecb[16 + j : 17 + j, :] = column_sum(grad.astype(f32)) * once
        normed_grad[...] = (second if j == 0 else normed_grad)[...] + mm_nt(grad, wup[:, cols])

    def first_back():
        for xx in (0, 1):
            there = pl.ds(256 * xx, 256)
            grad, normalized = normed_grad[there, :], n1[there, :]
            first_grad = norm_back(grad, normalized, s1b[there, 0:1], g1[...])
            low = first_grad.astype(bf16)
            attn_grad[there, :] = low
            second[there, :] = second[there, :] + first_grad
        res[...] = second[own_half, :]
        backward_values()
        low = attn_grad[...]

        def heads(cc):
            return pl.ds(pl.multiple_of(128 * (2 * x + cc), 128), 128)

        dob[...] = mm_nt(low, wo[heads(1 - c), :]).astype(bf16)
        send(dob, dor.at[c], NUM["do"], NUM["do"], core_dev)
        dor[c] = mm_nt(low, wo[heads(c), :]).astype(bf16)

    def norm_sums(which):
        if which == 0:
            grad, normalized, low, at = cotb[...].reshape(512, 512).astype(f32), n2[...], ffn_grad[...], 13
        else:
            grad, normalized, low, at = normed_grad[...], n1[...], attn_grad[...], 10
        vecb[at : at + 1, :] = column_sum(low.astype(f32)) * once
        vecb[at + 1 : at + 2, :] = column_sum(grad * normalized) * once
        vecb[at + 2 : at + 3, :] = column_sum(grad) * once

    turns = ((0, c), (1, c), (0, 1 - c), (1, 1 - c))

    def attention_back(turn):
        xx, cc = turns[turn]
        if turn == 2:
            arrived(dor.at[cc], NUM["do"])
        rows = rows_of(xx, cc)
        d_out = dor[cc, 256 * xx : 256 * xx + 256, :].astype(f32)
        numer_grad = d_out * inv[rows, :]
        product = numer_grad.astype(bf16).astype(f32) * att[rows, :]
        q_rows = q[rows, :]
        dq_rows = jnp.zeros((256, 128), f32)
        for h in range(2):
            total = -jnp.sum(jnp.where(head_lanes[h], product, 0.0), axis=1, keepdims=True)
            high = total.astype(bf16).astype(f32)
            edge = 64 * (1 - h)
            rest = jnp.where(lane == edge, high, jnp.where(lane == edge + 1, total - high, 0.0))
            grad_low = jnp.where(head_lanes[h], numer_grad, rest).astype(bf16)
            prob = probs[h, rows, :]
            score_grad = (prob.astype(f32) * mm_nt(grad_low, vback[h])).astype(bf16)
            dq_rows = dq_rows + jnp.where(head_lanes[h], mm(score_grad, k[:, mine]), 0.0)
            part = slice(64 * h, 64 * h + 64)
            dk_part = mm(jnp.transpose(q_rows)[part, :], score_grad)
            dv_part = mm(jnp.transpose(grad_low)[part, :], prob)
            dkt[part, :] = dk_part if turn == 0 else dkt[part, :] + dk_part
            dvt[part, :] = dv_part if turn == 0 else dvt[part, :] + dv_part
        dqkv[rows, 0:128] = (dq_rows * 0.125).astype(bf16)

    def projection_grads():
        for xx in (0, 1):
            for cc in (0, 1):
                rows = pl.ds(512 * xx + 256 * cc, 256)
                dqkv[rows, 128:256] = jnp.transpose(dkt[:, rows]).astype(bf16)
                dqkv[rows, 256:384] = jnp.where(usable_rows(xx, cc), jnp.transpose(dvt[:, rows]), 0.0).astype(bf16)

    def qnumber(t, step):
        return NUM["qkv"] + 12 * t + step

    part_stages = [
        travel(qown.at[t], qr1.at[t], qr3.at[t], qfull.at[t], functools.partial(qnumber, t), QSCATTER[t], QGATHER[t])
        for t in range(3)
    ]

    def projection_weights(t):
        value = mm_tn(lowb[...], dqkv[:, 128 * t : 128 * t + 128])
        qown[t] = value.astype(bf16).reshape(2, 4, 64, 128)
        part_stages[t][0][0]()

    def projection_step(t, step):
        part_stages[t][step][1]()
        if step + 1 < len(part_stages[t]):
            part_stages[t][step + 1][0]()

    def input_back(step):
        xx, cc = ((1 - x, 1 - c), (x, 1 - c), (1 - x, c), (x, c))[step]
        block = mm_nt(dqkv[rows_of(xx, cc), :], wq[...])
        vecb[20:21, :] = column_sum(block) if step == 0 else vecb[20:21, :] + column_sum(block)
        if step < 2:
            dxb[step] = block.astype(bf16)
            send(dxb.at[step], dxr0.at[step], NUM["dx_core"] + step, NUM["dx_core"] + step, core_dev)
        elif step == 2:
            arrived(dxr0.at[0], NUM["dx_core"])
            dxb[2] = (block + dxr0[0].astype(f32)).astype(bf16)
            send(dxb.at[2], dxr1, NUM["dx_x"], NUM["dx_x"], x_dev)
        else:
            arrived(dxr0.at[1], NUM["dx_core"] + 1)
            dxo[...] = block + dxr0[1].astype(f32) + res[...]

    def input_out():
        arrived(dxr1, NUM["dx_x"])
        igb[...] = (dxo[...] + dxr1[...].astype(f32)).astype(bf16).reshape(2, 128, 512)
        give_back(igb, ig_out, "ig")

    def vectors(step):
        if step == 0:
            group_iota = lax.broadcasted_iota(jnp.int32, (8, 512), 0).astype(f32)
            column_total = vecb[20:21, :] + column_sum(res[...])
            vecb[0:8, :] = jnp.where(group_iota == group_row, column_total, 0.0)
            vecb[8:10, :] = jnp.zeros((2, 512), f32)
            vecb[8:9, mine] = column_sum(dqkv[:, 0:128].astype(f32))
            vecb[9:10, mine] = column_sum(dqkv[:, 256:384].astype(f32))
            vecb[20:24, :] = jnp.zeros((4, 512), f32)
            send(vecb, vecr.at[0], NUM["vec"], NUM["vec"], core_dev)
        else:
            level = step - 1
            arrived(vecr.at[level], NUM["vec"] + level)
            value = (vecb if level == 0 else vecr.at[4 + level])[...] + vecr[level]
            if level < 4:
                vecr[5 + level] = value
                send(vecr.at[5 + level], vecr.at[level + 1], NUM["vec"] + level + 1, NUM["vec"] + level + 1,
                     (x_dev, y_dev, near_dev, mirror_dev)[level])
            else:
                vec_out[...] = value

    tasks = {(NORM, 0, 0): first_back, (SPLIT, 0, 0): projection_grads, (RETURN, 0, 0): input_out, (RETURN, 1, 0): layer_back}
    for kind, task, count in (
        (FILL, lane_fill, LANES), (FFN, ffn_back, 4), (ATTN, attention_back, 4), (PROBS, other_probs, 2), (WEIGHT, projection_weights, 3),
        (INPUT, input_back, 4), (SMALL, vectors, 6), (SUMS, norm_sums, 2),
    ):
        for at in range(count):
            tasks[kind, at, 0] = functools.partial(task, at)
    for n in range(LANES):
        for step in range(len(lane_stages[n]) + 1):
            tasks[LANE, n, step] = functools.partial(lane_step, n, step)
    for t in range(3):
        for step in range(len(part_stages[t])):
            tasks[PART, t, step] = functools.partial(projection_step, t, step)
    for at, entry in enumerate(ORDER):
        tasks.pop(entry)()
    assert not tasks

    for name, out in (("lo", lo_out), ("ig", ig_out)):
        for i in (0, 1):
            @pl.when(2 * c + i != z)
            def _():
                arrived(out.at[i], NUM[name] + i)
    land([copy for copy in local_copies if copy is not None])
    for copy, when in pending:
        if when is None:
            copy.wait_send()
        else:
            pl.when(when)(copy.wait_send)


VECTOR_ROWS = (8, 9, 10, 11, 12, 13, 14, 15)


def finish(lo, ig, full, qfull, vec, *refs):
    lo_out, ig_out, down_out, up_out, out_out, qkv_out, pair_out = refs[:7]
    vector_outs, up_bias_out = refs[7:15], refs[15]
    lo_wide, ig_wide, full_wide, qkv_wide, rows, up_bias, sems = *refs[16:20], refs[20:28], refs[28], refs[29]
    writes = []

    def write(src, dst):
        made = pltpu.make_async_copy(src, dst, sems.at[len(writes)])
        made.start()
        writes.append(made)

    for n in range(LANES):
        for half in range(2):
            at = pl.ds(256 * half, 256)
            full_wide[n, at, :] = full[n, half].reshape(256, 512).astype(f32)
            if n < 4:
                write(full_wide.at[n, at], down_out.at[pl.ds(512 * n + 256 * half, 256)])
            elif n < 8:
                write(full_wide.at[n, at], up_out.at[at, pl.ds(512 * (n - 4), 512)])
            else:
                write(full_wide.at[n, at], out_out.at[at])
    for t in range(3):
        for h in range(4):
            columns = pl.ds(512 * t + 128 * h, 128)
            qkv_wide[:, columns] = qfull[t, h // 2, h % 2].reshape(512, 128).astype(f32)
        columns = pl.ds(512 * t, 512)
        write(qkv_wide.at[:, columns], qkv_out.at[:, columns])
    for block, wide, out in ((lo, lo_wide, lo_out), (ig, ig_wide, ig_out)):
        wide[...] = block[...].astype(f32)
        write(wide, out)
    write(vec.at[pl.ds(0, 8)], pair_out)
    for at, row, out in zip(VECTOR_ROWS, rows, vector_outs):
        row[...] = vec[at : at + 1, :]
        write(row, out)
    for j in range(4):
        up_bias[:, 512 * j : 512 * j + 512] = vec[16 + j : 17 + j, :]
    write(up_bias, up_bias_out)
    for made in writes:
        made.wait()


def pair_plan(mesh):
    return dict(mesh.shape) == {"batch": 4, "seq": 8}


def fused_local(
    block_input, cotangent, groups, lengths, pair_table, qkv_weight, q_bias, v_bias, out_weight,
    out_bias, norm1_gain, norm1_bias, up_weight, up_bias, down_weight, down_bias, norm2_gain, norm2_bias,
):
    any_spec, smem = pl.BlockSpec(memory_space=pl.ANY), pl.BlockSpec(memory_space=pltpu.SMEM)

    def row(vector):
        return vector[None, :]

    operands = (
        block_input, cotangent, groups, lengths, pair_table, qkv_weight, row(q_bias), row(v_bias),
        out_weight, row(out_bias), row(norm1_gain), row(norm1_bias), up_weight, row(up_bias),
        down_weight, row(down_bias), row(norm2_gain), row(norm2_bias),
    )
    in_specs = [smem if i in (2, 3) else any_spec for i in range(len(operands))]
    vmem = pl.BlockSpec(memory_space=pltpu.VMEM)
    out_shape = [
        pltpu.VMEM(shape, dtype)
        for shape, dtype in (
            ((2, 128, 512), bf16), ((2, 128, 512), bf16), ((LANES, 2, 2, 2, 4, 16, 512), bf16),
            ((3, 2, 2, 2, 4, 64, 128), bf16), ((24, 512), f32),
        )
    ]
    scratch = [
        pltpu.VMEM(shape, dtype)
        for shape, dtype in (
            ((2, 128, 512), bf16), ((2, 128, 512), bf16),
            ((2, 4, 128, 512), bf16), ((1024, 512), bf16), ((2, 2, 128, 512), bf16),
            ((8, 512), f32), ((8, 512), f32), ((8, 512), f32),
            ((512, 1536), bf16), ((512, 384), bf16), ((512, 512), bf16), ((512, 2048), bf16), ((2048, 512), bf16),
            ((1, 512), f32), ((1, 512), f32), ((1, 512), f32), ((1, 512), f32), ((1, 512), f32),
            ((1, 2048), f32), ((1, 512), f32), ((1, 512), f32), ((1, 512), f32),
            ((512, 512), bf16), ((1024, 128), bf16), ((1024, 512), bf16),
            ((4, 1024, 256), bf16), ((2, 1024, 128), bf16),
            ((1024, 128), f32), ((1024, 128), f32),
            ((4, 2, 512, 256), f32), ((512, 512), bf16),
            ((512, 2048), f32), ((512, 2048), bf16), ((512, 2048), bf16),
            ((256, 512), f32), ((2, 128, 512), bf16), ((2, 128, 512), bf16),
            ((512, 512), f32), ((512, 512), f32), ((512, 128), f32), ((512, 128), f32),
            ((512, 512), bf16),
            ((512, 512), bf16), ((512, 512), bf16), ((512, 512), f32), ((512, 512), f32),
            ((512, 128), bf16), ((2, 512, 128), bf16), ((2, 1024, 1024), bf16),
            ((128, 1024), f32), ((128, 1024), f32), ((1024, 384), bf16),
            ((3, 256, 512), bf16), ((2, 256, 512), bf16), ((256, 512), bf16), ((256, 512), f32),
            ((24, 512), f32), ((9, 24, 512), f32),
            ((LANES, 2, 2, 4, 16, 512), bf16), ((LANES, 2, 4, 16, 512), bf16), ((LANES, 4, 16, 512), bf16),
            ((LANES, 3, 2, 16, 512), bf16),
            ((3, 2, 4, 64, 128), bf16), ((3, 4, 64, 128), bf16), ((3, 3, 2, 64, 128), bf16),
        )
    ] + [
        pltpu.SemaphoreType.DMA((NUM.count,)),
        pltpu.SemaphoreType.DMA((NUM.count,)),
        pltpu.SemaphoreType.DMA((LOCAL,)),
    ]
    results = pl.pallas_call(
        fused,
        out_shape=out_shape,
        in_specs=in_specs,
        out_specs=[vmem] * len(out_shape),
        scratch_shapes=scratch,
        compiler_params=pltpu.CompilerParams(
            collective_id=0, has_side_effects=True, vmem_limit_bytes=54 * 2**20
        ),
    )(*operands)
    shapes = [(2, 128, 512)] * 2 + [(2048, 512), (512, 2048), (512, 512), (512, 1536), (8, 512)]
    shapes += [(1, 512)] * 8 + [(1, 2048)]
    scratch_sizes = [(2, 128, 512)] * 2 + [(LANES, 512, 512), (512, 1536)] + [(1, 512)] * 8 + [(1, 2048)]
    results = pl.pallas_call(
        finish,
        out_shape=[jax.ShapeDtypeStruct(shape, f32) for shape in shapes],
        in_specs=[vmem] * 5,
        out_specs=[any_spec] * len(shapes),
        scratch_shapes=[pltpu.VMEM(shape, f32) for shape in scratch_sizes] + [pltpu.SemaphoreType.DMA((40,))],
        compiler_params=pltpu.CompilerParams(vmem_limit_bytes=40 * 2**20),
    )(*results)
    layer_out, input_grad, down_grad, up_grad, out_grad, qkv_grad, pair_grad = results[:7]
    q_grad, v_grad, ob_grad, g1_grad, b1_grad, db_grad, g2_grad, b2_grad = [r.reshape(512) for r in results[7:15]]
    return (
        layer_out, input_grad, pair_grad, qkv_grad, q_grad, v_grad,
        out_grad, ob_grad, g1_grad, b1_grad, up_grad, results[15].reshape(2048), down_grad, db_grad, g2_grad, b2_grad,
    )


def solution(mesh):
    in_specs = (
        P("batch", "seq", None),
        P("batch", "seq", None),
        P("batch"),
        P("batch"),
        P(),
        P(),
        P(),
        P(),
        P(),
        P(),
        P(),
        P(),
        P(),
        P(),
        P(),
        P(),
        P(),
        P(),
    )
    out_specs = (
        P("batch", "seq", None),
        P("batch", "seq", None),
        P(),
        P(),
        P(),
        P(),
        P(),
        P(),
        P(),
        P(),
        P(),
        P(),
        P(),
        P(),
        P(),
        P(),
    )
    return jax.shard_map(fused_local if pair_plan(mesh) else local, mesh=mesh, in_specs=in_specs, out_specs=out_specs, check_vma=False)
```
